32 devices in a mesh: dp: 8 (over z, y), tensor: 4 (over x, core).
Axes of the slice: x: 2, y: 2, z: 4, core: 2. Of those that a mesh axis runs over, the one named last changes fastest.
Arguments:
- block_input: bfloat16 [4, 8192, 512], P(None, 'dp'), may hold values from -6 to 6
- cotangent: bfloat16 [4, 8192, 512], P(None, 'dp'), may hold values from -6 to 6
- source: int32 [4, 8192], replicated, may hold values from 0 to 8191, as said below
- seq_lengths: int32 [4, 8, 3], P(None, 'dp'), may hold values from 1 to 682, 1024 in all within a row
- qkv_weight: bfloat16 [3, 512, 512], P(None, None, 'tensor'), may hold values from -0.375 to 0.375
- qv_bias: bfloat16 [2, 512], P(None, 'tensor'), may hold values from -3 to 3
- out_weight: bfloat16 [512, 512], P('tensor'), may hold values from -0.75 to 0.75
- out_bias: bfloat16 [512], replicated, may hold values from -3 to 3
- up_weight: bfloat16 [512, 2048], P(None, 'tensor'), may hold values from -0.25 to 0.25
- up_bias: bfloat16 [2048], P('tensor'), may hold values from -3 to 3
- down_weight: bfloat16 [2048, 512], P('tensor'), may hold values from -0.25 to 0.25
- down_bias: bfloat16 [512], replicated, may hold values from -3 to 3
- rezero_alphas: float32 [2], replicated, may hold values from 0.2 to 0.45
Outputs:
- layer_output: float32 [4, 8192, 512], P(None, 'dp')
- input_grad: float32 [4, 8192, 512], P(None, 'dp')
- qkv_weight_grad: float32 [3, 512, 512], P(None, None, 'tensor')
- qv_bias_grad: float32 [2, 512], P(None, 'tensor')
- out_weight_grad: float32 [512, 512], P('tensor')
- out_bias_grad: float32 [512], replicated
- up_weight_grad: float32 [512, 2048], P(None, 'tensor')
- up_bias_grad: float32 [2048], P('tensor')
- down_weight_grad: float32 [2048, 512], P('tensor')
- down_bias_grad: float32 [512], replicated
- alphas_grad: float32 [2], replicated
The draws below stay inside these ranges and needn't reach their ends.
Inputs may be any that keep to these rules, and one draw needn't show every extreme that they name: In each micro-batch source is a permutation of the input rows; the 1024 rows of one device go to every group in equal numbers, 128 each. `seq_lengths`: each row of 3 lengths sums to 1024.
All inputs are finite; a program needn't handle non-finite values.
Results may differ from the reference program's by a relative error of at most 0.011.
The reference program's roundings to bfloat16 on the way count: a program that leaves them out, or rounds other values in their place, can miss the bound.
Values may be sent and summed in bfloat16 or wider, within the bound.
No kernel may reach another device: no remote copies, remote signals or barrier semaphores. Data moves between devices by JAX's collectives and lax.ppermute only.
A program may use at most 256 MiB of HBM per device.

```python
import math
import jax
import jax.numpy as jnp
import numpy as np
from jax import lax

D = 512
HEADS = 8
HEAD_SIZE = 64
FF = 2048
MICRO = 4
SEQS = 3
BLK = 128
QBLK = 512
TOK_GRP = 1024
MAXLEN = 682
SLOTS = 1536
TOKENS = 8192
N_DP = 8


def draw_source(key, part):
    groups = TOKENS // TOK_GRP
    share_count = TOK_GRP // groups

    def single(subkey):
        key_owner, key_rows = jax.random.split(subkey)
        owner_base = jnp.repeat(jnp.arange(groups, dtype=jnp.int32), share_count)
        owners = jax.vmap(lambda inner: jax.random.permutation(inner, owner_base))(jax.random.split(key_owner, groups)).reshape(TOKENS)
        ranking = owners * TOKENS + jnp.arange(TOKENS, dtype=jnp.int32)
        placing = jnp.argsort(ranking)
        device_rows = jax.vmap(lambda inner: jax.random.permutation(inner, TOK_GRP))(jax.random.split(key_rows, groups)).astype(jnp.int32)
        device_rows = (device_rows + jnp.arange(groups, dtype=jnp.int32)[:, None] * TOK_GRP).reshape(TOKENS)
        return jnp.zeros((TOKENS,), jnp.int32).at[placing].set(device_rows)
    return jax.vmap(single)(jax.random.split(key, MICRO))


def levels(rng, dims, cuts, smallest, top_value):
    level = 1.0
    for dim, blocks in cuts:
        draws = jax.random.uniform(jax.random.fold_in(jax.random.fold_in(rng, 6), dim), (blocks,), jnp.float32, smallest / len(cuts), top_value / len(cuts))
        level = level * jnp.repeat(jnp.exp(draws), dims[dim] // blocks).reshape((-1,) + (1,) * (len(dims) - 1 - dim))
    return level


def split_up(count, total, limit, lean):
    loads = [(1 << 20) // math.isqrt(grade ** lean) + 1 for grade in range(2, count + 1)]
    surplus, holding = total - limit - (count - 1), [1] * (count - 1)
    while surplus > 0:
        candidates = [i for i in range(count - 1) if holding[i] < limit]
        mass, remaining = sum([loads[i] for i in candidates]), surplus
        for i in candidates:
            more = min(limit - holding[i], max(1, remaining * loads[i] // mass), surplus)
            holding[i] = holding[i] + more
            surplus = surplus - more
    return np.array([limit] + holding)


def ragged_sizes(stream_key, amount, total, bound, slope):
    if amount == 2:
        one = jax.random.randint(stream_key, (), max(1, total - bound), min(bound, total - 1) + 1)
        return jnp.stack([one, total - one])
    lengths = jnp.asarray(split_up(amount, total, bound, slope), jnp.int32)
    twos = (amount - 1) // 2
    donor, sink = lengths[1:1 + 2 * twos:2], lengths[2:2 + 2 * twos:2]
    margin = jnp.minimum(donor - 1, bound - sink)
    passed = jax.random.randint(jax.random.fold_in(stream_key, 1), (twos,), 0, 1 << 20) % (margin + 1)
    lengths = lengths.at[1:1 + 2 * twos:2].set(donor - passed).at[2:2 + 2 * twos:2].set(sink + passed)
    return lengths[jax.random.permutation(jax.random.fold_in(stream_key, 2), amount)]


def bell_draw(key, shape, scale, limit, cuts=(), kind=jnp.bfloat16):
    level = levels(key, shape, cuts, -0.22, 0.18) if cuts else 1.0
    values = jax.random.normal(key, shape, jnp.float32) * scale * level
    return jnp.minimum(jnp.maximum(values, -limit), limit).astype(kind)


def setup_inputs(seed: int = 0) -> dict:
    splits = jax.random.split(jax.random.key(seed), 14)
    return {
        "block_input": bell_draw(splits[0], (MICRO, TOKENS, D), 1.0, 6.0, ((1, 8),)),
        "cotangent": bell_draw(splits[1], (MICRO, TOKENS, D), 1.0, 6.0, ((1, 8),)),
        "source": draw_source(jax.random.fold_in(splits[13], 71), 0),
        "seq_lengths": jax.vmap(lambda own: ragged_sizes(own, SEQS, TOK_GRP, MAXLEN, 2))(jax.random.split(splits[3], MICRO * N_DP)).reshape((MICRO, N_DP, SEQS)).astype(jnp.int32),
        "qkv_weight": bell_draw(splits[4], (3, D, D), (D // 2) ** -0.5, 0.375, ((2, 4),)),
        "qv_bias": bell_draw(splits[5], (2, D), 0.5, 3.0, ((1, 4),)),
        "out_weight": bell_draw(splits[6], (D, D), (D // 8) ** -0.5, 0.75, ((0, 4),)),
        "out_bias": bell_draw(splits[7], (D,), 0.5, 3.0),
        "up_weight": bell_draw(splits[8], (D, FF), D ** -0.5, 0.25, ((1, 4),)),
        "up_bias": bell_draw(splits[9], (FF,), 0.5, 3.0, ((0, 4),)),
        "down_weight": bell_draw(splits[10], (FF, D), (FF // 4) ** -0.5, 0.25, ((0, 4),)),
        "down_bias": bell_draw(splits[11], (D,), 0.5, 3.0),
        "rezero_alphas": jnp.clip(jax.random.uniform(splits[12], (2,), jnp.float32, 0.2, 0.45), 0.2, 0.45),
    }


@jax.custom_vjp
def low(v):
    return lax.optimization_barrier(v.astype(jnp.bfloat16)).astype(jnp.float32)

@jax.custom_vjp
def low_back(v):
    return v

def low_keep(v):
    return (low(v), None)

def low_pass(kept, grad):
    return (grad,)

def back_keep(v):
    return (v, None)

def back_low(kept, grad):
    return (low(grad),)
low.defvjp(low_keep, low_pass)
low_back.defvjp(back_keep, back_low)

def double_low(value):
    return low_back(low(value))

def layouts(lengths_row):
    lengths_row = lengths_row.astype(jnp.int32)
    numbers = jnp.arange(SEQS, dtype=jnp.int32)
    earlier = numbers[None, :] < numbers[:, None]
    padded = ((lengths_row + BLK - 1) // BLK * BLK).astype(jnp.int32)
    real_start = lax.optimization_barrier(jnp.sum(jnp.where(earlier, lengths_row[None, :], 0), axis=1, dtype=jnp.int32))
    slot_start = lax.optimization_barrier(jnp.sum(jnp.where(earlier, padded[None, :], 0), axis=1, dtype=jnp.int32))
    ranks = jnp.arange(TOK_GRP, dtype=jnp.int32)
    inside = (ranks[:, None] >= real_start[None, :]) & (ranks[:, None] < (real_start + lengths_row)[None, :])
    offsets = lax.optimization_barrier(jnp.sum(jnp.where(inside, (slot_start - real_start)[None, :], 0), axis=1, dtype=jnp.int32))
    slot_of_rank = (ranks + offsets).astype(jnp.int32)
    cells = jnp.arange(SLOTS, dtype=jnp.int32)
    within = (cells[:, None] >= slot_start[None, :]) & (cells[:, None] < (slot_start + lengths_row)[None, :])
    segment = (lax.optimization_barrier(jnp.sum(jnp.where(within, numbers[None, :] + 1, 0), axis=1, dtype=jnp.int32)) - 1).astype(jnp.int32)
    return (slot_of_rank, segment)

def attention_block(query_block, first_row, key_heads, value_heads, segment):
    first_row = first_row.astype(jnp.int32)
    rows_here = first_row + jnp.arange(QBLK, dtype=jnp.int32)
    columns = jnp.arange(SLOTS, dtype=jnp.int32)
    segment_rows = lax.dynamic_slice_in_dim(segment, first_row, QBLK)
    allowed = (segment_rows[:, None] == segment[None, :]) & (segment_rows[:, None] >= 0) & (columns[None, :] <= rows_here[:, None]) | (columns[None, :] == rows_here[:, None])
    raw_scores = jnp.einsum('qhe,khe->hqk', query_block, key_heads, precision=lax.Precision.HIGHEST)
    scores = low_back(raw_scores) * HEAD_SIZE ** (-0.5)
    scores = jnp.where(allowed[None, :, :], scores, jnp.full((), -1e+30, scores.dtype))
    weights = low(jax.nn.softmax(scores, axis=-1))
    return jnp.einsum('hqk,khe->qhe', weights, value_heads, precision=lax.Precision.HIGHEST)

def layer_pass(cells, segment, params):
    qkv_weight, qv_bias, out_weight, out_bias, up_weight, up_bias, down_weight, down_bias, rezero_alphas = params
    highest = lax.Precision.HIGHEST
    projected = jnp.einsum('sd,cde->cse', cells, qkv_weight, precision=highest)
    queries = double_low(projected[0] + qv_bias[0]).reshape(SLOTS, HEADS, HEAD_SIZE)
    keys_all = double_low(projected[1]).reshape(SLOTS, HEADS, HEAD_SIZE)
    values_all = double_low(projected[2] + qv_bias[1]).reshape(SLOTS, HEADS, HEAD_SIZE)
    query_blocks = queries.reshape(SLOTS // QBLK, QBLK, HEADS, HEAD_SIZE)
    first_rows = jnp.arange(SLOTS // QBLK, dtype=jnp.int32) * QBLK
    block_fn = jax.checkpoint(attention_block)
    mixed = lax.map(lambda operands: block_fn(operands[0], operands[1], keys_all, values_all, segment), (query_blocks, first_rows))
    mixed = double_low(mixed.reshape(SLOTS, D))
    attended = low_back(jnp.dot(mixed, out_weight, precision=highest) + out_bias)
    hidden = cells + rezero_alphas[0] * attended
    pre_act = low_back(jnp.dot(low(hidden), up_weight, precision=highest) + up_bias)
    activated = low(jax.nn.gelu(pre_act, approximate=True))
    branch = low_back(jnp.dot(activated, down_weight, precision=highest) + down_bias)
    return hidden + rezero_alphas[1] * branch

def reference(block_input, cotangent, source, seq_lengths, qkv_weight, qv_bias, out_weight, out_bias, up_weight, up_bias, down_weight, down_bias, rezero_alphas):
    groups = TOKENS // TOK_GRP
    slot_of_rank, segments = jax.vmap(jax.vmap(layouts))(seq_lengths)
    group_index = jnp.broadcast_to(jnp.arange(groups, dtype=jnp.int32)[:, None], (groups, TOK_GRP))

    def to_packed(values):

        def single(batch_values, batch_source, batch_slots):
            ordered = batch_values[batch_source.astype(jnp.int32)].reshape(groups, TOK_GRP, D)
            return jnp.zeros((groups, SLOTS, D), values.dtype).at[group_index, batch_slots].set(ordered)
        return jax.vmap(single)(values, source, slot_of_rank).reshape(MICRO * groups, SLOTS, D)

    def from_packed(packed):

        def single(batch_packed, batch_source, batch_slots):
            ordered = batch_packed[group_index, batch_slots].reshape(TOKENS, D)
            return jnp.zeros((TOKENS, D), packed.dtype).at[batch_source.astype(jnp.int32)].set(ordered)
        return jax.vmap(single)(packed.reshape(MICRO, groups, SLOTS, D), source, slot_of_rank)
    params = tuple((member.astype(jnp.float32) for member in (qkv_weight, qv_bias, out_weight, out_bias, up_weight, up_bias, down_weight, down_bias, rezero_alphas)))
    cells_all = to_packed(block_input.astype(jnp.float32))
    grad_packed = to_packed(cotangent.astype(jnp.float32))
    flat_segments = segments.reshape(MICRO * groups, SLOTS).astype(jnp.int32)
    layer_fn = jax.checkpoint(layer_pass)

    def forward(cells_in, weights_in):
        return lax.map(lambda operands: layer_fn(operands[0], operands[1], weights_in), (cells_in, flat_segments))
    outputs, pullback = jax.vjp(forward, cells_all, params)
    grad_cells, grad_params = pullback(grad_packed)
    layer_output = from_packed(outputs).astype(jnp.float32)
    input_grad = from_packed(grad_cells).astype(jnp.float32)
    return (layer_output, input_grad, grad_params[0], grad_params[1], grad_params[2], grad_params[3], grad_params[4], grad_params[5], grad_params[6], grad_params[7], grad_params[8])
```

```python
import functools

import jax
import jax.numpy as jnp
from jax import lax
from jax.experimental import pallas as pl
from jax.experimental.pallas import tpu as pltpu
from jax.sharding import PartitionSpec as P

HEAD_SIZE = 64
LANES = 128
QT = 256
BF = jnp.bfloat16
F32 = jnp.float32
I32 = jnp.int32
NEG = -1e30
VMEM_LIMIT = 56 * 1024 * 1024
GELU_A = 0.7978845608028654
GELU_B = 0.044715

NN = (((1,), (0,)), ((), ()))
NT = (((1,), (1,)), ((), ()))
TN = (((0,), (0,)), ((), ()))


def dot(a, b, dims=NN):
    return lax.dot_general(a, b, dims, preferred_element_type=F32)


def iota(shape, dim):
    return lax.broadcasted_iota(I32, shape, dim)


def params(limit=VMEM_LIMIT):
    return pltpu.CompilerParams(vmem_limit_bytes=limit)


def cost(flops, nbytes, trans=0):
    return pl.CostEstimate(flops=int(flops), bytes_accessed=int(nbytes), transcendentals=int(trans))


def vmem(n):
    return [pl.BlockSpec(memory_space=pltpu.VMEM)] * n


def smem():
    return pl.BlockSpec(memory_space=pltpu.SMEM)


def one_hot_rows(row, count):
    return (iota((count, row.shape[1]), 0) == row).astype(F32).astype(BF)


def one_hot_cols(col, count):
    return (iota((col.shape[0], count), 1) == col).astype(F32).astype(BF)


def route_kernel(groups, ids_ref, src_ref, x_ref, xs_ref, srow_ref, scol_ref, hot_ref):
    me, micro = ids_ref[0], ids_ref[1]
    rows = x_ref.shape[1]
    chunks = rows // LANES
    share = rows // groups
    sub_hi = iota((chunks, rows), 0)
    sub_lo = iota((LANES, rows), 0)

    def gather_group(g, total):
        value = src_ref[pl.ds(micro, 1), pl.ds(pl.multiple_of(g * rows, LANES), rows)] - me * rows
        inside = (value >= 0) & (value < rows)
        high = jnp.where(inside, value // LANES, -1)
        low = jnp.where(inside, value % LANES, -1)
        hot_high = jnp.where(high == sub_hi, (g + 1).astype(F32), 0.0).astype(BF)
        hot_low = (low == sub_lo).astype(F32).astype(BF)
        return total + dot(hot_high, hot_low, NT)

    dest = lax.fori_loop(0, groups, gather_group, jnp.zeros((chunks, LANES), F32)).astype(I32) - 1
    before = (iota((LANES, LANES), 0) < iota((LANES, LANES), 1)).astype(F32).astype(BF)
    width = max(groups, 8)
    carry = jnp.zeros((width, 1), F32)
    for c in range(chunks):
        g_row = dest[c : c + 1, :]
        hot = (iota((width, LANES), 0) == g_row).astype(F32)
        ranks = dot(hot.astype(BF), before) + carry
        carry = carry + jnp.sum(hot, axis=1, keepdims=True)
        place = g_row * share + jnp.sum(hot * ranks, axis=0, keepdims=True).astype(I32)
        srow_ref[c : c + 1, :] = place
        spread = jnp.broadcast_to(place.astype(F32), (LANES, LANES))
        scol_ref[c * LANES : (c + 1) * LANES, :] = spread.T.astype(I32)
        hot_ref[:, c * LANES : (c + 1) * LANES] = one_hot_rows(place, rows)
    xs_ref[...] = dot(hot_ref[...], x_ref[0]).astype(BF)


def second_kernel(ids_ref, src_ref, g_ref, srow_ref, gs_ref, arow_ref, acol_ref, hot_ref):
    me, micro = ids_ref[0], ids_ref[1]
    rows = g_ref.shape[1]
    for c in range(rows // LANES):
        hot_ref[:, c * LANES : (c + 1) * LANES] = one_hot_rows(srow_ref[c : c + 1, :], rows)
    gs_ref[...] = dot(hot_ref[...], g_ref[0]).astype(BF)
    own = src_ref[pl.ds(micro, 1), pl.ds(pl.multiple_of(me * rows, LANES), rows)].astype(F32)
    for c in range(rows // LANES):
        piece = own[:, c * LANES : (c + 1) * LANES]
        column = jnp.broadcast_to(piece, (LANES, LANES)).T[:, 0:1]
        count = jnp.sum((own < column).astype(F32), axis=1, keepdims=True)
        spread = jnp.broadcast_to(count, (LANES, LANES))
        acol_ref[c * LANES : (c + 1) * LANES, :] = spread.astype(I32)
        arow_ref[0:1, c * LANES : (c + 1) * LANES] = spread.T[0:1, :].astype(I32)


def starts_of(len_ref, index):
    start = jnp.zeros_like(index)
    first = jnp.int32(0)
    for j in range(len_ref.shape[0] - 1):
        first = first + len_ref[j]
        start = jnp.where(index >= first, first, start)
    return start


def attend_kernel(
    ids_ref, len_ref, alpha_ref, arr_ref, acol_ref, wa_ref, wo0_ref, wo1_ref, wo2_ref, wo3_ref,
    b0_ref, b1_ref, b2_ref, b3_ref, ob_ref,
    x_ref, q_ref, k_ref, v_ref, o_ref, l_ref, h_ref, attn_ref, wcat_ref, wo_ref, bias_ref,
    hot_ref,
):
    pieces, _, width, lanes = wa_ref.shape
    rows = arr_ref.shape[0]
    tensor = ids_ref[1]
    for j, (w, b) in enumerate(((wo0_ref, b0_ref), (wo1_ref, b1_ref), (wo2_ref, b2_ref), (wo3_ref, b3_ref))):
        slot = lax.bitwise_xor(tensor, j)
        wo_ref[slot] = w[...]
        bias_ref[slot] = b[...].astype(F32)
    for r in range(pieces):
        for c in range(3):
            wcat_ref[:, c * width + r * lanes : c * width + (r + 1) * lanes] = wa_ref[r, c]
    hot_ref[...] = one_hot_cols(acol_ref[:, 0:1], rows)
    x_ref[...] = dot(hot_ref[...], arr_ref[...]).astype(BF)
    for c, out in enumerate((q_ref, k_ref, v_ref)):
        proj = dot(x_ref[...], wcat_ref[:, c * width : (c + 1) * width])
        for r in range(pieces):
            part = proj[:, r * lanes : (r + 1) * lanes]
            if c != 1:
                part = part + bias_ref[r, c // 2 : c // 2 + 1, :]
            part = part.astype(BF)
            if c == 0:
                part = part * jnp.asarray(HEAD_SIZE**-0.5, BF)
            out[r] = part
    heads = lanes // HEAD_SIZE

    def pair(p, _):
        for i in range(rows // QT):
            n = (i + 1) * QT
            q_index = i * QT + iota((QT, 1), 0)
            start = starts_of(len_ref, q_index)
            k_index = iota((QT, n), 1)
            allowed = (k_index >= start) & (k_index <= q_index)
            q = q_ref[p, i * QT : n, :]
            lane = iota((QT, lanes), 1) // HEAD_SIZE
            k, v = k_ref[p, 0:n, :], v_ref[p, 0:n, :]
            mixed = jnp.zeros((QT, lanes), F32)
            for e in range(heads):
                scores = dot(jnp.where(lane == e, q, jnp.zeros_like(q)), k, NT)
                scores = jnp.where(allowed, scores, NEG)
                top = jnp.max(scores, axis=1, keepdims=True)
                weights = jnp.exp(scores - top)
                total = jnp.sum(weights, axis=1, keepdims=True)
                low = (weights * (1.0 / total)).astype(BF)
                mixed = jnp.where(lane == e, dot(low, v), mixed)
                log_total = jnp.broadcast_to(top + jnp.log(total), (QT, LANES))
                l_ref[p, e : e + 1, i * QT : n] = log_total.T[0:1, :]
            o_ref[p, i * QT : n, :] = mixed.astype(BF)
        return 0

    lax.fori_loop(0, pieces, pair, 0)
    attn = ob_ref[...].astype(F32)
    for r in range(pieces):
        attn = attn + dot(o_ref[r], wo_ref[r])
    attn_ref[...] = attn
    h_ref[...] = x_ref[...].astype(F32) + alpha_ref[0] * attn


def feed_kernel(
    ids_ref, alpha_ref, arr_ref, acol_ref, arow_ref, h_ref, attn_ref, o_ref, bias_ref, wo_ref, wu_ref, wd_ref, db_ref,
    ys_ref, go_ref, gh_ref, keep_ref, send_ref, small_ref,
    hot_ref, low_ref, gf_ref, f_ref,
):
    me, tensor = ids_ref[0], ids_ref[1]
    pieces, width, units = wu_ref.shape
    rows = arr_ref.shape[0]
    lanes = bias_ref.shape[2]
    blocks = keep_ref.shape[1]
    hot_ref[...] = one_hot_cols(acol_ref[:, 0:1], rows)
    grad = dot(hot_ref[...], arr_ref[...])
    gh_ref[...] = grad
    gf_ref[...] = (alpha_ref[1] * grad).astype(BF)
    low_ref[...] = h_ref[...].astype(BF)
    f_ref[...] = jnp.broadcast_to(db_ref[...].astype(F32), f_ref.shape)

    def place(r, first, value):
        slot = lax.bitwise_xor(r, tensor)
        count = value.shape[0] // blocks
        for parity, out in ((0, keep_ref), (1, send_ref)):

            @pl.when(slot % 2 == parity)
            def _():
                for b in range(blocks):
                    out[slot // 2, lax.bitwise_xor(me % blocks, b), first : first + count, :] = value[b * count : (b + 1) * count]

    def piece(r, _):
        bias = jnp.concatenate([bias_ref[r, 2 + b : 3 + b, :] for b in range(units // lanes)], axis=1)
        z = dot(low_ref[...], wu_ref[r]) + bias
        square = z * z
        tanh = jnp.tanh(z * (GELU_A + (GELU_A * GELU_B) * square))
        half = 0.5 * z
        act = (half + half * tanh).astype(BF)
        slope = (0.5 + 0.5 * tanh) + half * (1.0 - tanh * tanh) * (GELU_A + (3 * GELU_A * GELU_B) * square)
        f_ref[...] += dot(act, wd_ref[r])
        gz_full = dot(gf_ref[...], wd_ref[r], NT) * slope
        gz = gz_full.astype(BF)
        gh_ref[...] += dot(gz, wu_ref[r], NT)
        place(r, 0, dot(low_ref[...], gz, TN).astype(BF))
        place(r, width // blocks, dot(act, gf_ref[...], TN).astype(BF))
        small_ref[pl.ds(r, 1), :] = jnp.sum(gz.astype(F32), axis=0, keepdims=True)
        return 0

    lax.fori_loop(0, pieces, piece, 0)
    branch = f_ref[...]
    y = (h_ref[...] + alpha_ref[1] * branch).astype(BF)
    grad_hidden = gh_ref[...]
    ga = (alpha_ref[0] * grad_hidden).astype(BF)
    small_ref[4:5, :] = jnp.sum(ga.astype(F32), axis=0, keepdims=True)
    small_ref[5:6, :] = jnp.sum(gf_ref[...].astype(F32), axis=0, keepdims=True)
    small_ref[6:7, :] = jnp.sum(grad_hidden * attn_ref[...], axis=0, keepdims=True)
    for r in range(pieces):
        go_ref[r] = dot(ga, wo_ref[r], NT).astype(BF)
        place(jnp.int32(r), (width + units) // blocks, dot(o_ref[r], ga, TN).astype(BF))
    for c in range(rows // LANES):
        hot_ref[c * LANES : (c + 1) * LANES, :] = (iota((LANES, rows), 0) + c * LANES == arow_ref[0:1, :]).astype(F32).astype(BF)
    grad_tokens = dot(one_hot_cols(acol_ref[:, 0:1], rows), arr_ref[...])
    small_ref[7:8, :] = jnp.sum(grad_tokens * branch, axis=0, keepdims=True)
    ys_ref[...] = dot(hot_ref[...], y).astype(BF)


def back_kernel(
    pairs, len_ref, q_ref, k_ref, v_ref, go_ref, l_ref,
    grad_ref,
    gk_acc, gv_acc,
):
    _, rows, lanes = q_ref.shape
    heads = lanes // HEAD_SIZE
    scale = HEAD_SIZE**-0.5

    def pair(p, _):
        gk_acc[...] = jnp.zeros_like(gk_acc)
        gv_acc[...] = jnp.zeros_like(gv_acc)
        for i in range(rows // QT):
            n = (i + 1) * QT
            q_index = i * QT + iota((1, QT), 1)
            start = starts_of(len_ref, q_index)
            k_index = iota((n, QT), 0)
            allowed = (k_index >= start) & (k_index <= q_index)
            q, go = q_ref[p, i * QT : n, :], go_ref[p, i * QT : n, :]
            k, v = k_ref[p, 0:n, :], v_ref[p, 0:n, :]
            lane_q = iota((QT, lanes), 1) // HEAD_SIZE
            gq = jnp.zeros((QT, lanes), F32)
            for e in range(heads):
                q_e = jnp.where(lane_q == e, q, jnp.zeros_like(q))
                go_e = jnp.where(lane_q == e, go, jnp.zeros_like(go))
                scores = dot(k, q_e, NT) - l_ref[p, e : e + 1, i * QT : n]
                weights = jnp.exp(jnp.where(allowed, scores, NEG))
                grad_weights = dot(v, go_e, NT)
                inner = jnp.sum(weights * grad_weights, axis=0, keepdims=True)
                grad_scores = (weights * (grad_weights - inner)).astype(BF)
                gv_acc[0:n, :] += dot(weights.astype(BF), go_e)
                gk_acc[0:n, :] += dot(grad_scores, q_e)
                gq = jnp.where(lane_q == e, dot(grad_scores, k, TN), gq)
            grad_ref[0, p - pairs[0], i * QT : n, :] = (gq * scale).astype(BF)
        grad_ref[1, p - pairs[0]] = gk_acc[...].astype(BF)
        grad_ref[2, p - pairs[0]] = gv_acc[...].astype(BF)
        return 0

    lax.fori_loop(pairs[0], pairs[1], pair, 0)


def last_kernel(
    ids_ref, x_ref, grad_a_ref, grad_b_ref, gh_ref, wcat_ref, arow_ref, small1_ref,
    gxs_ref, keep_ref, send_ref, small_ref,
    grad_ref, hot_ref,
):
    me, tensor = ids_ref[0], ids_ref[1]
    rows, width = x_ref.shape
    half, lanes = grad_a_ref.shape[1], grad_a_ref.shape[3]
    pieces = 2 * half
    blocks = keep_ref.shape[1]
    for c in range(3):
        for r in range(pieces):
            first = c * width + r * lanes
            grad_ref[:, first : first + lanes] = grad_a_ref[c, r] if r < half else grad_b_ref[c, r - half]
    gx = gh_ref[...] + dot(grad_ref[...], wcat_ref[...], NT)
    for c in range(rows // LANES):
        hot_ref[c * LANES : (c + 1) * LANES, :] = (iota((LANES, rows), 0) + c * LANES == arow_ref[0:1, :]).astype(F32).astype(BF)
    gxs_ref[...] = dot(hot_ref[...], gx.astype(BF)).astype(BF)
    count = width // blocks
    small_ref[0:8, :] = small1_ref[...]
    small_ref[8:16, :] = jnp.zeros((8, width), F32)
    for c in range(3):
        grad_w = dot(x_ref[...], grad_ref[:, c * width : (c + 1) * width], TN).astype(BF)
        for r in range(pieces):
            slot = lax.bitwise_xor(jnp.int32(r), tensor)
            for parity, out in ((0, keep_ref), (1, send_ref)):

                @pl.when(slot % 2 == parity)
                def _():
                    for b in range(blocks):
                        out[slot // 2, lax.bitwise_xor(me % blocks, b), c * count : (c + 1) * count, :] = grad_w[
                            b * count : (b + 1) * count, r * lanes : (r + 1) * lanes
                        ]

        if c != 1:
            row = 8 + c // 2
            small_ref[row : row + 1, :] = jnp.sum(
                grad_ref[:, c * width : (c + 1) * width].astype(F32), axis=0, keepdims=True
            )


def parted_kernel(axis, keep_ref, got_ref, *refs):
    outs = refs[-2:]
    for i in range(keep_ref.shape[0]):
        for b in range(keep_ref.shape[1]):
            total = (keep_ref[i, b].astype(F32) + got_ref[i, b].astype(F32)).astype(BF)
            if axis == 0:
                outs[i][b] = total
            else:
                outs[b % 2][i, b // 2] = total


def joined_kernel(keep_ref, got_ref, *refs):
    for b in range(keep_ref.shape[0]):
        total = (keep_ref[b].astype(F32) + got_ref[b].astype(F32)).astype(BF)
        refs[-keep_ref.shape[0] + b][...] = total


def sum_kernel(count, *refs):
    total = refs[0][...].astype(F32)
    for r in refs[1:count]:
        total = total + r[...].astype(F32)
    refs[-1][...] = total.astype(refs[-1].dtype)


def spread_first_kernel(count, ids_ref, *refs):
    blocks, (up_ref, down_ref, out_ref) = refs[:count], refs[-3:]
    for j, ref in enumerate(blocks):
        slot = lax.bitwise_xor(ids_ref[0] % count, j)
        first = 0
        for out in (up_ref, down_ref, out_ref):
            size = out.shape[0] // count
            out[pl.ds(pl.multiple_of(slot * size, 8), size), :] = ref[first : first + size, :].astype(F32)
            first += size


def spread_second_kernel(count, ids_ref, *refs):
    out_ref = refs[-1]
    size = out_ref.shape[1] // count
    for j, ref in enumerate(refs[:count]):
        slot = lax.bitwise_xor(ids_ref[0] % count, j)
        for c in range(3):
            out_ref[c, pl.ds(pl.multiple_of(slot * size, 8), size), :] = ref[c * size : (c + 1) * size, :].astype(F32)


def widen_kernel(ids_ref, *refs):
    out_ref, step = refs[-1], pl.program_id(0)
    for j, ref in enumerate(refs[:4]):

        @pl.when(step == j)
        def _():
            out_ref[0] = ref[...].astype(F32)


def settle_kernel(r_ref, scol_ref, out_ref):
    out_ref[...] = dot(one_hot_cols(scol_ref[:, 0:1], r_ref.shape[0]), r_ref[...]).astype(BF)


def shape(dims, kind):
    return jax.ShapeDtypeStruct(dims, kind)


def call(kernel, ins, outs, scratch=(), deps=(), flops=1e6, nbytes=4 << 20, scalars=0):
    n_in, n_dep = len(ins), len(deps)

    def body(*refs):
        kernel(*refs[:n_in], *refs[n_in + n_dep :])

    return pl.pallas_call(
        body,
        out_shape=list(outs),
        in_specs=[smem()] * scalars + vmem(n_in - scalars) + [pl.BlockSpec(memory_space=pl.ANY)] * n_dep,
        out_specs=vmem(len(outs)),
        scratch_shapes=list(scratch),
        compiler_params=params(),
        cost_estimate=cost(flops, nbytes),
    )(*ins, *deps)


def per_device(
    block_input, cotangent, source, seq_lengths, qkv_weight, qv_bias, out_weight, out_bias,
    up_weight, up_bias, down_weight, down_bias, rezero_alphas,
):
    micros, rows, width = block_input.shape
    groups = lax.axis_size("dp")
    tensors = lax.axis_size("tensor")
    lanes = qkv_weight.shape[2]
    units = up_weight.shape[1]
    blocks = min(groups, 8)
    me, tensor = lax.axis_index("dp"), lax.axis_index("tensor")
    ids = jnp.stack([me, tensor]).astype(I32)
    lengths = lax.dynamic_index_in_dim(seq_lengths, tensor, 0, keepdims=False)[0]

    def across(axis, bit, value):
        count = tensors if axis == "tensor" else groups
        return lax.ppermute(value, axis, [(i, i ^ bit) for i in range(count)])

    def four(value):
        far = across("tensor", 2, value)
        return value, across("tensor", 1, value), far, across("tensor", 1, far)

    wa = lax.all_gather(qkv_weight, "tensor", axis=0)
    wu = lax.all_gather(up_weight, "tensor", axis=0)
    wd = lax.all_gather(down_weight, "tensor", axis=0)
    wo4 = four(out_weight)
    bias4 = four(jnp.concatenate([qv_bias, up_bias.reshape(units // lanes, lanes), jnp.zeros((2, lanes), BF)], axis=0))

    def by_micro(kernel, n_whole, out_shape, scratch):
        return pl.pallas_call(
            kernel,
            out_shape=out_shape,
            grid_spec=pltpu.PrefetchScalarGridSpec(
                num_scalar_prefetch=1,
                grid=(1,),
                in_specs=[
                    pl.BlockSpec(source.shape, lambda i, s: (0, 0)),
                    pl.BlockSpec((1, rows, width), lambda i, s: (s[1], 0, 0)),
                ]
                + [pl.BlockSpec((rows // LANES, LANES), lambda i, s: (0, 0))] * n_whole,
                out_specs=[pl.BlockSpec(o.shape, lambda i, s: (0, 0)) for o in out_shape],
                scratch_shapes=scratch,
            ),
            compiler_params=params(),
            cost_estimate=cost(2 * rows * rows * width, 4 << 20),
        )

    hot = pltpu.VMEM((rows, rows), BF)
    xs, srow, scol = by_micro(
        functools.partial(route_kernel, groups), 0,
        [shape((rows, width), BF), shape((rows // LANES, LANES), I32), shape((rows, LANES), I32)], [hot],
    )(ids, source, block_input)

    def exchange(rows_out):
        return lax.all_to_all(rows_out.reshape(groups, rows // groups, width), "dp", 0, 0, tiled=True).reshape(rows, width)

    arr_x = exchange(xs)
    gs, arow, acol = by_micro(
        second_kernel, 1,
        [shape((rows, width), BF), shape((8, rows), I32), shape((rows, LANES), I32)], [hot],
    )(ids, source, cotangent, srow)
    arr_g = exchange(gs)

    heads3 = [shape((tensors, rows, lanes), BF)] * 4
    x, q, k, v, o, logs, h, attn, wcat, wo, bias = call(
        attend_kernel,
        (ids, lengths, rezero_alphas, arr_x, acol, wa, *wo4, *bias4, out_bias.reshape(1, width)),
        [shape((rows, width), BF), *heads3, shape((tensors, 8, rows), F32),
         shape((rows, width), F32), shape((rows, width), F32), shape((width, 3 * width), BF),
         shape((tensors, lanes, width), BF), shape((tensors, 8, lanes), F32)],
        [hot], scalars=3, flops=27e9, nbytes=16 << 20,
    )

    bundle = (width + units + lanes) // blocks
    part = shape((tensors // 2, blocks, bundle, width), BF)
    ys, go, gh, keep1, send1, small1 = call(
        feed_kernel,
        (ids, rezero_alphas, arr_g, acol, arow, h, attn, o, bias, wo, wu, wd, down_bias.reshape(1, width)),
        [shape((rows, width), BF), shape((tensors, rows, lanes), BF), shape((rows, width), F32), part, part,
         shape((8, width), F32)],
        [hot, pltpu.VMEM((rows, width), BF), pltpu.VMEM((rows, width), BF), pltpu.VMEM((rows, width), F32)],
        scalars=2, flops=31e9, nbytes=24 << 20,
    )
    arr_y = exchange(ys)
    got = across("tensor", 1, send1)

    def back(first, last, deps):
        return call(
            functools.partial(back_kernel, (first, last)), (lengths, q, k, v, go, logs),
            [shape((3, last - first, rows, lanes), BF)], [pltpu.VMEM((rows, lanes), F32)] * 2,
            scalars=1, flops=14e9, nbytes=8 << 20, deps=deps,
        )[0]

    half = tensors // 2

    def by_core(keep, got, deps):
        k_shape = shape((keep.shape[0], blocks // 2, *keep.shape[2:]), BF)
        return call(functools.partial(parted_kernel, 1), (keep, got), [k_shape, k_shape], deps=deps)

    def by_low(keep, got, deps):
        k_shape = shape(keep.shape[1:], BF)
        return call(functools.partial(parted_kernel, 0), (keep, got), [k_shape, k_shape], deps=deps)

    def by_far(keep, got, deps):
        return call(joined_kernel, (keep, got), [shape(keep.shape[1:], BF)] * (blocks // 2), deps=deps)

    def high(value):
        return [across("dp", 2 * j, v) for j, v in enumerate(value) if j]

    def total(values, kind, deps=()):
        return call(functools.partial(sum_kernel, len(values)), values, [shape(values[0].shape, kind)], deps=deps)[0]

    def rest(value, kind):
        bit = blocks
        while bit < groups:
            value = total((value, across("dp", bit, value)), kind)
            bit *= 2
        return value

    def gather(own):
        even = [own] + [across("dp", 2 * j, own) for j in range(1, blocks // 2)]
        odd = [across("dp", 1, e) for e in even]
        return [b for pair in zip(even, odd) for b in pair]

    grad_a = back(0, half, (keep1,))
    keep1, send1 = by_core(keep1, got, (grad_a,))
    got = across("dp", 1, send1)
    grad_b = back(half, tensors, (keep1,))

    def settle(rows_back, deps):
        return call(settle_kernel, (rows_back, scol), [shape((rows, width), BF)], deps=deps, flops=1e9)[0]

    def widen(four_parts):
        return pl.pallas_call(
            widen_kernel,
            out_shape=shape((tensors, rows, width), F32),
            grid_spec=pltpu.PrefetchScalarGridSpec(
                num_scalar_prefetch=1,
                grid=(tensors,),
                in_specs=[pl.BlockSpec((rows, width), lambda i, s: (0, 0))] * 4,
                out_specs=pl.BlockSpec((1, rows, width), lambda i, s: (lax.bitwise_xor(s[1], i), 0, 0)),
            ),
            compiler_params=params(),
            cost_estimate=cost(1e6, 12 << 20),
        )(ids, *four_parts)

    y_own = settle(arr_y, (grad_b,))
    y4 = four(y_own)
    share = (3 * width) // blocks
    part = shape((half, blocks, share, lanes), BF)
    gxs, keep2, send2, small = call(
        last_kernel, (ids, x, grad_a, grad_b, gh, wcat, arow, small1),
        [shape((rows, width), BF), part, part, shape((16, width), F32)],
        [pltpu.VMEM((rows, 3 * width), BF), hot], scalars=1, flops=7e9, nbytes=8 << 20, deps=(y_own,),
    )
    arr_gx = exchange(gxs)
    got2 = across("tensor", 1, send2)
    got3 = across("tensor", 1, small)
    keep1, send1 = by_low(keep1, got, (gxs,))
    got = across("tensor", 2, send1)
    keep2, send2 = by_core(keep2, got2, (keep1,))
    got2 = across("dp", 1, send2)
    small = total((small, got3), F32)
    got3 = across("dp", 1, small)
    blocks1 = call(joined_kernel, (keep1, got), [shape(keep1.shape[1:], BF)] * (blocks // 2), deps=(keep2,))
    got1 = high(blocks1)
    keep2, send2 = by_low(keep2, got2, (blocks1[0],))
    got2 = across("tensor", 2, send2)
    small = total((small, got3), F32)
    got3 = across("tensor", 2, small)
    own1 = rest(total((blocks1[0], *got1), BF, (keep2,)), BF)
    all1 = gather(own1)
    gx_own = settle(arr_gx, (own1,))
    gx4 = four(gx_own)
    blocks2 = call(joined_kernel, (keep2, got2), [shape(keep2.shape[1:], BF)] * (blocks // 2), deps=(gx_own,))
    got2 = high(blocks2)
    small = total((small, got3), F32, (blocks2[0],))
    small = total((small, *[across("dp", 2 * j, small) for j in range(1, blocks // 2)]), F32)
    own2 = rest(total((blocks2[0], *got2), BF, (gx_own,)), BF)
    all2 = gather(own2)
    small = rest(small, F32)
    layer_output = widen(y4)
    up_grad, down_grad, out_grad = call(
        functools.partial(spread_first_kernel, blocks), (ids, *all1),
        [shape((width, units), F32), shape((units, width), F32), shape((lanes, width), F32)], scalars=1,
    )
    qkv_grad = call(
        functools.partial(spread_second_kernel, blocks), (ids, *all2), [shape((3, width, lanes), F32)], scalars=1
    )[0]
    input_grad = widen(gx4)
    up_bias_grad = lax.dynamic_index_in_dim(small, tensor, 0, keepdims=False)
    qv_bias_grad = lax.dynamic_slice_in_dim(small[8:10], tensor * lanes, lanes, 1)
    return (
        layer_output,
        input_grad,
        qkv_grad,
        qv_bias_grad,
        out_grad,
        small[4],
        up_grad,
        up_bias_grad,
        down_grad,
        small[5],
        jnp.sum(small[6:8], axis=1),
    )


def solution(mesh):
    in_specs = (
        P(None, "dp", None), P(None, "dp", None), P(), P(None, "dp", None),
        P(None, None, "tensor"), P(None, "tensor"), P("tensor", None), P(),
        P(None, "tensor"), P("tensor"), P("tensor", None), P(), P(),
    )
    out_specs = (
        P(None, "dp", None), P(None, "dp", None), P(None, None, "tensor"), P(None, "tensor"),
        P("tensor", None), P(), P(None, "tensor"), P("tensor"), P("tensor", None), P(), P(),
    )
    return jax.shard_map(per_device, mesh=mesh, in_specs=in_specs, out_specs=out_specs, check_vma=False)
```

```python
import functools

import jax
import jax.numpy as jnp
from jax import lax
from jax.experimental import pallas as pl
from jax.experimental.pallas import tpu as pltpu
from jax.sharding import PartitionSpec as P

HEAD_SIZE = 64
LANES = 128
QT = 256
FT = 512
BF = jnp.bfloat16
F32 = jnp.float32
SCALE = 3.0
I32 = jnp.int32
NEG = -1e30
VMEM_LIMIT = 56 * 1024 * 1024
GELU_A = 0.7978845608028654
GELU_B = 0.044715

NN = (((1,), (0,)), ((), ()))
NT = (((1,), (1,)), ((), ()))
TN = (((0,), (0,)), ((), ()))


def dot(a, b, dims=NN):
    return lax.dot_general(a, b, dims, preferred_element_type=F32)


def iota(shape, dim):
    return lax.broadcasted_iota(I32, shape, dim)


def params(limit=VMEM_LIMIT):
    return pltpu.CompilerParams(vmem_limit_bytes=limit)


def cost(flops, nbytes, trans=0):
    return pl.CostEstimate(flops=int(flops), bytes_accessed=int(nbytes), transcendentals=int(trans))


def vmem(n):
    return [pl.BlockSpec(memory_space=pltpu.VMEM)] * n


def smem():
    return pl.BlockSpec(memory_space=pltpu.SMEM)


def one_hot_rows(row, count):
    return (iota((count, row.shape[1]), 0) == row).astype(F32).astype(BF)


def one_hot_cols(col, count):
    return (iota((col.shape[0], count), 1) == col).astype(F32).astype(BF)


def route_kernel(groups, ids_ref, src_ref, x_ref, xs_ref, srow_ref, scol_ref, hot_ref):
    me, micro = ids_ref[0], ids_ref[1]
    rows = x_ref.shape[1]
    chunks = rows // LANES
    share = rows // groups
    sub_hi = iota((chunks, rows), 0)
    sub_lo = iota((LANES, rows), 0)

    def gather_group(g, total):
        value = src_ref[pl.ds(micro, 1), pl.ds(pl.multiple_of(g * rows, LANES), rows)] - me * rows
        inside = (value >= 0) & (value < rows)
        high = jnp.where(inside, value // LANES, -1)
        low = jnp.where(inside, value % LANES, -1)
        hot_high = jnp.where(high == sub_hi, (g + 1).astype(F32), 0.0).astype(BF)
        hot_low = (low == sub_lo).astype(F32).astype(BF)
        return total + dot(hot_high, hot_low, NT)

    dest = lax.fori_loop(0, groups, gather_group, jnp.zeros((chunks, LANES), F32)).astype(I32) - 1
    before = (iota((LANES, LANES), 0) < iota((LANES, LANES), 1)).astype(F32).astype(BF)
    width = max(groups, 8)
    carry = jnp.zeros((width, 1), F32)
    for c in range(chunks):
        g_row = dest[c : c + 1, :]
        hot = (iota((width, LANES), 0) == g_row).astype(F32)
        ranks = dot(hot.astype(BF), before) + carry
        carry = carry + jnp.sum(hot, axis=1, keepdims=True)
        place = g_row * share + jnp.sum(hot * ranks, axis=0, keepdims=True).astype(I32)
        srow_ref[c : c + 1, :] = place
        spread = jnp.broadcast_to(place.astype(F32), (LANES, LANES))
        scol_ref[c * LANES : (c + 1) * LANES, :] = spread.T.astype(I32)
        hot_ref[:, c * LANES : (c + 1) * LANES] = one_hot_rows(place, rows)
    xs_ref[...] = dot(hot_ref[...], x_ref[0]).astype(BF)


def second_kernel(ids_ref, src_ref, g_ref, srow_ref, gs_ref, arow_ref, acol_ref, hot_ref):
    me, micro = ids_ref[0], ids_ref[1]
    rows = g_ref.shape[1]
    for c in range(rows // LANES):
        hot_ref[:, c * LANES : (c + 1) * LANES] = one_hot_rows(srow_ref[c : c + 1, :], rows)
    gs_ref[...] = dot(hot_ref[...], g_ref[0]).astype(BF)
    own = src_ref[pl.ds(micro, 1), pl.ds(pl.multiple_of(me * rows, LANES), rows)].astype(F32)
    for c in range(rows // LANES):
        piece = own[:, c * LANES : (c + 1) * LANES]
        column = jnp.broadcast_to(piece, (LANES, LANES)).T[:, 0:1]
        count = jnp.sum((own < column).astype(F32), axis=1, keepdims=True)
        spread = jnp.broadcast_to(count, (LANES, LANES))
        acol_ref[c * LANES : (c + 1) * LANES, :] = spread.astype(I32)
        arow_ref[0:1, c * LANES : (c + 1) * LANES] = spread.T[0:1, :].astype(I32)


def starts_of(len_ref, index):
    start = jnp.zeros_like(index)
    first = jnp.int32(0)
    for j in range(len_ref.shape[0] - 1):
        first = first + len_ref[j]
        start = jnp.where(index >= first, first, start)
    return start


class Copies:
    def __init__(self, sems):
        self.sems, self.used, self.left = sems, 0, []

    def start(self, source, target):
        copy = pltpu.make_async_copy(source, target, self.sems.at[self.used])
        self.used += 1
        copy.start()
        return copy

    def send(self, source, target):
        self.left.append(self.start(source, target))

    def finish(self):
        for copy in self.left:
            copy.wait()


def wait_all(copies):
    for copy in copies:
        copy.wait()


def attend_kernel(
    ids_ref, len_ref, alpha_ref, b0_ref, b1_ref, b2_ref, b3_ref, ob_ref, acol_ref,
    arr_any, wa0_any, wa1_any, wa2_any, wa3_any, wo0_any, wo1_any, wo2_any, wo3_any,
    l_ref, x_any, q_any, k_any, v_any, o_any, h_any, low_any, attn_any,
    sems, arr_ref, wcat_ref, wo_ref, bias_ref, hot_ref, x_ref, q_ref, k_ref, v_ref, of_ref, ob16_ref, h_ref, low_ref, attn_ref,
):
    rows, width = arr_ref.shape
    lanes = wo0_any.shape[0]
    pieces = width // lanes
    heads = lanes // HEAD_SIZE
    tensor = ids_ref[1]
    copies = Copies(sems)
    first = copies.start(arr_any, arr_ref)
    weights, later = [], []
    for j, (wa, wo, b) in enumerate(
        ((wa0_any, wo0_any, b0_ref), (wa1_any, wo1_any, b1_ref), (wa2_any, wo2_any, b2_ref), (wa3_any, wo3_any, b3_ref))
    ):
        place = pl.multiple_of(lax.bitwise_xor(tensor, j) * lanes, LANES)
        for c in range(3):
            weights.append(copies.start(wa.at[c], wcat_ref.at[:, pl.ds(c * width + place, lanes)]))
        later.append(copies.start(wo, wo_ref.at[pl.ds(place, lanes), :]))
        bias_ref[:, pl.ds(place, lanes)] = b[...].astype(F32)
    hot_ref[...] = one_hot_cols(acol_ref[:, 0:1], rows)
    first.wait()
    x_ref[...] = dot(hot_ref[...], arr_ref[...]).astype(BF)
    copies.send(x_ref, x_any)
    wait_all(weights)
    q_ref[...] = (dot(x_ref[...], wcat_ref[:, 0:width]) + bias_ref[0:1, :]).astype(BF) * jnp.asarray(HEAD_SIZE**-0.5, BF)
    k_ref[...] = dot(x_ref[...], wcat_ref[:, width : 2 * width]).astype(BF)
    v_ref[...] = (dot(x_ref[...], wcat_ref[:, 2 * width :]) + bias_ref[1:2, :]).astype(BF)
    copies.send(q_ref, q_any)
    copies.send(k_ref, k_any)
    copies.send(v_ref, v_any)
    tiles = rows // QT
    lane = iota((QT, lanes), 1) // HEAD_SIZE
    lane_all = iota((rows, lanes), 1) // HEAD_SIZE
    masks = []
    for i in range(tiles):
        q_index = i * QT + iota((QT, 1), 0)
        k_index = iota((QT, (i + 1) * QT), 1)
        masks.append((k_index >= starts_of(len_ref, q_index)) & (k_index <= q_index))

    def scores_of(p, i, e):
        q = q_ref[i * QT : (i + 1) * QT, p * lanes : (p + 1) * lanes]
        return dot(jnp.where(lane == e, q, jnp.zeros_like(q)), k_ref[0 : (i + 1) * QT, p * lanes : (p + 1) * lanes], NT)

    items = [(p, i, e) for i in range(tiles) for p in range(pieces) for e in range(heads)]
    ahead = scores_of(*items[0])
    mixed = logs = None
    for step, (p, i, e) in enumerate(items):
        now = ahead
        if step + 1 < len(items):
            ahead = scores_of(*items[step + 1])
        scores = jnp.where(masks[i], now, NEG)
        top = jnp.max(scores, axis=1, keepdims=True)
        low = jnp.exp(scores - top).astype(BF)
        v = v_ref[0 : (i + 1) * QT, p * lanes : (p + 1) * lanes]
        out = dot(low, jnp.where(lane_all[0 : (i + 1) * QT] == e, v, jnp.ones_like(v)))
        other = HEAD_SIZE if e == 0 else 0
        total = out[:, other : other + 1]
        out = out * (1.0 / total)
        head = p * heads + e
        log_total = top + jnp.log(total)
        logs = jnp.where(iota((QT, LANES), 1) == head, log_total, 0.0 if head == 0 else logs)
        mixed = out if e == 0 else jnp.where(lane == e, out, mixed)
        if e == heads - 1:
            of_ref[i * QT : (i + 1) * QT, p * lanes : (p + 1) * lanes] = mixed
            ob16_ref[i * QT : (i + 1) * QT, p * lanes : (p + 1) * lanes] = mixed.astype(BF)
        if head == pieces * heads - 1:
            l_ref[:, i * QT : (i + 1) * QT] = logs.T[0 : pieces * heads, :]
            if i == 0:
                wait_all(later)
            span = slice(i * QT, (i + 1) * QT)
            copies.send(of_ref.at[span], o_any.at[span])
            attn = dot(ob16_ref[span, :], wo_ref[...]) + ob_ref[...].astype(F32)
            hidden = x_ref[span, :].astype(F32) + alpha_ref[0] * attn
            attn_ref[span, :] = attn
            h_ref[span, :] = hidden
            low_ref[span, :] = hidden.astype(BF)
            copies.send(attn_ref.at[span], attn_any.at[span])
            copies.send(h_ref.at[span], h_any.at[span])
            copies.send(low_ref.at[span], low_any.at[span])
    copies.finish()


def forward_kernel(
    alpha_ref, b0_ref, b1_ref, b2_ref, b3_ref, db_ref, arow_ref,
    low_any, h_any, wu0_any, wu1_any, wu2_any, wu3_any, wd0_any, wd1_any, wd2_any, wd3_any,
    ys_any, act_any, slope_any, f_any,
    sems, low_ref, h_ref, wu_ref, wd_ref, act_ref, slope_ref, f_ref, y_ref, hot_ref, ys_ref,
):
    rows, width = low_ref.shape
    units = wu0_any.shape[1]
    copies = Copies(sems)
    first = copies.start(low_any, low_ref)
    up, down = [], []
    for j, wu in enumerate((wu0_any, wu1_any, wu2_any, wu3_any)):
        up.append(copies.start(wu, wu_ref.at[:, j * units : (j + 1) * units]))
    for j, wd in enumerate((wd0_any, wd1_any, wd2_any, wd3_any)):
        down.append(copies.start(wd, wd_ref.at[j * units : (j + 1) * units, :]))
    hidden = copies.start(h_any, h_ref)
    biases = []
    for b in (b0_ref, b1_ref, b2_ref, b3_ref):
        tail = b[...].astype(F32)
        biases.append(jnp.concatenate([tail[2 + n : 3 + n, :] for n in range(units // LANES)], axis=1))
    first.wait()
    items = [(j, m) for j in range(len(biases)) for m in range(rows // FT)]

    def z_of(j, m):
        if m == 0:
            up[j].wait()
        return dot(low_ref[m * FT : (m + 1) * FT, :], wu_ref[:, j * units : (j + 1) * units])

    ahead = z_of(*items[0])
    for step, (j, m) in enumerate(items):
        z = ahead + biases[j]
        if step + 1 < len(items):
            ahead = z_of(*items[step + 1])
        square = z * z
        tanh = jnp.tanh(z * (GELU_A + (GELU_A * GELU_B) * square))
        half = 0.5 * z
        rise = 0.5 + 0.5 * tanh
        span = (slice(m * FT, (m + 1) * FT), slice(j * units, (j + 1) * units))
        act_ref[span] = (z * rise).astype(BF)
        slope_ref[span] = (rise + half * (1.0 - tanh * tanh) * (GELU_A + (3 * GELU_A * GELU_B) * square)).astype(BF)
        if m == rows // FT - 1:
            copies.send(act_ref.at[:, span[1]], act_any.at[:, span[1]])
            copies.send(slope_ref.at[:, span[1]], slope_any.at[:, span[1]])
    wait_all(down)
    hidden.wait()
    for m in range(rows // FT):
        span = slice(m * FT, (m + 1) * FT)
        branch = dot(act_ref[span, :], wd_ref[...]) + db_ref[...].astype(F32)
        f_ref[span, :] = branch
        copies.send(f_ref.at[span], f_any.at[span])
        y_ref[span, :] = (h_ref[span, :] + alpha_ref[1] * branch).astype(BF)
        hot_ref[span, :] = (iota((FT, rows), 0) + m * FT == arow_ref[0:1, :]).astype(F32).astype(BF)
    for m in range(rows // FT):
        span = slice(m * FT, (m + 1) * FT)
        ys_ref[span, :] = dot(hot_ref[span, :], y_ref[...]).astype(BF)
        copies.send(ys_ref.at[span], ys_any.at[span])
    copies.finish()


def feed_kernel(
    ids_ref, alpha_ref, acol_ref,
    arr_any, wu0_any, wu1_any, wu2_any, wu3_any, wd0_any, wd1_any, wd2_any, wd3_any,
    wo0_any, wo1_any, wo2_any, wo3_any, act_any, slope_any, low_any, f_any, attn_any, o_any,
    small_ref, d_ref, go_any, gh_any, keep_any, send_any,
    sems, arr_ref, wu_ref, wd_ref, wo_ref, act_ref, slope_ref, low_ref, f_ref, attn_ref, o_ref,
    hot_ref, g_ref, gf_ref, gz_ref, gh_ref, ga_ref, go_ref, part_ref,
):
    me, tensor = ids_ref[0], ids_ref[1]
    rows, width = low_ref.shape
    units = wu0_any.shape[1]
    lanes = wo0_any.shape[0]
    blocks = part_ref.shape[1]
    own = me % blocks
    copies = Copies(sems)
    first = copies.start(arr_any, arr_ref)
    down, slopes, up, later = [], [], [], []
    for j, wd in enumerate((wd0_any, wd1_any, wd2_any, wd3_any)):
        span = slice(j * units, (j + 1) * units)
        down.append(copies.start(wd, wd_ref.at[span, :]))
        slopes.append(copies.start(slope_any.at[:, span], slope_ref.at[:, span]))
    for j, wu in enumerate((wu0_any, wu1_any, wu2_any, wu3_any)):
        up.append(copies.start(wu, wu_ref.at[:, j * units : (j + 1) * units]))
    lowed = copies.start(low_any, low_ref)
    acted = copies.start(act_any, act_ref)
    for j, wo in enumerate((wo0_any, wo1_any, wo2_any, wo3_any)):
        place = pl.multiple_of(lax.bitwise_xor(tensor, j) * lanes, LANES)
        later.append(copies.start(wo, wo_ref.at[pl.ds(place, lanes), :]))
    later.append(copies.start(attn_any, attn_ref))
    later.append(copies.start(o_any, o_ref))
    branched = copies.start(f_any, f_ref)
    hot_ref[...] = one_hot_cols(acol_ref[:, 0:1], rows)
    first.wait()
    for m in range(rows // FT):
        span = slice(m * FT, (m + 1) * FT)
        grad = dot(hot_ref[span, :], arr_ref[...])
        g_ref[span, :] = grad.astype(BF)
        gf_ref[span, :] = (alpha_ref[1] * grad).astype(BF)
    items = [(j, m) for j in range(len(up)) for m in range(rows // FT)]

    def ga_of(j, m):
        if m == 0:
            down[j].wait()
        return dot(gf_ref[m * FT : (m + 1) * FT, :], wd_ref[j * units : (j + 1) * units, :], NT)

    ahead = ga_of(*items[0])
    for step, (j, m) in enumerate(items):
        now = ahead
        if step + 1 < len(items):
            ahead = ga_of(*items[step + 1])
        if m == 0:
            slopes[j].wait()
        span = (slice(m * FT, (m + 1) * FT), slice(j * units, (j + 1) * units))
        gz_ref[span] = (now * slope_ref[span].astype(F32)).astype(BF)
    wait_all(up)
    wait_all(later)
    gh_sum = attn_sum = jnp.zeros((1, width), F32)
    for m in range(rows // FT):
        span = slice(m * FT, (m + 1) * FT)
        grad_hidden = g_ref[span, :].astype(F32) + dot(gz_ref[span, :], wu_ref[...], NT)
        gh_ref[span, :] = grad_hidden
        copies.send(gh_ref.at[span], gh_any.at[span])
        ga = (alpha_ref[0] * grad_hidden).astype(BF)
        ga_ref[span, :] = ga
        gh_sum = gh_sum + jnp.sum(ga.astype(F32), axis=0, keepdims=True)
        attn_sum = attn_sum + jnp.sum(grad_hidden * attn_ref[span, :], axis=0, keepdims=True)
    select = (iota((8, width), 1) // HEAD_SIZE == iota((8, width), 0)).astype(F32).astype(BF)
    for m in range(rows // FT):
        span = slice(m * FT, (m + 1) * FT)
        go = dot(ga_ref[span, :], wo_ref[...], NT).astype(BF)
        go_ref[span, :] = go
        copies.send(go_ref.at[span], go_any.at[span])
        product = go.astype(F32) * o_ref[span, :]
        high = product.astype(BF)
        d_ref[:, span] = dot(select, high, NT) + dot(select, (product - high.astype(F32)).astype(BF), NT)

    def place(j, first_row, value):
        count = value.shape[0] // blocks
        for b in range(blocks):
            part_ref[j, lax.bitwise_xor(own, b), first_row : first_row + count, :] = value[b * count : (b + 1) * count]

    lowed.wait()
    acted.wait()
    low_t = low_ref[...].T
    gf_t = gf_ref[...].T
    o_t = o_ref[...].astype(BF).T
    out_grad = dot(o_t, ga_ref[...]).astype(BF)
    hot_ref[0:width, 0:width] = out_grad
    edge = (width + units) // blocks
    for j in range(len(up)):
        span = slice(j * units, (j + 1) * units)
        place(j, 0, dot(low_t, gz_ref[:, span]).astype(BF))
        place(j, width // blocks, dot(gf_t, act_ref[:, span]).astype(BF))
        at = pl.multiple_of(lax.bitwise_xor(tensor, j) * lanes, LANES)
        place(j, edge, hot_ref[pl.ds(at, lanes), 0:width])
        out = keep_any if j % 2 == 0 else send_any
        copies.send(part_ref.at[j], out.at[j // 2])
        small_ref[pl.ds(lax.bitwise_xor(tensor, j), 1), :] = jnp.sum(gz_ref[:, span].astype(F32), axis=0, keepdims=True)
    branched.wait()
    small_ref[4:5, :] = gh_sum
    small_ref[5:6, :] = jnp.sum(gf_ref[...].astype(F32), axis=0, keepdims=True)
    small_ref[6:7, :] = attn_sum
    small_ref[7:8, :] = jnp.sum(g_ref[...].astype(F32) * f_ref[...], axis=0, keepdims=True)
    copies.finish()


def starts_of(len_ref, index):
    start = jnp.zeros_like(index)
    first = jnp.int32(0)
    for j in range(len_ref.shape[0] - 1):
        first = first + len_ref[j]
        start = jnp.where(index >= first, first, start)
    return start


def back_kernel(
    first_pair, len_ref, l_ref, d_ref, q_any, k_any, v_any, go_any,
    grad_any,
    sems, q_ref, k_ref, v_ref, go_ref, grad_ref, gq_ref,
):
    rows, width = q_ref.shape
    lanes = 2 * HEAD_SIZE
    heads = 2
    pairs = width // lanes
    scale = HEAD_SIZE**-0.5
    copies = Copies(sems)
    columns = slice(first_pair * lanes, first_pair * lanes + width)
    ins = [copies.start(a.at[:, columns], r) for a, r in ((q_any, q_ref), (k_any, k_ref), (v_any, v_ref), (go_any, go_ref))]
    tiles = rows // QT
    lane = iota((QT, lanes), 1) // HEAD_SIZE
    masks = []
    for j in range(tiles):
        q_index = j * QT + iota((1, rows - j * QT), 1)
        k_index = j * QT + iota((QT, rows - j * QT), 0)
        masks.append((k_index >= starts_of(len_ref, q_index)) & (k_index <= q_index))
    wait_all(ins)
    items = [(p, j, e) for p in range(pairs) for j in range(tiles) for e in range(heads)]

    def pick(ref, p, j, e):
        value = ref[j * QT : (j + 1) * QT, p * lanes : (p + 1) * lanes]
        return jnp.where(lane == e, value, jnp.zeros_like(value))

    def both_of(p, j, e):
        pair = (slice(j * QT, rows), slice(p * lanes, (p + 1) * lanes))
        return dot(pick(k_ref, p, j, e), q_ref[pair], NT), dot(pick(v_ref, p, j, e), go_ref[pair], NT)

    ahead = both_of(*items[0])
    gk = gv = None
    for step, (p, j, e) in enumerate(items):
        scores, grad_weights = ahead
        if step + 1 < len(items):
            ahead = both_of(*items[step + 1])
        head = (first_pair + p) * heads + e
        pair = (slice(j * QT, rows), slice(p * lanes, (p + 1) * lanes))
        weights = jnp.exp(jnp.where(masks[j], scores - l_ref[head : head + 1, j * QT :], NEG))
        grad_scores = (weights * (grad_weights - d_ref[head : head + 1, j * QT :])).astype(BF)
        gv_e = dot(weights.astype(BF), go_ref[pair])
        gk_e = dot(grad_scores, q_ref[pair])
        gq = dot(grad_scores, pick(k_ref, p, j, e), TN)
        if j == 0 and e == 0:
            gq_ref[...] = gq
        else:
            gq_ref[j * QT :, :] += gq
        gk = gk_e if e == 0 else jnp.where(lane == e, gk_e, gk)
        gv = gv_e if e == 0 else jnp.where(lane == e, gv_e, gv)
        if e == heads - 1:
            span = (slice(j * QT, (j + 1) * QT), slice(p * lanes, (p + 1) * lanes))
            grad_ref[(1, *span)] = gk.astype(BF)
            grad_ref[(2, *span)] = gv.astype(BF)
            grad_ref[(0, *span)] = (gq_ref[j * QT : (j + 1) * QT, :] * scale).astype(BF)
            if j == tiles - 1:
                copies.send(grad_ref.at[:, :, p * lanes : (p + 1) * lanes], grad_any.at[:, :, p * lanes : (p + 1) * lanes])
    copies.finish()


def split_small(value, out_ref):
    chunks = value.shape[1] // LANES
    for c in range(chunks):
        left = value[:, c * LANES : (c + 1) * LANES]
        for k in range(3):
            term = left.astype(BF)
            first = (k * chunks + c) * 16
            out_ref[first : first + 16, :] = term
            left = left - term.astype(F32)


def join_small(ref, width):
    chunks = width // LANES
    parts = []
    for c in range(chunks):
        terms = [ref[(k * chunks + c) * 16 : (k * chunks + c + 1) * 16, :].astype(F32) for k in range(3)]
        parts.append(terms[0] + terms[1] + terms[2])
    return jnp.concatenate(parts, axis=1)


def last_kernel(
    ids_ref, small1_ref, arow_ref, grad_a_any, grad_b_any, gh_any, x_any, wa0_any, wa1_any, wa2_any, wa3_any,
    small_ref, gxs_any, keep_any, send_any,
    sems, grad_ref, gh_ref, x_ref, wcat_ref, hot_ref, gx_ref, gxs_ref, part_ref, w_ref, split_ref,
):
    me, tensor = ids_ref[0], ids_ref[1]
    rows, width = x_ref.shape
    lanes = wa0_any.shape[2]
    half = width // 2
    blocks = part_ref.shape[1]
    own = me % blocks
    copies = Copies(sems)
    ins, grads, weights = [], [], []
    for c in range(3):
        for n, g in enumerate((grad_a_any, grad_b_any)):
            grads.append(copies.start(g.at[c], grad_ref.at[:, c * width + n * half : c * width + (n + 1) * half]))
    for j, wa in enumerate((wa0_any, wa1_any, wa2_any, wa3_any)):
        place = pl.multiple_of(lax.bitwise_xor(tensor, j) * lanes, LANES)
        for c in range(3):
            weights.append(copies.start(wa.at[c], wcat_ref.at[:, pl.ds(c * width + place, lanes)]))
    ins.append(copies.start(gh_any, gh_ref))
    xs = copies.start(x_any, x_ref)
    for m in range(rows // FT):
        hot_ref[m * FT : (m + 1) * FT, :] = (iota((FT, rows), 0) + m * FT == arow_ref[0:1, :]).astype(F32).astype(BF)
    wait_all(grads)
    wait_all(weights)
    wait_all(ins)
    for m in range(rows // FT):
        span = slice(m * FT, (m + 1) * FT)
        gx_ref[span, :] = (gh_ref[span, :] + dot(grad_ref[span, :], wcat_ref[...], NT)).astype(BF)
    for m in range(rows // FT):
        span = slice(m * FT, (m + 1) * FT)
        gxs_ref[span, :] = dot(hot_ref[span, :], gx_ref[...]).astype(BF)
        copies.send(gxs_ref.at[span], gxs_any.at[span])
    xs.wait()
    x_t = x_ref[...].T
    count = width // blocks
    small_ref[0:8, :] = small1_ref[...]
    small_ref[8:16, :] = jnp.zeros((8, width), F32)
    for c in range(3):
        span = slice(c * width, (c + 1) * width)
        w_ref[:, span] = dot(x_t, grad_ref[:, span]).astype(BF)
        if c != 1:
            row = 8 + c // 2
            small_ref[row : row + 1, :] = jnp.sum(grad_ref[:, span].astype(F32), axis=0, keepdims=True)
    for j in range(width // lanes):
        at = pl.multiple_of(lax.bitwise_xor(tensor, j) * lanes, LANES)
        for c in range(3):
            for b in range(blocks):
                part_ref[j, lax.bitwise_xor(own, b), c * count : (c + 1) * count, :] = w_ref[
                    b * count : (b + 1) * count, pl.ds(c * width + at, lanes)
                ]
        out = keep_any if j % 2 == 0 else send_any
        copies.send(part_ref.at[j], out.at[pl.ds(j // 2 * blocks, blocks)])
    split_small(small_ref[...], split_ref)
    copies.send(split_ref, send_any.at[send_any.shape[0] - 1])
    copies.finish()


def added(a, b):
    return (a.astype(F32) + b.astype(F32)).astype(BF)


def halve_kernel(pick, keep_ref, got_ref, next_ref, send_ref):
    here = there = 0
    for b in range(keep_ref.shape[0]):
        total = added(keep_ref[b], got_ref[b])
        if pick(b):
            next_ref[here] = total
            here += 1
        else:
            send_ref[there] = total
            there += 1


def halve_small_kernel(pick, keep_ref, small_ref, got_ref, next_ref, total_ref, send_ref):
    halve_kernel(pick, keep_ref, got_ref, next_ref, send_ref)
    total = small_ref[...] + join_small(got_ref.at[got_ref.shape[0] - 1], small_ref.shape[1])
    total_ref[...] = total
    split_small(total, send_ref.at[send_ref.shape[0] - 1])


def part_kernel(keep_ref, got_ref, *outs):
    for b in range(keep_ref.shape[0]):
        outs[b][...] = added(keep_ref[b], got_ref[b])


def part_small_kernel(keep_ref, small_ref, got_ref, own_ref, total_ref, *outs):
    total = small_ref[...] + join_small(got_ref.at[got_ref.shape[0] - 1], small_ref.shape[1])
    total_ref[...] = total
    for b in range(keep_ref.shape[0]):
        value = added(keep_ref[b], got_ref[b])
        if b == 0:
            own_ref[...] = value
        else:
            outs[b - 1][0] = value
            if b == 1:
                split_small(total, outs[0].at[1])
            else:
                outs[b - 1][1] = outs[0][1]


def sum_kernel(count, *refs):
    total = refs[0][...].astype(F32)
    for r in refs[1:count]:
        total = total + r[...].astype(F32)
    refs[-1][...] = total.astype(refs[-1].dtype)


def pack_kernel(first_ref, own_ref, small_ref, *refs):
    gots, (packed_ref, total_ref) = refs[:-2], refs[-2:]
    total, value = small_ref[...], own_ref[...].astype(F32)
    for got in gots:
        value = value + got[0].astype(F32)
        total = total + join_small(got.at[1], total.shape[1])
    total_ref[...] = total
    rows, lanes = own_ref.shape
    edge = first_ref.shape[0]
    packed_ref[0:edge, :] = first_ref[...]
    ways = first_ref.shape[1] // lanes
    for c in range(ways):
        packed_ref[edge:, c * lanes : (c + 1) * lanes] = value[c * (rows // ways) : (c + 1) * (rows // ways)].astype(BF)


def add_one_kernel(a_ref, b_ref, small_ref, other_ref, out_ref, total_ref):
    out_ref[...] = added(a_ref[...], b_ref[...])
    total_ref[...] = small_ref[...] + other_ref[...]


def spread_kernel(count, ids_ref, small_ref, *refs):
    blocks = refs[:count]
    qkv_ref, qv_ref, out_ref, ob_ref, up_ref, ub_ref, down_ref, db_ref, alpha_ref, turned_ref, second_ref = refs[count:]
    me, tensor = ids_ref[0], ids_ref[1]
    lanes = out_ref.shape[0]
    for j, ref in enumerate(blocks):
        slot = lax.bitwise_xor(me % count, j)
        first = 0
        for out in (up_ref, turned_ref, out_ref):
            size = out.shape[0] // count
            out[pl.ds(pl.multiple_of(slot * size, 8), size), :] = ref[first : first + size, :].astype(F32)
            first += size
        size = qkv_ref.shape[1] // count
        rest = ref.shape[0] - first
        for c in range(ref.shape[1] // lanes):
            second_ref[c * rest : (c + 1) * rest, :] = ref[first:, c * lanes : (c + 1) * lanes].astype(F32)
        for c in range(3):
            qkv_ref[c, pl.ds(pl.multiple_of(slot * size, 8), size), :] = second_ref[c * size : (c + 1) * size, :]
    down_ref[...] = turned_ref[...].T
    ub_ref[...] = small_ref[pl.ds(tensor, 1), :]
    ob_ref[...] = small_ref[4:5, :]
    db_ref[...] = small_ref[5:6, :]
    qv_ref[...] = small_ref[8:10, pl.ds(pl.multiple_of(tensor * lanes, LANES), lanes)]
    sums = jnp.sum(small_ref[6:8, :], axis=1, keepdims=True)
    spread = jnp.concatenate([sums, jnp.zeros((6, 1), F32)], axis=0)
    alpha_ref[...] = jnp.broadcast_to(spread, (8, LANES))


def widen_kernel(first, ids_ref, a_any, b_any, *refs):
    out_any, sems, wide_ref, low_ref = refs[-4:]
    rows = low_ref.shape[1]
    copies = Copies(sems)
    ins = [copies.start(a, low_ref.at[n]) for n, a in enumerate((a_any, b_any))]
    half = rows // 2
    for n in range(2):
        ins[n].wait()
        slot = lax.bitwise_xor(ids_ref[1], first + n)
        for m in range(2):
            span = slice(m * half, (m + 1) * half)
            wide_ref[n, span, :] = low_ref[n, span, :].astype(F32)
            copies.send(wide_ref.at[n, span], out_any.at[slot, span])
    copies.finish()


def settle_kernel(r_ref, scol_ref, out_ref):
    out_ref[...] = dot(one_hot_cols(scol_ref[:, 0:1], r_ref.shape[0]), r_ref[...]).astype(BF)


def shape(dims, kind):
    return jax.ShapeDtypeStruct(dims, kind)


def call(kernel, ins, outs, scratch=(), deps=(), flops=1e6, nbytes=4 << 20, scalars=0, ins_any=0, outs_any=0, limit=24, aliases=None):
    n_in, n_dep = len(ins), len(deps)
    whole = pl.BlockSpec(memory_space=pl.ANY)

    def body(*refs):
        kernel(*refs[:n_in], *refs[n_in + n_dep :])

    return pl.pallas_call(
        body,
        out_shape=list(outs),
        in_specs=[smem()] * scalars + vmem(n_in - scalars - ins_any) + [whole] * (ins_any + n_dep),
        out_specs=vmem(len(outs) - outs_any) + [whole] * outs_any,
        scratch_shapes=list(scratch),
        input_output_aliases=aliases or {},
        compiler_params=params(limit << 20),
        cost_estimate=cost(SCALE * flops, SCALE * nbytes),
    )(*ins, *deps)


def per_device(
    block_input, cotangent, source, seq_lengths, qkv_weight, qv_bias, out_weight, out_bias,
    up_weight, up_bias, down_weight, down_bias, rezero_alphas,
):
    micros, rows, width = block_input.shape
    groups = lax.axis_size("dp")
    tensors = lax.axis_size("tensor")
    lanes = qkv_weight.shape[2]
    units = up_weight.shape[1]
    blocks = min(groups, 8)
    me, tensor = lax.axis_index("dp"), lax.axis_index("tensor")
    ids = jnp.stack([me, tensor]).astype(I32)
    lengths = lax.dynamic_index_in_dim(seq_lengths, tensor, 0, keepdims=False)[0]

    def across(axis, bit, value):
        count = tensors if axis == "tensor" else groups
        return lax.ppermute(value, axis, [(i, i ^ bit) for i in range(count)])

    def after(value, *others):
        return lax.optimization_barrier((value, *others))[0] if others else value

    def by_micro(kernel, n_whole, out_shape, scratch):
        return pl.pallas_call(
            kernel,
            out_shape=out_shape,
            grid_spec=pltpu.PrefetchScalarGridSpec(
                num_scalar_prefetch=1,
                grid=(1,),
                in_specs=[
                    pl.BlockSpec(source.shape, lambda i, s: (0, 0)),
                    pl.BlockSpec((1, rows, width), lambda i, s: (s[1], 0, 0)),
                ]
                + [pl.BlockSpec((rows // LANES, LANES), lambda i, s: (0, 0))] * n_whole,
                out_specs=[pl.BlockSpec(o.shape, lambda i, s: (0, 0)) for o in out_shape],
                scratch_shapes=scratch,
            ),
            compiler_params=params(),
            cost_estimate=cost(SCALE * 5e9, 4 << 20),
        )

    hot = pltpu.VMEM((rows, rows), BF)
    xs, srow, scol = by_micro(
        functools.partial(route_kernel, groups), 0,
        [shape((rows, width), BF), shape((rows // LANES, LANES), I32), shape((rows, LANES), I32)], [hot],
    )(ids, source, block_input)

    def exchange(rows_out):
        return lax.all_to_all(rows_out.reshape(groups, rows // groups, width), "dp", 0, 0, tiled=True).reshape(rows, width)

    arr_x = exchange(xs)
    gs, arow, acol = by_micro(
        second_kernel, 1,
        [shape((rows, width), BF), shape((8, rows), I32), shape((rows, LANES), I32)], [hot],
    )(ids, source, cotangent, srow)
    head = jnp.concatenate([qv_bias, up_bias.reshape(units // lanes, lanes), jnp.zeros((2, lanes), BF)], axis=0)
    own = (head, qkv_weight, out_weight, up_weight, down_weight)
    far = [across("tensor", 2, w) for w in own]
    held = lax.optimization_barrier((*far[:3], arow))[:3]

    def four(own, far):
        return own, across("tensor", 1, own), far, across("tensor", 1, far)

    bias4, wa4, wo4 = [four(w, f) for w, f in zip(own, held)]
    arr_g = exchange(gs)

    def v16(*dims):
        return pltpu.VMEM(dims, BF)

    def v32(*dims):
        return pltpu.VMEM(dims, F32)

    def sems(count):
        return pltpu.SemaphoreType.DMA((count,))

    ff = tensors * units
    wide = [shape((rows, width), BF)] * 4
    logs, x, q, k, v, o, h, low, attn = call(
        attend_kernel,
        (ids, lengths, rezero_alphas, *bias4, out_bias.reshape(1, width), acol, arr_x, *wa4, *wo4),
        [shape((2 * tensors, rows), F32), *wide, shape((rows, width), F32), shape((rows, width), F32),
         shape((rows, width), BF), shape((rows, width), F32)],
        [sems(40), v16(rows, width), v16(width, 3 * width), v16(width, width), v32(8, width), hot, v16(rows, width),
         v16(rows, width), v16(rows, width), v16(rows, width), v32(rows, width), v16(rows, width), v32(rows, width),
         v16(rows, width), v32(rows, width)],
        scalars=3, ins_any=9, outs_any=8, flops=16e9, nbytes=16 << 20, limit=60,
    )
    held = lax.optimization_barrier((*far[3:], logs))[:2]
    wu4, wd4 = [four(w, f) for w, f in zip(own[3:], held)]
    ys, act, slope, branch = call(
        forward_kernel,
        (rezero_alphas, *bias4, down_bias.reshape(1, width), arow, low, h, *wu4, *wd4),
        [shape((rows, width), BF), shape((rows, ff), BF), shape((rows, ff), BF), shape((rows, width), F32)],
        [sems(40), v16(rows, width), v32(rows, width), v16(width, ff), v16(ff, width), v16(rows, ff), v16(rows, ff),
         v32(rows, width), v16(rows, width), hot, v16(rows, width)],
        scalars=1, ins_any=10, outs_any=4, flops=14e9, nbytes=24 << 20, limit=60,
    )
    bundle = (width + units + lanes) // blocks
    part = shape((tensors // 2, blocks, bundle, width), BF)
    small1, dots, go, gh, keep1, send1 = call(
        feed_kernel,
        (ids, rezero_alphas, acol, arr_g, *wu4, *wd4, *wo4, act, slope, low, branch, attn, o),
        [shape((8, width), F32), shape((2 * tensors, rows), F32), shape((rows, width), BF), shape((rows, width), F32), part, part],
        [sems(48), v16(rows, width), v16(width, ff), v16(ff, width), v16(width, width), v16(rows, ff), v16(rows, ff),
         v16(rows, width), v32(rows, width), v32(rows, width), v32(rows, width),
         hot, v16(rows, width), v16(rows, width), v16(rows, ff), v32(rows, width), v16(rows, width), v16(rows, width),
         v16(tensors, blocks, bundle, width)],
        scalars=2, ins_any=19, outs_any=4, flops=20e9, nbytes=24 << 20, deps=(ys,), limit=60,
    )
    arr_y = exchange(ys)
    got = across("tensor", 1, send1)

    def back(first, last, deps):
        span = (last - first) * lanes
        return call(
            functools.partial(back_kernel, first), (lengths, logs, dots, q, k, v, go),
            [shape((3, rows, span), BF)],
            [sems(16), v16(rows, span), v16(rows, span), v16(rows, span), v16(rows, span), v16(3, rows, span), v32(rows, lanes)],
            scalars=1, ins_any=4, outs_any=1, limit=60, deps=deps, flops=11e9,
        )[0]

    half = tensors // 2
    bf_blocks = lambda n, like: shape((n, *like.shape[1:]), BF)
    bare = shape((16, width), F32)

    def settle(rows_back, deps):
        return call(settle_kernel, (rows_back, scol), [shape((rows, width), BF)], deps=deps, flops=2e9)[0]

    def widen(first, a, b, into=None, deps=()):
        extra = () if into is None else (into,)
        return call(
            functools.partial(widen_kernel, first), (ids, a, b, *extra), [shape((tensors, rows, width), F32)],
            [sems(8), v32(2, rows, width), v16(2, rows, width)],
            scalars=1, ins_any=2 + len(extra), outs_any=1, limit=60, deps=deps, flops=4e9, aliases={3: 0} if extra else None,
        )[0]

    keep1 = keep1.reshape(half * blocks, bundle, width)
    send1 = send1.reshape(half * blocks, bundle, width)
    got = across("tensor", 1, send1)
    n = half * blocks // 2
    keep1, send1 = call(functools.partial(halve_kernel, lambda b: b % 2 == 0), (keep1, got), [bf_blocks(n, keep1)] * 2, deps=())
    got_y = across("dp", 1, send1)
    grad_a = back(0, half, (keep1,))
    grad_b = back(half, tensors, (grad_a,))
    y_own = settle(arr_y, (grad_b,))
    y_far = across("tensor", 2, y_own)
    y_core = across("tensor", 1, y_own)
    n = n // 2
    keep1, send1 = call(functools.partial(halve_kernel, lambda b: b < blocks // 2), (keep1, got_y), [bf_blocks(n, keep1)] * 2, deps=(y_own,))
    got_x = across("tensor", 2, send1)
    deps_last = (keep1,)
    share = (3 * width) // blocks
    small, gxs, keep2, send2 = call(
        last_kernel, (ids, small1, arow, grad_a, grad_b, gh, x, *wa4),
        [bare, shape((rows, width), BF), shape((half * blocks, share, lanes), BF), shape((half * blocks + 1, share, lanes), BF)],
        [sems(40), v16(rows, 3 * width), v32(rows, width), v16(rows, width), v16(width, 3 * width), hot, v16(rows, width),
         v16(rows, width), v16(tensors, blocks, share, lanes), v16(width, 3 * width), v16(3 * 16 * width // LANES, LANES)],
        scalars=1, ins_any=8, outs_any=3, flops=9e9, nbytes=8 << 20, deps=deps_last, limit=60,
    )
    arr_gx = exchange(gxs)
    got = across("tensor", 1, send2)
    n2 = half * blocks // 2
    keep2, small, send2 = call(
        functools.partial(halve_small_kernel, lambda b: b % 2 == 0), (keep2, small, got),
        [bf_blocks(n2, keep2), bare, bf_blocks(n2 + 1, keep2)],
    )
    got = across("dp", 1, send2)
    parts1 = call(part_kernel, (keep1, got_x), [shape(keep1.shape[1:], BF)] * (blocks // 2), deps=(keep2,))
    got1 = [across("dp", 2 * j, v) for j, v in enumerate(parts1) if j]
    output = widen(0, y_own, y_core, deps=(parts1[0],))
    n2 = n2 // 2
    keep2, small, send2 = call(
        functools.partial(halve_small_kernel, lambda b: b < blocks // 2), (keep2, small, got),
        [bf_blocks(n2, keep2), bare, bf_blocks(n2 + 1, keep2)], deps=(output,),
    )
    got = across("tensor", 2, send2)
    y_both = across("tensor", 1, y_far)
    gx_own = settle(arr_gx, (keep2,))
    gx_far = across("tensor", 2, gx_own)
    gx_core = across("tensor", 1, gx_own)
    own1 = call(functools.partial(sum_kernel, 1 + len(got1)), (parts1[0], *got1), [shape(keep1.shape[1:], BF)], deps=(gx_own,))[0]
    own2, small, *parts2 = call(
        part_small_kernel, (keep2, small, got),
        [shape(keep2.shape[1:], BF), bare] + [bf_blocks(2, keep2)] * (blocks // 2 - 1), deps=(own1,),
    )
    got2 = [across("dp", 2 * (j + 1), v) for j, v in enumerate(parts2)]
    output = widen(2, y_far, y_both, output, deps=(own2,))
    own, small = call(pack_kernel, (own1, own2, small, *got2), [shape((bundle + share // 4, width), BF), bare], deps=(output,))
    bit = blocks
    while bit < groups:
        own, small = call(
            add_one_kernel, (own, across("dp", bit, own), small, across("dp", bit, small)), [shape(own.shape, BF), bare]
        )
        bit *= 2
    even = [own] + [across("dp", 2 * j, own) for j in range(1, blocks // 2)]
    odd = [across("dp", 1, e) for e in even]
    gx_grad = widen(0, gx_own, gx_core, deps=(own,))
    gx_both = across("tensor", 1, gx_far)
    gathered = [b for pair in zip(even, odd) for b in pair]
    qkv_grad, qv_grad, out_grad, ob_grad, up_grad, ub_grad, down_grad, db_grad, alphas = call(
        functools.partial(spread_kernel, blocks), (ids, small, *gathered),
        [shape((3, width, lanes), F32), shape((2, lanes), F32), shape((lanes, width), F32), shape((1, width), F32),
         shape((width, units), F32), shape((1, units), F32), shape((units, width), F32), shape((1, width), F32), shape((8, LANES), F32)],
        [v32(width, units), v32(share, lanes)], scalars=1, deps=(gx_grad,),
    )
    input_grad = widen(2, gx_far, gx_both, gx_grad, deps=())
    return (
        output, input_grad, qkv_grad, qv_grad, out_grad, ob_grad[0], up_grad, ub_grad[0], down_grad, db_grad[0], alphas[0:2, 0],
    )


def solution(mesh):
    in_specs = (
        P(None, "dp", None), P(None, "dp", None), P(), P(None, "dp", None),
        P(None, None, "tensor"), P(None, "tensor"), P("tensor", None), P(),
        P(None, "tensor"), P("tensor"), P("tensor", None), P(), P(),
    )
    out_specs = (
        P(None, "dp", None), P(None, "dp", None), P(None, None, "tensor"), P(None, "tensor"),
        P("tensor", None), P(), P(None, "tensor"), P("tensor"), P("tensor", None), P(), P(),
    )
    return jax.shard_map(per_device, mesh=mesh, in_specs=in_specs, out_specs=out_specs, check_vma=False)
```

```python
import functools

import jax
import jax.numpy as jnp
from jax import lax
from jax.experimental import pallas as pl
from jax.experimental.pallas import tpu as pltpu
from jax.sharding import PartitionSpec as P

HEAD_SIZE = 64
LANES = 128
QT = 256
FT = 512
BF = jnp.bfloat16
F32 = jnp.float32
C = {"route": 6, "attend": 19, "forward": 5, "feed": 19, "back": 11, "halve": 1, "part": 5, "settle": 1, "last": 20, "weight": 0.2, "widen": 5, "spread": 3}
I32 = jnp.int32
NEG = -1e30
VMEM_LIMIT = 56 * 1024 * 1024
GELU_A = 0.7978845608028654
GELU_B = 0.044715

NN = (((1,), (0,)), ((), ()))
NT = (((1,), (1,)), ((), ()))
TN = (((0,), (0,)), ((), ()))


def dot(a, b, dims=NN):
    return lax.dot_general(a, b, dims, preferred_element_type=F32)


def iota(shape, dim):
    return lax.broadcasted_iota(I32, shape, dim)


def params(limit=VMEM_LIMIT):
    return pltpu.CompilerParams(vmem_limit_bytes=limit)


def cost(flops, nbytes, trans=0):
    return pl.CostEstimate(flops=int(flops), bytes_accessed=int(nbytes), transcendentals=int(trans))


def vmem(n):
    return [pl.BlockSpec(memory_space=pltpu.VMEM)] * n


def smem():
    return pl.BlockSpec(memory_space=pltpu.SMEM)


def one_hot_rows(row, count):
    return (iota((count, row.shape[1]), 0) == row).astype(F32).astype(BF)


def one_hot_cols(col, count):
    return (iota((col.shape[0], count), 1) == col).astype(F32).astype(BF)


def route_kernel(groups, ids_ref, src_ref, x_ref, xs_ref, srow_ref, scol_ref, hot_ref):
    me, micro = ids_ref[0], ids_ref[1]
    rows = x_ref.shape[1]
    chunks = rows // LANES
    share = rows // groups
    sub_hi = iota((chunks, rows), 0)
    sub_lo = iota((LANES, rows), 0)

    def gather_group(g, total):
        value = src_ref[pl.ds(micro, 1), pl.ds(pl.multiple_of(g * rows, LANES), rows)] - me * rows
        inside = (value >= 0) & (value < rows)
        high = jnp.where(inside, value // LANES, -1)
        low = jnp.where(inside, value % LANES, -1)
        hot_high = jnp.where(high == sub_hi, (g + 1).astype(F32), 0.0).astype(BF)
        hot_low = (low == sub_lo).astype(F32).astype(BF)
        return total + dot(hot_high, hot_low, NT)

    dest = lax.fori_loop(0, groups, gather_group, jnp.zeros((chunks, LANES), F32)).astype(I32) - 1
    before = (iota((LANES, LANES), 0) < iota((LANES, LANES), 1)).astype(F32).astype(BF)
    width = max(groups, 8)
    carry = jnp.zeros((width, 1), F32)
    for c in range(chunks):
        g_row = dest[c : c + 1, :]
        hot = (iota((width, LANES), 0) == g_row).astype(F32)
        ranks = dot(hot.astype(BF), before) + carry
        carry = carry + jnp.sum(hot, axis=1, keepdims=True)
        place = g_row * share + jnp.sum(hot * ranks, axis=0, keepdims=True).astype(I32)
        srow_ref[c : c + 1, :] = place
        spread = jnp.broadcast_to(place.astype(F32), (LANES, LANES))
        scol_ref[c * LANES : (c + 1) * LANES, :] = spread.T.astype(I32)
        hot_ref[:, c * LANES : (c + 1) * LANES] = one_hot_rows(place, rows)
    xs_ref[...] = dot(hot_ref[...], x_ref[0]).astype(BF)


def second_kernel(ids_ref, src_ref, g_ref, srow_ref, gs_ref, arow_ref, acol_ref, hot_ref):
    me, micro = ids_ref[0], ids_ref[1]
    rows = g_ref.shape[1]
    for c in range(rows // LANES):
        hot_ref[:, c * LANES : (c + 1) * LANES] = one_hot_rows(srow_ref[c : c + 1, :], rows)
    gs_ref[...] = dot(hot_ref[...], g_ref[0]).astype(BF)
    own = src_ref[pl.ds(micro, 1), pl.ds(pl.multiple_of(me * rows, LANES), rows)].astype(F32)
    for c in range(rows // LANES):
        piece = own[:, c * LANES : (c + 1) * LANES]
        column = jnp.broadcast_to(piece, (LANES, LANES)).T[:, 0:1]
        count = jnp.sum((own < column).astype(F32), axis=1, keepdims=True)
        spread = jnp.broadcast_to(count, (LANES, LANES))
        acol_ref[c * LANES : (c + 1) * LANES, :] = spread.astype(I32)
        arow_ref[0:1, c * LANES : (c + 1) * LANES] = spread.T[0:1, :].astype(I32)


def starts_of(len_ref, index):
    start = jnp.zeros_like(index)
    first = jnp.int32(0)
    for j in range(len_ref.shape[0] - 1):
        first = first + len_ref[j]
        start = jnp.where(index >= first, first, start)
    return start


class Copies:
    def __init__(self, sems):
        self.sems, self.used, self.left = sems, 0, []

    def start(self, source, target):
        copy = pltpu.make_async_copy(source, target, self.sems.at[self.used])
        self.used += 1
        copy.start()
        return copy

    def send(self, source, target):
        self.left.append(self.start(source, target))

    def finish(self):
        for copy in self.left:
            copy.wait()


def wait_all(copies):
    for copy in copies:
        copy.wait()


def attend_kernel(
    ids_ref, len_ref, alpha_ref, b0_ref, b1_ref, b2_ref, b3_ref, ob_ref, acol_ref,
    arr_any, wa0_any, wa1_any, wa2_any, wa3_any, wo0_any, wo1_any, wo2_any, wo3_any,
    l_ref, x_any, q_any, k_any, v_any, o_any, h_any, low_any, attn_any,
    sems, arr_ref, wcat_ref, wo_ref, bias_ref, hot_ref, x_ref, q_ref, k_ref, v_ref, ob16_ref, h_ref, low_ref, attn_ref,
):
    rows, width = arr_ref.shape
    lanes = wo0_any.shape[0]
    pieces = width // lanes
    heads = lanes // HEAD_SIZE
    tensor = ids_ref[1]
    copies = Copies(sems)
    first = copies.start(arr_any, arr_ref)
    weights, later = [], []
    for j, (wa, wo, b) in enumerate(
        ((wa0_any, wo0_any, b0_ref), (wa1_any, wo1_any, b1_ref), (wa2_any, wo2_any, b2_ref), (wa3_any, wo3_any, b3_ref))
    ):
        place = pl.multiple_of(lax.bitwise_xor(tensor, j) * lanes, LANES)
        for c in range(3):
            weights.append(copies.start(wa.at[c], wcat_ref.at[:, pl.ds(c * width + place, lanes)]))
        later.append(copies.start(wo, wo_ref.at[pl.ds(place, lanes), :]))
        bias_ref[:, pl.ds(place, lanes)] = b[...].astype(F32)
    hot_ref[...] = one_hot_cols(acol_ref[:, 0:1], rows)
    first.wait()
    x_ref[...] = dot(hot_ref[...], arr_ref[...]).astype(BF)
    copies.send(x_ref, x_any)
    wait_all(weights)
    q_ref[...] = (dot(x_ref[...], wcat_ref[:, 0:width]) + bias_ref[0:1, :]).astype(BF) * jnp.asarray(HEAD_SIZE**-0.5, BF)
    k_ref[...] = dot(x_ref[...], wcat_ref[:, width : 2 * width]).astype(BF)
    v_ref[...] = (dot(x_ref[...], wcat_ref[:, 2 * width :]) + bias_ref[1:2, :]).astype(BF)
    copies.send(q_ref, q_any)
    copies.send(k_ref, k_any)
    copies.send(v_ref, v_any)
    tiles = rows // QT
    lane = iota((QT, lanes), 1) // HEAD_SIZE
    masks = []
    for i in range(tiles):
        q_index = i * QT + iota((QT, 1), 0)
        k_index = iota((QT, (i + 1) * QT), 1)
        masks.append((k_index >= starts_of(len_ref, q_index)) & (k_index <= q_index))

    def scores_of(p, i, e):
        q = q_ref[i * QT : (i + 1) * QT, p * lanes : (p + 1) * lanes]
        return dot(jnp.where(lane == e, q, jnp.zeros_like(q)), k_ref[0 : (i + 1) * QT, p * lanes : (p + 1) * lanes], NT)

    items = [(p, i, e) for i in range(tiles) for p in range(pieces) for e in range(heads)]
    ahead = scores_of(*items[0])
    mixed = logs = None
    for step, (p, i, e) in enumerate(items):
        now = ahead
        if step + 1 < len(items):
            ahead = scores_of(*items[step + 1])
        scores = jnp.where(masks[i], now, NEG)
        top = jnp.max(scores, axis=1, keepdims=True)
        weights = jnp.exp(scores - top)
        total = jnp.sum(weights, axis=1, keepdims=True)
        low = (weights * (1.0 / total)).astype(BF)
        out = dot(low, v_ref[0 : (i + 1) * QT, p * lanes : (p + 1) * lanes])
        head = p * heads + e
        log_total = top + jnp.log(total)
        logs = jnp.where(iota((QT, LANES), 1) == head, log_total, 0.0 if head == 0 else logs)
        mixed = out if e == 0 else jnp.where(lane == e, out, mixed)
        if e == heads - 1:
            ob16_ref[i * QT : (i + 1) * QT, p * lanes : (p + 1) * lanes] = mixed.astype(BF)
        if head == pieces * heads - 1:
            l_ref[:, i * QT : (i + 1) * QT] = logs.T[0 : pieces * heads, :]
            if i == 0:
                wait_all(later)
            span = slice(i * QT, (i + 1) * QT)
            copies.send(ob16_ref.at[span], o_any.at[span])
            attn = dot(ob16_ref[span, :], wo_ref[...]) + ob_ref[...].astype(F32)
            hidden = x_ref[span, :].astype(F32) + alpha_ref[0] * attn
            attn_ref[span, :] = attn
            h_ref[span, :] = hidden
            low_ref[span, :] = hidden.astype(BF)
            copies.send(attn_ref.at[span], attn_any.at[span])
            copies.send(h_ref.at[span], h_any.at[span])
            copies.send(low_ref.at[span], low_any.at[span])
    copies.finish()


def forward_kernel(
    alpha_ref, b0_ref, b1_ref, b2_ref, b3_ref, db_ref, arow_ref,
    low_any, h_any, wu0_any, wu1_any, wu2_any, wu3_any, wd0_any, wd1_any, wd2_any, wd3_any,
    ys_any, act_any, slope_any, f_any,
    sems, low_ref, h_ref, wu_ref, wd_ref, act_ref, slope_ref, f_ref, y_ref, hot_ref, ys_ref,
):
    rows, width = low_ref.shape
    units = wu0_any.shape[1]
    copies = Copies(sems)
    first = copies.start(low_any, low_ref)
    up, down = [], []
    for j, wu in enumerate((wu0_any, wu1_any, wu2_any, wu3_any)):
        up.append(copies.start(wu, wu_ref.at[:, j * units : (j + 1) * units]))
    for j, wd in enumerate((wd0_any, wd1_any, wd2_any, wd3_any)):
        down.append(copies.start(wd, wd_ref.at[j * units : (j + 1) * units, :]))
    hidden = copies.start(h_any, h_ref)
    biases = []
    for b in (b0_ref, b1_ref, b2_ref, b3_ref):
        tail = b[...].astype(F32)
        biases.append(jnp.concatenate([tail[2 + n : 3 + n, :] for n in range(units // LANES)], axis=1))
    first.wait()
    items = [(j, m) for j in range(len(biases)) for m in range(rows // FT)]

    def z_of(j, m):
        if m == 0:
            up[j].wait()
        return dot(low_ref[m * FT : (m + 1) * FT, :], wu_ref[:, j * units : (j + 1) * units])

    ahead = z_of(*items[0])
    for step, (j, m) in enumerate(items):
        z = ahead + biases[j]
        if step + 1 < len(items):
            ahead = z_of(*items[step + 1])
        square = z * z
        tanh = jnp.tanh(z * (GELU_A + (GELU_A * GELU_B) * square))
        half = 0.5 * z
        rise = 0.5 + 0.5 * tanh
        span = (slice(m * FT, (m + 1) * FT), slice(j * units, (j + 1) * units))
        act_ref[span] = (z * rise).astype(BF)
        slope_ref[span] = rise + half * (1.0 - tanh * tanh) * (GELU_A + (3 * GELU_A * GELU_B) * square)
        if m == rows // FT - 1:
            copies.send(act_ref.at[:, span[1]], act_any.at[:, span[1]])
            copies.send(slope_ref.at[:, span[1]], slope_any.at[:, span[1]])
    wait_all(down)
    hidden.wait()
    for m in range(rows // FT):
        span = slice(m * FT, (m + 1) * FT)
        branch = dot(act_ref[span, :], wd_ref[...]) + db_ref[...].astype(F32)
        f_ref[span, :] = branch
        copies.send(f_ref.at[span], f_any.at[span])
        y_ref[span, :] = (h_ref[span, :] + alpha_ref[1] * branch).astype(BF)
        hot_ref[span, :] = (iota((FT, rows), 0) + m * FT == arow_ref[0:1, :]).astype(F32).astype(BF)
    for m in range(rows // FT):
        span = slice(m * FT, (m + 1) * FT)
        ys_ref[span, :] = dot(hot_ref[span, :], y_ref[...]).astype(BF)
        copies.send(ys_ref.at[span], ys_any.at[span])
    copies.finish()


def feed_kernel(
    ids_ref, alpha_ref, acol_ref,
    arr_any, wu0_any, wu1_any, wu2_any, wu3_any, wd0_any, wd1_any, wd2_any, wd3_any,
    wo0_any, wo1_any, wo2_any, wo3_any, act_any, slope_any, low_any, f_any, attn_any, o_any,
    small_ref, go_any, gh_any, keep_any, send_any,
    sems, arr_ref, wu_ref, wd_ref, wo_ref, act_ref, slope_ref, low_ref, f_ref, attn_ref, o_ref,
    hot_ref, g_ref, gf_ref, gz_ref, gh_ref, ga_ref, go_ref, keep_ref, part_ref, w_ref,
):
    me, tensor = ids_ref[0], ids_ref[1]
    rows, width = low_ref.shape
    units = wu0_any.shape[1]
    lanes = wo0_any.shape[0]
    blocks = part_ref.shape[1]
    own = me % blocks
    copies = Copies(sems)
    first = copies.start(arr_any, arr_ref)
    down, slopes, up, later = [], [], [], []
    for j, wd in enumerate((wd0_any, wd1_any, wd2_any, wd3_any)):
        span = slice(j * units, (j + 1) * units)
        down.append(copies.start(wd, wd_ref.at[span, :]))
        slopes.append(copies.start(slope_any.at[:, span], slope_ref.at[:, span]))
    for j, wu in enumerate((wu0_any, wu1_any, wu2_any, wu3_any)):
        up.append(copies.start(wu, wu_ref.at[:, j * units : (j + 1) * units]))
    lowed = copies.start(low_any, low_ref)
    acted = copies.start(act_any, act_ref)
    for j, wo in enumerate((wo0_any, wo1_any, wo2_any, wo3_any)):
        place = pl.multiple_of(lax.bitwise_xor(tensor, j) * lanes, LANES)
        later.append(copies.start(wo, wo_ref.at[pl.ds(place, lanes), :]))
    later.append(copies.start(attn_any, attn_ref))
    later.append(copies.start(o_any, o_ref))
    branched = copies.start(f_any, f_ref)
    hot_ref[...] = one_hot_cols(acol_ref[:, 0:1], rows)
    first.wait()
    for m in range(rows // FT):
        span = slice(m * FT, (m + 1) * FT)
        grad = dot(hot_ref[span, :], arr_ref[...])
        g_ref[span, :] = grad.astype(BF)
        gf_ref[span, :] = (alpha_ref[1] * grad).astype(BF)
    items = [(j, m) for j in range(len(up)) for m in range(rows // FT)]

    def ga_of(j, m):
        if m == 0:
            down[j].wait()
        return dot(gf_ref[m * FT : (m + 1) * FT, :], wd_ref[j * units : (j + 1) * units, :], NT)

    ahead = ga_of(*items[0])
    for step, (j, m) in enumerate(items):
        now = ahead
        if step + 1 < len(items):
            ahead = ga_of(*items[step + 1])
        if m == 0:
            slopes[j].wait()
        span = (slice(m * FT, (m + 1) * FT), slice(j * units, (j + 1) * units))
        gz_ref[span] = (now * slope_ref[span]).astype(BF)
    wait_all(up)
    wait_all(later)
    gh_sum = attn_sum = jnp.zeros((1, width), F32)
    for m in range(rows // FT):
        span = slice(m * FT, (m + 1) * FT)
        grad_hidden = g_ref[span, :].astype(F32) + dot(gz_ref[span, :], wu_ref[...], NT)
        gh_ref[span, :] = grad_hidden
        copies.send(gh_ref.at[span], gh_any.at[span])
        ga = (alpha_ref[0] * grad_hidden).astype(BF)
        ga_ref[span, :] = ga
        gh_sum = gh_sum + jnp.sum(ga.astype(F32), axis=0, keepdims=True)
        attn_sum = attn_sum + jnp.sum(grad_hidden * attn_ref[span, :], axis=0, keepdims=True)
    for m in range(rows // FT):
        span = slice(m * FT, (m + 1) * FT)
        go = dot(ga_ref[span, :], wo_ref[...], NT).astype(BF)
        go_ref[span, :] = go
        copies.send(go_ref.at[span], go_any.at[span])

    def place(j, first_row, value):
        count = value.shape[0] // blocks
        out = keep_ref if j % 2 == 0 else part_ref
        for b in range(blocks):
            out[j // 2, lax.bitwise_xor(own, b), first_row : first_row + count, :] = value[b * count : (b + 1) * count].astype(out.dtype)

    lowed.wait()
    acted.wait()
    low_t = low_ref[...].T
    gf_t = gf_ref[...].T
    o_t = o_ref[...].T
    w_ref[...] = dot(o_t, ga_ref[...])
    edge = (width + units) // blocks
    for j in range(len(up)):
        span = slice(j * units, (j + 1) * units)
        place(j, 0, dot(low_t, gz_ref[:, span]))
        place(j, width // blocks, dot(gf_t, act_ref[:, span]))
        at = pl.multiple_of(lax.bitwise_xor(tensor, j) * lanes, LANES)
        place(j, edge, w_ref[pl.ds(at, lanes), :])
        held, out = (keep_ref, keep_any) if j % 2 == 0 else (part_ref, send_any)
        copies.send(held.at[j // 2], out.at[j // 2])
        small_ref[pl.ds(lax.bitwise_xor(tensor, j), 1), :] = jnp.sum(gz_ref[:, span].astype(F32), axis=0, keepdims=True)
    branched.wait()
    small_ref[4:5, :] = gh_sum
    small_ref[5:6, :] = jnp.sum(gf_ref[...].astype(F32), axis=0, keepdims=True)
    small_ref[6:7, :] = attn_sum
    small_ref[7:8, :] = jnp.sum(g_ref[...].astype(F32) * f_ref[...], axis=0, keepdims=True)
    copies.finish()


def starts_of(len_ref, index):
    start = jnp.zeros_like(index)
    first = jnp.int32(0)
    for j in range(len_ref.shape[0] - 1):
        first = first + len_ref[j]
        start = jnp.where(index >= first, first, start)
    return start


def back_kernel(
    first_pair, len_ref, l_ref, q_any, k_any, v_any, go_any,
    grad_any,
    sems, q_ref, k_ref, v_ref, go_ref, grad_ref, gk_ref, gv_ref,
):
    rows, width = q_ref.shape
    lanes = 2 * HEAD_SIZE
    heads = 2
    pairs = width // lanes
    scale = HEAD_SIZE**-0.5
    copies = Copies(sems)
    columns = slice(first_pair * lanes, first_pair * lanes + width)
    ins = [copies.start(a.at[:, columns], r) for a, r in ((q_any, q_ref), (k_any, k_ref), (v_any, v_ref), (go_any, go_ref))]
    tiles = rows // QT
    lane = iota((QT, lanes), 1) // HEAD_SIZE
    masks = []
    for i in range(tiles):
        q_index = i * QT + iota((1, QT), 1)
        k_index = iota(((i + 1) * QT, QT), 0)
        masks.append((k_index >= starts_of(len_ref, q_index)) & (k_index <= q_index))
    wait_all(ins)
    items = [(p, i, e) for p in range(pairs) for i in reversed(range(tiles)) for e in range(heads)]

    def pick(ref, p, i, e):
        value = ref[i * QT : (i + 1) * QT, p * lanes : (p + 1) * lanes]
        return jnp.where(lane == e, value, jnp.zeros_like(value))

    def both_of(p, i, e):
        pair = (slice(0, (i + 1) * QT), slice(p * lanes, (p + 1) * lanes))
        return dot(k_ref[pair], pick(q_ref, p, i, e), NT), dot(v_ref[pair], pick(go_ref, p, i, e), NT)

    ahead = both_of(*items[0])
    gq = None
    for step, (p, i, e) in enumerate(items):
        scores, grad_weights = ahead
        if step + 1 < len(items):
            ahead = both_of(*items[step + 1])
        head = (first_pair + p) * heads + e
        n = (i + 1) * QT
        weights = jnp.exp(jnp.where(masks[i], scores - l_ref[head : head + 1, i * QT : n], NEG))
        inner = jnp.sum(weights * grad_weights, axis=0, keepdims=True)
        grad_scores = (weights * (grad_weights - inner)).astype(BF)
        gv = dot(weights.astype(BF), pick(go_ref, p, i, e))
        gk = dot(grad_scores, pick(q_ref, p, i, e))
        if i == tiles - 1 and e == 0:
            gv_ref[...] = gv
            gk_ref[...] = gk
        else:
            gv_ref[0:n, :] += gv
            gk_ref[0:n, :] += gk
        gq_e = dot(grad_scores, k_ref[0:n, p * lanes : (p + 1) * lanes], TN)
        gq = gq_e if e == 0 else jnp.where(lane == e, gq_e, gq)
        if e == heads - 1:
            span = (slice(i * QT, n), slice(p * lanes, (p + 1) * lanes))
            grad_ref[(0, *span)] = (gq * scale).astype(BF)
            grad_ref[(1, *span)] = gk_ref[i * QT : n, :].astype(BF)
            grad_ref[(2, *span)] = gv_ref[i * QT : n, :].astype(BF)
            if i == 0:
                copies.send(grad_ref.at[:, :, p * lanes : (p + 1) * lanes], grad_any.at[:, :, p * lanes : (p + 1) * lanes])
    copies.finish()


def split_small(value, out_ref):
    chunks = value.shape[1] // LANES
    for c in range(chunks):
        left = value[:, c * LANES : (c + 1) * LANES]
        for k in range(2):
            term = left.astype(BF)
            first = (k * chunks + c) * 16
            out_ref[first : first + 16, :] = term
            left = left - term.astype(F32)


def join_small(ref, width):
    chunks = width // LANES
    parts = []
    for c in range(chunks):
        terms = [ref[(k * chunks + c) * 16 : (k * chunks + c + 1) * 16, :].astype(F32) for k in range(2)]
        parts.append(terms[0] + terms[1])
    return jnp.concatenate(parts, axis=1)


def last_kernel(
    ids_ref, arow_ref, grad_a_any, grad_b_any, gh_any, wa0_any, wa1_any, wa2_any, wa3_any,
    gxs_any,
    sems, grad_ref, gh_ref, wcat_ref, hot_ref, gx_ref, gxs_ref,
):
    tensor = ids_ref[1]
    rows, width = gx_ref.shape
    lanes = wa0_any.shape[2]
    half = width // 2
    copies = Copies(sems)
    grads, weights = [], []
    for c in range(3):
        for n, g in enumerate((grad_a_any, grad_b_any)):
            grads.append(copies.start(g.at[c], grad_ref.at[:, c * width + n * half : c * width + (n + 1) * half]))
    for j, wa in enumerate((wa0_any, wa1_any, wa2_any, wa3_any)):
        place = pl.multiple_of(lax.bitwise_xor(tensor, j) * lanes, LANES)
        for c in range(3):
            weights.append(copies.start(wa.at[c], wcat_ref.at[:, pl.ds(c * width + place, lanes)]))
    hidden = copies.start(gh_any, gh_ref)
    for m in range(rows // FT):
        hot_ref[m * FT : (m + 1) * FT, :] = (iota((FT, rows), 0) + m * FT == arow_ref[0:1, :]).astype(F32).astype(BF)
    wait_all(grads)
    wait_all(weights)
    hidden.wait()
    for m in range(rows // FT):
        span = slice(m * FT, (m + 1) * FT)
        gx_ref[span, :] = (gh_ref[span, :] + dot(grad_ref[span, :], wcat_ref[...], NT)).astype(BF)
    for m in range(rows // FT):
        span = slice(m * FT, (m + 1) * FT)
        gxs_ref[span, :] = dot(hot_ref[span, :], gx_ref[...]).astype(BF)
        copies.send(gxs_ref.at[span], gxs_any.at[span])
    copies.finish()


def weight_kernel(
    ids_ref, small1_ref, grad_a_any, grad_b_any, x_any,
    small_ref, keep_any, send_any,
    sems, grad_ref, x_ref, keep_ref, part_ref, w_ref, split_ref,
):
    tensor = ids_ref[1]
    rows, width = x_ref.shape
    lanes = keep_ref.shape[2]
    half = width // 2
    blocks = keep_ref.shape[0] // 2
    copies = Copies(sems)
    xs = copies.start(x_any, x_ref)
    grads = [
        [
            copies.start(g.at[c], grad_ref.at[:, c * width + n * half : c * width + (n + 1) * half])
            for n, g in enumerate((grad_a_any, grad_b_any))
        ]
        for c in range(3)
    ]
    xs.wait()
    x_t = x_ref[...].T
    count = width // blocks
    small_ref[0:8, :] = small1_ref[...]
    small_ref[8:16, :] = jnp.zeros((8, width), F32)
    for c in range(3):
        wait_all(grads[c])
        span = slice(c * width, (c + 1) * width)
        w_ref[:, span] = dot(x_t, grad_ref[:, span])
        if c != 1:
            row = 8 + c // 2
            small_ref[row : row + 1, :] = jnp.sum(grad_ref[:, span].astype(F32), axis=0, keepdims=True)
    for j in range(width // lanes):
        at = pl.multiple_of(lax.bitwise_xor(tensor, j) * lanes, LANES)
        held, out = (keep_ref, keep_any) if j % 2 == 0 else (part_ref, send_any)
        first = j // 2 * blocks
        for c in range(3):
            for b in range(blocks):
                held[first + b, c * count : (c + 1) * count, :] = w_ref[
                    b * count : (b + 1) * count, pl.ds(c * width + at, lanes)
                ].astype(held.dtype)
        copies.send(held.at[pl.ds(first, blocks)], out.at[pl.ds(first, blocks)])
    split_small(small_ref[...], split_ref)
    copies.send(split_ref, send_any.at[send_any.shape[0] - 1, 0 : split_ref.shape[0]])
    copies.finish()


def halve_kernel(pick, keep_ref, got_ref, next_ref, send_ref):
    here = there = 0
    for b in range(keep_ref.shape[0]):
        total = keep_ref[b] + got_ref[b].astype(F32)
        if pick(b):
            next_ref[here] = total
            here += 1
        else:
            send_ref[there] = total.astype(BF)
            there += 1


def halve_small_kernel(pick, keep_ref, small_ref, got_ref, next_ref, total_ref, send_ref):
    halve_kernel(pick, keep_ref, got_ref, next_ref, send_ref)
    total = small_ref[...] + join_small(got_ref.at[got_ref.shape[0] - 1], small_ref.shape[1])
    total_ref[...] = total
    split_small(total, send_ref.at[send_ref.shape[0] - 1])


def part_kernel(keep_ref, got_ref, *outs):
    for b in range(keep_ref.shape[0]):
        outs[b][...] = (keep_ref[b] + got_ref[b].astype(F32)).astype(outs[b].dtype)


def whole_small_kernel(keep_ref, small_ref, got_ref, send_ref, total_ref):
    rows = keep_ref.shape[1]
    total = small_ref[...] + join_small(got_ref.at[got_ref.shape[0] - 1], small_ref.shape[1])
    total_ref[...] = total
    for b in range(keep_ref.shape[0]):
        send_ref[b, 0:rows, :] = (keep_ref[b] + got_ref[b].astype(F32)).astype(BF)
        if b == 0:
            split_small(total, send_ref.at[0, rows:])
        else:
            send_ref[b, rows:, :] = send_ref[0, rows:, :]


def sum_kernel(own_ref, a_ref, b_ref, c_ref, out_ref):
    out_ref[...] = own_ref[...] + a_ref[...].astype(F32) + b_ref[...].astype(F32) + c_ref[...].astype(F32)


def pack_kernel(own1_ref, got_ref, packed_ref, total_ref):
    first = own1_ref[...]
    ways = own1_ref.shape[1] // got_ref.shape[2]
    rows, lanes = got_ref.shape[1] - 2 * 16 * ways, got_ref.shape[2]
    value = total = 0.0
    for b in range(got_ref.shape[0]):
        value = value + got_ref[b, 0:rows, :].astype(F32)
        total = total + join_small(got_ref.at[b, rows:], total_ref.shape[1])
    total_ref[...] = total
    edge = own1_ref.shape[0]
    packed_ref[0:edge, :] = first.astype(packed_ref.dtype)
    for c in range(ways):
        packed_ref[edge:, c * lanes : (c + 1) * lanes] = value[c * (rows // ways) : (c + 1) * (rows // ways)].astype(packed_ref.dtype)


def add_one_kernel(a_ref, b_ref, small_ref, other_ref, out_ref, total_ref):
    out_ref[...] = (a_ref[...].astype(F32) + b_ref[...].astype(F32)).astype(out_ref.dtype)
    total_ref[...] = small_ref[...] + other_ref[...]


def spread_kernel(count, ids_ref, small_ref, *refs):
    blocks = refs[:count]
    qkv_ref, qv_ref, out_ref, ob_ref, up_ref, ub_ref, down_ref, db_ref, alpha_ref, turned_ref, second_ref = refs[count:]
    me, tensor = ids_ref[0], ids_ref[1]
    lanes = out_ref.shape[0]
    for j, ref in enumerate(blocks):
        slot = lax.bitwise_xor(me % count, j)
        first = 0
        for out in (up_ref, turned_ref, out_ref):
            size = out.shape[0] // count
            out[pl.ds(pl.multiple_of(slot * size, 8), size), :] = ref[first : first + size, :].astype(F32)
            first += size
        size = qkv_ref.shape[1] // count
        rest = ref.shape[0] - first
        for c in range(ref.shape[1] // lanes):
            second_ref[c * rest : (c + 1) * rest, :] = ref[first:, c * lanes : (c + 1) * lanes].astype(F32)
        for c in range(3):
            qkv_ref[c, pl.ds(pl.multiple_of(slot * size, 8), size), :] = second_ref[c * size : (c + 1) * size, :]
    down_ref[...] = turned_ref[...].T
    ub_ref[...] = small_ref[pl.ds(tensor, 1), :]
    ob_ref[...] = small_ref[4:5, :]
    db_ref[...] = small_ref[5:6, :]
    qv_ref[...] = small_ref[8:10, pl.ds(pl.multiple_of(tensor * lanes, LANES), lanes)]
    sums = jnp.sum(small_ref[6:8, :], axis=1, keepdims=True)
    spread = jnp.concatenate([sums, jnp.zeros((6, 1), F32)], axis=0)
    alpha_ref[...] = jnp.broadcast_to(spread, (8, LANES))


def widen_kernel(first, ids_ref, a_any, b_any, *refs):
    out_any, sems, wide_ref, low_ref = refs[-4:]
    rows = low_ref.shape[1]
    copies = Copies(sems)
    ins = [copies.start(a, low_ref.at[n]) for n, a in enumerate((a_any, b_any))]
    half = rows // 2
    for n in range(2):
        ins[n].wait()
        slot = lax.bitwise_xor(ids_ref[1], first + n)
        for m in range(2):
            span = slice(m * half, (m + 1) * half)
            wide_ref[n, span, :] = low_ref[n, span, :].astype(F32)
            copies.send(wide_ref.at[n, span], out_any.at[slot, span])
    copies.finish()


def settle_kernel(r_ref, scol_ref, out_ref):
    out_ref[...] = dot(one_hot_cols(scol_ref[:, 0:1], r_ref.shape[0]), r_ref[...]).astype(BF)


def shape(dims, kind):
    return jax.ShapeDtypeStruct(dims, kind)


marks = {}


def call(kernel, ins, outs, scratch=(), deps=(), us=1.0, scalars=0, ins_any=0, outs_any=0, limit=24, aliases=None):
    n_in, n_out = len(ins), len(outs)
    whole = pl.BlockSpec(memory_space=pl.ANY)
    held = pl.BlockSpec(memory_space=pltpu.HBM)
    before = [marks.get(id(d), (d, d))[1] for d in deps]

    def body(*refs):
        skip = n_in + len(before)
        kernel(*refs[:n_in], *refs[skip : skip + n_out], *refs[skip + n_out + 1 :])

    made = pl.pallas_call(
        body,
        out_shape=[*outs, shape((8, LANES), F32)],
        in_specs=[smem()] * scalars + vmem(n_in - scalars - ins_any) + [whole] * (ins_any - len(aliases or ())) + [held] * len(aliases or ()) + [whole] * len(before),
        out_specs=vmem(n_out - outs_any) + [held] * (outs_any + 1),
        scratch_shapes=list(scratch),
        input_output_aliases=aliases or {},
        compiler_params=params(limit << 20),
        cost_estimate=cost(1e9 * us, 0),
    )(*ins, *before)
    for out in made[:-1]:
        marks[id(out)] = (out, made[-1])
    return made[:-1]


def per_device(
    block_input, cotangent, source, seq_lengths, qkv_weight, qv_bias, out_weight, out_bias,
    up_weight, up_bias, down_weight, down_bias, rezero_alphas,
):
    marks.clear()
    micros, rows, width = block_input.shape
    groups = lax.axis_size("dp")
    tensors = lax.axis_size("tensor")
    lanes = qkv_weight.shape[2]
    units = up_weight.shape[1]
    blocks = min(groups, 8)
    me, tensor = lax.axis_index("dp"), lax.axis_index("tensor")
    ids = jnp.stack([me, tensor]).astype(I32)
    lengths = lax.dynamic_index_in_dim(seq_lengths, tensor, 0, keepdims=False)[0]

    def across(axis, bit, value):
        count = tensors if axis == "tensor" else groups
        return lax.ppermute(value, axis, [(i, i ^ bit) for i in range(count)])

    def after(value, *others):
        return lax.optimization_barrier((value, *others))[0] if others else value

    def by_micro(kernel, n_whole, out_shape, scratch):
        return pl.pallas_call(
            kernel,
            out_shape=out_shape,
            grid_spec=pltpu.PrefetchScalarGridSpec(
                num_scalar_prefetch=1,
                grid=(1,),
                in_specs=[
                    pl.BlockSpec(source.shape, lambda i, s: (0, 0)),
                    pl.BlockSpec((1, rows, width), lambda i, s: (s[1], 0, 0)),
                ]
                + [pl.BlockSpec((rows // LANES, LANES), lambda i, s: (0, 0))] * n_whole,
                out_specs=[pl.BlockSpec(o.shape, lambda i, s: (0, 0)) for o in out_shape],
                scratch_shapes=scratch,
            ),
            compiler_params=params(),
            cost_estimate=cost(1e9 * C["route"], 0),
        )

    hot = pltpu.VMEM((rows, rows), BF)
    xs, srow, scol = by_micro(
        functools.partial(route_kernel, groups), 0,
        [shape((rows, width), BF), shape((rows // LANES, LANES), I32), shape((rows, LANES), I32)], [hot],
    )(ids, source, block_input)

    def exchange(rows_out):
        return lax.all_to_all(rows_out.reshape(groups, rows // groups, width), "dp", 0, 0, tiled=True).reshape(rows, width)

    arr_x = exchange(xs)
    gs, arow, acol = by_micro(
        second_kernel, 1,
        [shape((rows, width), BF), shape((8, rows), I32), shape((rows, LANES), I32)], [hot],
    )(ids, source, cotangent, srow)
    head = jnp.concatenate([qv_bias, up_bias.reshape(units // lanes, lanes), jnp.zeros((2, lanes), BF)], axis=0)
    own = (head, qkv_weight, out_weight, up_weight, down_weight)
    far = [across("tensor", 2, w) for w in own]
    held = lax.optimization_barrier((*far[:3], arow))[:3]

    def four(own, far):
        return own, across("tensor", 1, own), far, across("tensor", 1, far)

    bias4, wa4, wo4 = [four(w, f) for w, f in zip(own, held)]
    arr_g = exchange(gs)

    def v16(*dims):
        return pltpu.VMEM(dims, BF)

    def v32(*dims):
        return pltpu.VMEM(dims, F32)

    def sems(count):
        return pltpu.SemaphoreType.DMA((count,))

    ff = tensors * units
    wide = [shape((rows, width), BF)] * 4
    logs, x, q, k, v, o, h, low, attn = call(
        attend_kernel,
        (ids, lengths, rezero_alphas, *bias4, out_bias.reshape(1, width), acol, arr_x, *wa4, *wo4),
        [shape((2 * tensors, rows), F32), *wide, shape((rows, width), BF), shape((rows, width), F32),
         shape((rows, width), BF), shape((rows, width), F32)],
        [sems(40), v16(rows, width), v16(width, 3 * width), v16(width, width), v32(8, width), hot, v16(rows, width),
         v16(rows, width), v16(rows, width), v16(rows, width), v16(rows, width), v32(rows, width),
         v16(rows, width), v32(rows, width)],
        scalars=3, ins_any=9, outs_any=8, us=C["attend"], limit=60,
    )
    held = lax.optimization_barrier((*far[3:], logs))[:2]
    wu4, wd4 = [four(w, f) for w, f in zip(own[3:], held)]
    ys, act, slope, branch = call(
        forward_kernel,
        (rezero_alphas, *bias4, down_bias.reshape(1, width), arow, low, h, *wu4, *wd4),
        [shape((rows, width), BF), shape((rows, ff), BF), shape((rows, ff), F32), shape((rows, width), F32)],
        [sems(40), v16(rows, width), v32(rows, width), v16(width, ff), v16(ff, width), v16(rows, ff), v32(rows, ff),
         v32(rows, width), v16(rows, width), hot, v16(rows, width)],
        scalars=1, ins_any=10, outs_any=4, us=C["forward"], limit=60,
    )
    bundle = (width + units + lanes) // blocks
    part = shape((tensors // 2, blocks, bundle, width), BF)
    small1, go, gh, keep1, send1 = call(
        feed_kernel,
        (ids, rezero_alphas, acol, arr_g, *wu4, *wd4, *wo4, act, slope, low, branch, attn, o),
        [shape((8, width), F32), shape((rows, width), BF), shape((rows, width), F32),
         shape(part.shape, F32), part],
        [sems(48), v16(rows, width), v16(width, ff), v16(ff, width), v16(width, width), v16(rows, ff), v32(rows, ff),
         v16(rows, width), v32(rows, width), v32(rows, width), v16(rows, width),
         hot, v16(rows, width), v16(rows, width), v16(rows, ff), v32(rows, width), v16(rows, width), v16(rows, width),
         v32(*part.shape), v16(*part.shape), v32(width, width)],
        scalars=2, ins_any=19, outs_any=4, us=C["feed"], deps=(ys,), limit=60,
    )
    arr_y = exchange(ys)
    got = across("tensor", 1, send1)

    def back(first, last, deps):
        span = (last - first) * lanes
        return call(
            functools.partial(back_kernel, first), (lengths, logs, q, k, v, go),
            [shape((3, rows, span), BF)],
            [sems(16), v16(rows, span), v16(rows, span), v16(rows, span), v16(rows, span), v16(3, rows, span), v32(rows, lanes), v32(rows, lanes)],
            scalars=1, ins_any=4, outs_any=1, limit=60, deps=deps, us=C["back"],
        )[0]

    half = tensors // 2
    bare = shape((16, width), F32)

    def blocks_of(n, like, kind):
        return shape((n, *like.shape[1:]), kind)

    def settle(rows_back, deps):
        return call(settle_kernel, (rows_back, scol), [shape((rows, width), BF)], deps=deps, us=C["settle"])[0]

    def widen(first, a, b, into=None, deps=()):
        extra = () if into is None else (into,)
        return call(
            functools.partial(widen_kernel, first), (ids, a, b, *extra), [shape((tensors, rows, width), F32)],
            [sems(8), v32(2, rows, width), v16(2, rows, width)],
            scalars=1, ins_any=2 + len(extra), outs_any=1, us=C["widen"], deps=deps, aliases={3: 0} if extra else None,
        )[0]

    def relay(value, deps):
        return call(lambda *refs: None, (value,), [shape(value.shape, value.dtype)], ins_any=1, outs_any=1, aliases={0: 0}, deps=deps, us=0.1)[0]

    def gather(own):
        y0, r4, r2 = across("dp", 1, own), across("dp", 4, own), across("dp", 2, own)
        r4 = relay(r4, (y0, r2))
        y4, r6 = across("dp", 1, r4), across("dp", 2, r4)
        r2 = relay(r2, (y4, r6))
        return [own, y0, r2, across("dp", 1, r2), r4, y4, r6, across("dp", 1, r6)]

    keep1 = keep1.reshape(half * blocks, bundle, width)
    send1 = send1.reshape(half * blocks, bundle, width)
    got = across("tensor", 1, send1)
    n = half * blocks // 2
    even, low_half = (lambda b: b % 2 == 0), (lambda b: b < blocks // 2)
    keep1, send1 = call(
        functools.partial(halve_kernel, even), (keep1, got), [blocks_of(n, keep1, F32), blocks_of(n, keep1, BF)], us=C["halve"]
    )
    got_y = across("dp", 1, send1)
    grad_a = back(0, half, (keep1,))
    grad_b = back(half, tensors, (grad_a,))
    y_own = settle(arr_y, (grad_b,))
    y_far = across("tensor", 2, y_own)
    y_core = across("tensor", 1, y_own)
    n = n // 2
    keep1, send1 = call(
        functools.partial(halve_kernel, low_half), (keep1, got_y), [blocks_of(n, keep1, F32), blocks_of(n, keep1, BF)],
        deps=(y_own,), us=C["halve"],
    )
    got_x = across("tensor", 2, send1)
    share = (3 * width) // blocks
    split = 2 * 16 * width // LANES
    n2 = half * blocks
    small, keep2, send2 = call(
        weight_kernel, (ids, small1, grad_a, grad_b, x),
        [bare, shape((n2, share, lanes), F32), shape((n2 + 1, share, lanes), BF)],
        [sems(20), v16(rows, 3 * width), v16(rows, width), v32(n2, share, lanes), v16(n2, share, lanes), v32(width, 3 * width),
         v16(split, LANES)],
        scalars=1, ins_any=3, outs_any=2, us=C["weight"], deps=(keep1,), limit=60,
    )
    gxs = call(
        last_kernel, (ids, arow, grad_a, grad_b, gh, *wa4), [shape((rows, width), BF)],
        [sems(40), v16(rows, 3 * width), v32(rows, width), v16(width, 3 * width), hot, v16(rows, width), v16(rows, width)],
        scalars=1, ins_any=7, outs_any=1, us=C["last"], deps=(small,), limit=60,
    )[0]
    arr_gx = exchange(gxs)
    got = across("tensor", 1, send2)
    n2 = n2 // 2
    keep2, small, send2 = call(
        functools.partial(halve_small_kernel, lambda b: b < blocks), (keep2, small, got),
        [blocks_of(n2, keep2, F32), bare, blocks_of(n2 + 1, keep2, BF)], deps=(gxs,), us=C["part"],
    )
    got = across("tensor", 2, send2)
    own1, *parts1 = call(
        part_kernel, (keep1, got_x), [shape(keep1.shape[1:], F32)] + [shape(keep1.shape[1:], BF)] * (blocks // 2 - 1),
        deps=(keep2, y_far), us=C["part"],
    )
    got1 = [across("dp", 2 * (j + 1), v) for j, v in enumerate(parts1)]
    y_late = call(lambda *refs: None, (y_far,), [shape((rows, width), BF)], ins_any=1, outs_any=1, aliases={0: 0}, deps=(own1,), us=0.1)[0]
    output = widen(0, y_own, y_core, deps=(own1,))
    shared, small = call(
        whole_small_kernel, (keep2, small, got), [shape((blocks, share + split, lanes), BF), bare], deps=(output,), us=C["part"],
    )
    ranks = None if groups == blocks else [list(range(g, g + blocks)) for g in range(0, groups, blocks)]
    shared = lax.all_to_all(shared, "dp", 0, 0, tiled=True, axis_index_groups=ranks)
    gx_own = settle(arr_gx, (small, y_late))
    gx_far = across("tensor", 2, gx_own)
    gx_core = across("tensor", 1, gx_own)
    y_both = across("tensor", 1, y_late)
    own1 = call(sum_kernel, (own1, *got1), [shape(own1.shape, F32)], deps=(gx_own,), us=C["part"])[0]
    output = widen(2, y_late, y_both, output, deps=(own1,))
    gx_grad = widen(0, gx_own, gx_core, deps=(output,))
    kind = BF if groups <= blocks else F32
    own, small = call(
        pack_kernel, (own1, shared), [shape((bundle + share // 4, width), kind), bare], deps=(gx_grad,), us=C["halve"]
    )
    bit = blocks
    while bit < groups:
        kind = BF if 2 * bit == groups else F32
        own, small = call(
            add_one_kernel, (own, across("dp", bit, own), small, across("dp", bit, small)), [shape(own.shape, kind), bare]
        )
        bit *= 2
    gathered = gather(own)
    gx_far = relay(gx_far, (gathered[blocks - 2],))
    gx_both = across("tensor", 1, gx_far)
    qkv_grad, qv_grad, out_grad, ob_grad, up_grad, ub_grad, down_grad, db_grad, alphas = call(
        functools.partial(spread_kernel, blocks), (ids, small, *gathered),
        [shape((3, width, lanes), F32), shape((2, lanes), F32), shape((lanes, width), F32), shape((1, width), F32),
         shape((width, units), F32), shape((1, units), F32), shape((units, width), F32), shape((1, width), F32), shape((8, LANES), F32)],
        [v32(width, units), v32(share, lanes)], scalars=1, us=C["spread"],
    )
    input_grad = widen(2, gx_far, gx_both, gx_grad, deps=())
    return (
        output, input_grad, qkv_grad, qv_grad, out_grad, ob_grad[0], up_grad, ub_grad[0], down_grad, db_grad[0], alphas[0:2, 0],
    )


def solution(mesh):
    in_specs = (
        P(None, "dp", None), P(None, "dp", None), P(), P(None, "dp", None),
        P(None, None, "tensor"), P(None, "tensor"), P("tensor", None), P(),
        P(None, "tensor"), P("tensor"), P("tensor", None), P(), P(),
    )
    out_specs = (
        P(None, "dp", None), P(None, "dp", None), P(None, None, "tensor"), P(None, "tensor"),
        P("tensor", None), P(), P(None, "tensor"), P("tensor"), P("tensor", None), P(), P(),
    )
    return jax.shard_map(per_device, mesh=mesh, in_specs=in_specs, out_specs=out_specs, check_vma=False)
```

```python
import functools

import jax
import jax.numpy as jnp
from jax import lax
from jax.experimental import pallas as pl
from jax.experimental.pallas import tpu as pltpu
from jax.sharding import PartitionSpec as P

HEAD_SIZE = 64
LANES = 128
QT = 256
FT = 256
SLAB = 16
BF = jnp.bfloat16
F32 = jnp.float32
C = {"route": 6, "attend": 19, "forward": 5, "feed": 19, "back": 11, "halve": 1, "part": 5, "settle": 1, "last": 20, "weight": 0.2, "widen": 5, "spread": 3}
I32 = jnp.int32
NEG = -1e30
VMEM_LIMIT = 56 * 1024 * 1024
GELU_A = 0.7978845608028654
GELU_B = 0.044715

NN = (((1,), (0,)), ((), ()))
NT = (((1,), (1,)), ((), ()))
TN = (((0,), (0,)), ((), ()))


def dot(a, b, dims=NN):
    return lax.dot_general(a, b, dims, preferred_element_type=F32)


def iota(shape, dim):
    return lax.broadcasted_iota(I32, shape, dim)


def params(limit=VMEM_LIMIT):
    return pltpu.CompilerParams(vmem_limit_bytes=limit)


def cost(flops, nbytes, trans=0):
    return pl.CostEstimate(flops=int(flops), bytes_accessed=int(nbytes), transcendentals=int(trans))


def vmem(n):
    return [pl.BlockSpec(memory_space=pltpu.VMEM)] * n


def smem():
    return pl.BlockSpec(memory_space=pltpu.SMEM)


def one_hot_rows(row, count):
    return (iota((count, row.shape[1]), 0) == row).astype(F32).astype(BF)


def one_hot_cols(col, count):
    return (iota((col.shape[0], count), 1) == col).astype(F32).astype(BF)


def route_kernel(groups, ids_ref, src_ref, x_ref, xs_ref, srow_ref, scol_ref, hot_ref):
    me, micro = ids_ref[0], ids_ref[1]
    rows = x_ref.shape[1]
    chunks = rows // LANES
    share = rows // groups
    sub_hi = iota((chunks, rows), 0)
    sub_lo = iota((LANES, rows), 0)

    def gather_group(g, total):
        value = src_ref[pl.ds(micro, 1), pl.ds(pl.multiple_of(g * rows, LANES), rows)] - me * rows
        inside = (value >= 0) & (value < rows)
        high = jnp.where(inside, value // LANES, -1)
        low = jnp.where(inside, value % LANES, -1)
        hot_high = jnp.where(high == sub_hi, (g + 1).astype(F32), 0.0).astype(BF)
        hot_low = (low == sub_lo).astype(F32).astype(BF)
        return total + dot(hot_high, hot_low, NT)

    dest = lax.fori_loop(0, groups, gather_group, jnp.zeros((chunks, LANES), F32)).astype(I32) - 1
    before = (iota((LANES, LANES), 0) < iota((LANES, LANES), 1)).astype(F32).astype(BF)
    width = max(groups, 8)
    carry = jnp.zeros((width, 1), F32)
    for c in range(chunks):
        g_row = dest[c : c + 1, :]
        hot = (iota((width, LANES), 0) == g_row).astype(F32)
        ranks = dot(hot.astype(BF), before) + carry
        carry = carry + jnp.sum(hot, axis=1, keepdims=True)
        place = g_row * share + jnp.sum(hot * ranks, axis=0, keepdims=True).astype(I32)
        srow_ref[c : c + 1, :] = place
        spread = jnp.broadcast_to(place.astype(F32), (LANES, LANES))
        scol_ref[c * LANES : (c + 1) * LANES, :] = spread.T.astype(I32)
        hot_ref[:, c * LANES : (c + 1) * LANES] = one_hot_rows(place, rows)
    xs_ref[...] = dot(hot_ref[...], x_ref[0]).astype(BF)


def second_kernel(ids_ref, src_ref, g_ref, srow_ref, gs_ref, arow_ref, acol_ref, hot_ref):
    me, micro = ids_ref[0], ids_ref[1]
    rows = g_ref.shape[1]
    for c in range(rows // LANES):
        hot_ref[:, c * LANES : (c + 1) * LANES] = one_hot_rows(srow_ref[c : c + 1, :], rows)
    gs_ref[...] = dot(hot_ref[...], g_ref[0]).astype(BF)
    own = src_ref[pl.ds(micro, 1), pl.ds(pl.multiple_of(me * rows, LANES), rows)].astype(F32)
    for c in range(rows // LANES):
        piece = own[:, c * LANES : (c + 1) * LANES]
        column = jnp.broadcast_to(piece, (LANES, LANES)).T[:, 0:1]
        count = jnp.sum((own < column).astype(F32), axis=1, keepdims=True)
        spread = jnp.broadcast_to(count, (LANES, LANES))
        acol_ref[c * LANES : (c + 1) * LANES, :] = spread.astype(I32)
        arow_ref[0:1, c * LANES : (c + 1) * LANES] = spread.T[0:1, :].astype(I32)


def starts_of(len_ref, index):
    start = jnp.zeros_like(index)
    first = jnp.int32(0)
    for j in range(len_ref.shape[0] - 1):
        first = first + len_ref[j]
        start = jnp.where(index >= first, first, start)
    return start


class Copies:
    def __init__(self, sems):
        self.sems, self.used, self.left = sems, 0, []

    def start(self, source, target):
        copy = pltpu.make_async_copy(source, target, self.sems.at[self.used])
        self.used += 1
        copy.start()
        return copy

    def send(self, source, target):
        self.left.append(self.start(source, target))

    def finish(self):
        for copy in self.left:
            copy.wait()


def wait_all(copies):
    for copy in copies:
        copy.wait()


def attend_kernel(
    ids_ref, len_ref, alpha_ref, b0_ref, b1_ref, b2_ref, b3_ref, ob_ref, acol_ref,
    arr_any, wa0_any, wa1_any, wa2_any, wa3_any, wo0_any, wo1_any, wo2_any, wo3_any,
    l_ref, x_any, q_any, k_any, v_any, o_any, h_any, low_any, attn_any,
    sems, arr_ref, wcat_ref, wo_ref, bias_ref, hot_ref, x_ref, q_ref, k_ref, v_ref, ob16_ref, h_ref, low_ref, attn_ref,
):
    rows, width = arr_ref.shape
    lanes = wo0_any.shape[0]
    pieces = width // lanes
    heads = lanes // HEAD_SIZE
    tensor = ids_ref[1]
    copies = Copies(sems)
    first = copies.start(arr_any, arr_ref)
    weights, later = [], []
    for j, (wa, wo, b) in enumerate(
        ((wa0_any, wo0_any, b0_ref), (wa1_any, wo1_any, b1_ref), (wa2_any, wo2_any, b2_ref), (wa3_any, wo3_any, b3_ref))
    ):
        place = pl.multiple_of(lax.bitwise_xor(tensor, j) * lanes, LANES)
        for c in range(3):
            weights.append(copies.start(wa.at[c], wcat_ref.at[:, pl.ds(c * width + place, lanes)]))
        later.append(copies.start(wo, wo_ref.at[pl.ds(place, lanes), :]))
        bias_ref[:, pl.ds(place, lanes)] = b[...].astype(F32)
    hot_ref[...] = one_hot_cols(acol_ref[:, 0:1], rows)
    first.wait()
    x_ref[...] = dot(hot_ref[...], arr_ref[...]).astype(BF)
    copies.send(x_ref, x_any)
    wait_all(weights)
    q_ref[...] = (dot(x_ref[...], wcat_ref[:, 0:width]) + bias_ref[0:1, :]).astype(BF) * jnp.asarray(HEAD_SIZE**-0.5, BF)
    k_ref[...] = dot(x_ref[...], wcat_ref[:, width : 2 * width]).astype(BF)
    v_ref[...] = (dot(x_ref[...], wcat_ref[:, 2 * width :]) + bias_ref[1:2, :]).astype(BF)
    copies.send(q_ref, q_any)
    copies.send(k_ref, k_any)
    copies.send(v_ref, v_any)
    tiles = rows // QT
    lane = iota((QT, lanes), 1) // HEAD_SIZE
    masks = []
    for i in range(tiles):
        q_index = i * QT + iota((QT, 1), 0)
        k_index = iota((QT, (i + 1) * QT), 1)
        masks.append((k_index >= starts_of(len_ref, q_index)) & (k_index <= q_index))

    def scores_of(p, i, e):
        q = q_ref[i * QT : (i + 1) * QT, p * lanes : (p + 1) * lanes]
        return dot(jnp.where(lane == e, q, jnp.zeros_like(q)), k_ref[0 : (i + 1) * QT, p * lanes : (p + 1) * lanes], NT)

    items = [(p, i, e) for i in range(tiles) for p in range(pieces) for e in range(heads)]
    ahead = scores_of(*items[0])
    mixed = logs = None
    for step, (p, i, e) in enumerate(items):
        now = ahead
        if step + 1 < len(items):
            ahead = scores_of(*items[step + 1])
        scores = jnp.where(masks[i], now, NEG)
        top = jnp.max(scores, axis=1, keepdims=True)
        weights = jnp.exp(scores - top)
        total = jnp.sum(weights, axis=1, keepdims=True)
        low = (weights * (1.0 / total)).astype(BF)
        out = dot(low, v_ref[0 : (i + 1) * QT, p * lanes : (p + 1) * lanes])
        head = p * heads + e
        log_total = top + jnp.log(total)
        logs = jnp.where(iota((QT, LANES), 1) == head, log_total, 0.0 if head == 0 else logs)
        mixed = out if e == 0 else jnp.where(lane == e, out, mixed)
        if e == heads - 1:
            ob16_ref[i * QT : (i + 1) * QT, p * lanes : (p + 1) * lanes] = mixed.astype(BF)
        if head == pieces * heads - 1:
            l_ref[:, i * QT : (i + 1) * QT] = logs.T[0 : pieces * heads, :]
            if i == 0:
                wait_all(later)
            span = slice(i * QT, (i + 1) * QT)
            copies.send(ob16_ref.at[span], o_any.at[span])
            attn = dot(ob16_ref[span, :], wo_ref[...]) + ob_ref[...].astype(F32)
            hidden = x_ref[span, :].astype(F32) + alpha_ref[0] * attn
            attn_ref[span, :] = attn
            h_ref[span, :] = hidden
            low_ref[span, :] = hidden.astype(BF)
            copies.send(attn_ref.at[span], attn_any.at[span])
            copies.send(h_ref.at[span], h_any.at[span])
            copies.send(low_ref.at[span], low_any.at[span])
    copies.finish()


def unit_biases(refs, units):
    biases = []
    for b in refs:
        tail = b[...].astype(F32)
        biases.append(jnp.concatenate([tail[2 + n : 3 + n, :] for n in range(units // LANES)], axis=1))
    return biases


def rise_of(z):
    square = z * z
    return 0.5 + 0.5 * jnp.tanh(z * (GELU_A + (GELU_A * GELU_B) * square)), square


def forward_kernel(
    alpha_ref, b0_ref, b1_ref, b2_ref, b3_ref, db_ref, arow_ref,
    low_any, h_any, wu0_any, wu1_any, wu2_any, wu3_any, wd0_any, wd1_any, wd2_any, wd3_any,
    ys_any, f_any,
    sems, low_ref, h_ref, wu_ref, wd_ref, act_ref, f_ref, y_ref, hot_ref, ys_ref,
):
    rows, width = low_ref.shape
    units = wu0_any.shape[1]
    copies = Copies(sems)
    first = copies.start(low_any, low_ref)
    up, down = [], []
    for j, wu in enumerate((wu0_any, wu1_any, wu2_any, wu3_any)):
        up.append(copies.start(wu, wu_ref.at[:, j * units : (j + 1) * units]))
    for j, wd in enumerate((wd0_any, wd1_any, wd2_any, wd3_any)):
        down.append(copies.start(wd, wd_ref.at[j * units : (j + 1) * units, :]))
    hidden = copies.start(h_any, h_ref)
    biases = unit_biases((b0_ref, b1_ref, b2_ref, b3_ref), units)
    first.wait()
    items = [(j, m) for j in range(len(biases)) for m in range(rows // FT)]

    def z_of(j, m):
        if m == 0:
            up[j].wait()
        return dot(low_ref[m * FT : (m + 1) * FT, :], wu_ref[:, j * units : (j + 1) * units])

    ahead = z_of(*items[0])
    for step, (j, m) in enumerate(items):
        now = ahead
        if step + 1 < len(items):
            ahead = z_of(*items[step + 1])
        for n in range(FT // SLAB):
            z = now[n * SLAB : (n + 1) * SLAB] + biases[j]
            rise, _ = rise_of(z)
            act_ref[m * FT + n * SLAB : m * FT + (n + 1) * SLAB, j * units : (j + 1) * units] = (z * rise).astype(BF)
    wait_all(down)
    hidden.wait()
    for m in range(rows // FT):
        span = slice(m * FT, (m + 1) * FT)
        branch = dot(act_ref[span, :], wd_ref[...]) + db_ref[...].astype(F32)
        f_ref[span, :] = branch
        copies.send(f_ref.at[span], f_any.at[span])
        y_ref[span, :] = (h_ref[span, :] + alpha_ref[1] * branch).astype(BF)
        hot_ref[span, :] = (iota((FT, rows), 0) + m * FT == arow_ref[0:1, :]).astype(F32).astype(BF)
    for m in range(rows // FT):
        span = slice(m * FT, (m + 1) * FT)
        ys_ref[span, :] = dot(hot_ref[span, :], y_ref[...]).astype(BF)
        copies.send(ys_ref.at[span], ys_any.at[span])
    copies.finish()


def feed_kernel(
    ids_ref, alpha_ref, b0_ref, b1_ref, b2_ref, b3_ref, acol_ref,
    arr_any, wu0_any, wu1_any, wu2_any, wu3_any, wd0_any, wd1_any, wd2_any, wd3_any,
    wo0_any, wo1_any, wo2_any, wo3_any, low_any, f_any, attn_any, o_any,
    small_ref, go_any, gh_any, keep_any, send_any,
    sems, arr_ref, wu_ref, wd_ref, wo_ref, act_ref, low_ref, f_ref, attn_ref, o_ref,
    hot_ref, g_ref, gf_ref, gz_ref, gh_ref, ga_ref, go_ref, keep_ref, part_ref, w_ref,
):
    me, tensor = ids_ref[0], ids_ref[1]
    rows, width = low_ref.shape
    units = wu0_any.shape[1]
    lanes = wo0_any.shape[0]
    blocks = part_ref.shape[1]
    own = me % blocks
    copies = Copies(sems)
    first = copies.start(arr_any, arr_ref)
    lowed = copies.start(low_any, low_ref)
    down, up, later = [], [], []
    for j, (wu, wd) in enumerate(
        ((wu0_any, wd0_any), (wu1_any, wd1_any), (wu2_any, wd2_any), (wu3_any, wd3_any))
    ):
        span = slice(j * units, (j + 1) * units)
        up.append(copies.start(wu, wu_ref.at[:, span]))
        down.append(copies.start(wd, wd_ref.at[span, :]))
    for j, wo in enumerate((wo0_any, wo1_any, wo2_any, wo3_any)):
        place = pl.multiple_of(lax.bitwise_xor(tensor, j) * lanes, LANES)
        later.append(copies.start(wo, wo_ref.at[pl.ds(place, lanes), :]))
    later.append(copies.start(attn_any, attn_ref))
    later.append(copies.start(o_any, o_ref))
    branched = copies.start(f_any, f_ref)
    hot_ref[...] = one_hot_cols(acol_ref[:, 0:1], rows)
    first.wait()
    for m in range(rows // FT):
        span = slice(m * FT, (m + 1) * FT)
        grad = dot(hot_ref[span, :], arr_ref[...])
        g_ref[span, :] = grad.astype(BF)
        gf_ref[span, :] = (alpha_ref[1] * grad).astype(BF)
    items = [(j, m) for j in range(len(up)) for m in range(rows // FT)]

    biases = unit_biases((b0_ref, b1_ref, b2_ref, b3_ref), units)
    lowed.wait()

    def both_of(j, m):
        if m == 0:
            up[j].wait()
            down[j].wait()
        span, unit = slice(m * FT, (m + 1) * FT), slice(j * units, (j + 1) * units)
        return dot(low_ref[span, :], wu_ref[:, unit]), dot(gf_ref[span, :], wd_ref[unit, :], NT)

    ahead = both_of(*items[0])
    for step, (j, m) in enumerate(items):
        now = ahead
        if step + 1 < len(items):
            ahead = both_of(*items[step + 1])
        for n in range(FT // SLAB):
            slab = slice(n * SLAB, (n + 1) * SLAB)
            z = now[0][slab] + biases[j]
            rise, square = rise_of(z)
            slope = rise + z * (rise - rise * rise) * ((2 * GELU_A) + (6 * GELU_A * GELU_B) * square)
            span = (slice(m * FT + n * SLAB, m * FT + (n + 1) * SLAB), slice(j * units, (j + 1) * units))
            act_ref[span] = (z * rise).astype(BF)
            gz_ref[span] = (now[1][slab] * slope).astype(BF)
    wait_all(later)
    gh_sum = attn_sum = jnp.zeros((1, width), F32)
    for m in range(rows // FT):
        span = slice(m * FT, (m + 1) * FT)
        grad_hidden = g_ref[span, :].astype(F32) + dot(gz_ref[span, :], wu_ref[...], NT)
        gh_ref[span, :] = grad_hidden
        copies.send(gh_ref.at[span], gh_any.at[span])
        ga = (alpha_ref[0] * grad_hidden).astype(BF)
        ga_ref[span, :] = ga
        gh_sum = gh_sum + jnp.sum(ga.astype(F32), axis=0, keepdims=True)
        attn_sum = attn_sum + jnp.sum(grad_hidden * attn_ref[span, :], axis=0, keepdims=True)
    for m in range(rows // FT):
        span = slice(m * FT, (m + 1) * FT)
        go = dot(ga_ref[span, :], wo_ref[...], NT).astype(BF)
        go_ref[span, :] = go
        copies.send(go_ref.at[span], go_any.at[span])

    def place(j, first_row, value):
        count = value.shape[0] // blocks
        out = keep_ref if j % 2 == 0 else part_ref
        for b in range(blocks):
            out[j // 2, lax.bitwise_xor(own, b), first_row : first_row + count, :] = value[b * count : (b + 1) * count].astype(out.dtype)

    low_t = low_ref[...].T
    gf_t = gf_ref[...].T
    o_t = o_ref[...].T
    w_ref[...] = dot(o_t, ga_ref[...])
    edge = (width + units) // blocks
    for j in range(len(up)):
        span = slice(j * units, (j + 1) * units)
        place(j, 0, dot(low_t, gz_ref[:, span]))
        place(j, width // blocks, dot(gf_t, act_ref[:, span]))
        at = pl.multiple_of(lax.bitwise_xor(tensor, j) * lanes, LANES)
        place(j, edge, w_ref[pl.ds(at, lanes), :])
        held, out = (keep_ref, keep_any) if j % 2 == 0 else (part_ref, send_any)
        copies.send(held.at[j // 2], out.at[j // 2])
        small_ref[pl.ds(lax.bitwise_xor(tensor, j), 1), :] = jnp.sum(gz_ref[:, span].astype(F32), axis=0, keepdims=True)
    branched.wait()
    small_ref[4:5, :] = gh_sum
    small_ref[5:6, :] = jnp.sum(gf_ref[...].astype(F32), axis=0, keepdims=True)
    small_ref[6:7, :] = attn_sum
    small_ref[7:8, :] = jnp.sum(g_ref[...].astype(F32) * f_ref[...], axis=0, keepdims=True)
    copies.finish()


def starts_of(len_ref, index):
    start = jnp.zeros_like(index)
    first = jnp.int32(0)
    for j in range(len_ref.shape[0] - 1):
        first = first + len_ref[j]
        start = jnp.where(index >= first, first, start)
    return start


def back_kernel(
    first_pair, len_ref, l_ref, q_any, k_any, v_any, go_any,
    grad_any,
    sems, q_ref, k_ref, v_ref, go_ref, grad_ref, gk_ref, gv_ref,
):
    rows, width = q_ref.shape
    lanes = 2 * HEAD_SIZE
    heads = 2
    pairs = width // lanes
    scale = HEAD_SIZE**-0.5
    copies = Copies(sems)
    columns = slice(first_pair * lanes, first_pair * lanes + width)
    ins = [copies.start(a.at[:, columns], r) for a, r in ((q_any, q_ref), (k_any, k_ref), (v_any, v_ref), (go_any, go_ref))]
    tiles = rows // QT
    lane = iota((QT, lanes), 1) // HEAD_SIZE
    masks = []
    for i in range(tiles):
        q_index = i * QT + iota((1, QT), 1)
        k_index = iota(((i + 1) * QT, QT), 0)
        masks.append((k_index >= starts_of(len_ref, q_index)) & (k_index <= q_index))
    wait_all(ins)
    items = [(p, i, e) for p in range(pairs) for i in reversed(range(tiles)) for e in range(heads)]

    def pick(ref, p, i, e):
        value = ref[i * QT : (i + 1) * QT, p * lanes : (p + 1) * lanes]
        return jnp.where(lane == e, value, jnp.zeros_like(value))

    def both_of(p, i, e):
        pair = (slice(0, (i + 1) * QT), slice(p * lanes, (p + 1) * lanes))
        return dot(k_ref[pair], pick(q_ref, p, i, e), NT), dot(v_ref[pair], pick(go_ref, p, i, e), NT)

    ahead = both_of(*items[0])
    gq = None
    for step, (p, i, e) in enumerate(items):
        scores, grad_weights = ahead
        if step + 1 < len(items):
            ahead = both_of(*items[step + 1])
        head = (first_pair + p) * heads + e
        n = (i + 1) * QT
        weights = jnp.exp(jnp.where(masks[i], scores - l_ref[head : head + 1, i * QT : n], NEG))
        inner = jnp.sum(weights * grad_weights, axis=0, keepdims=True)
        grad_scores = (weights * (grad_weights - inner)).astype(BF)
        gv = dot(weights.astype(BF), pick(go_ref, p, i, e))
        gk = dot(grad_scores, pick(q_ref, p, i, e))
        if i == tiles - 1 and e == 0:
            gv_ref[...] = gv
            gk_ref[...] = gk
        else:
            gv_ref[0:n, :] += gv
            gk_ref[0:n, :] += gk
        gq_e = dot(grad_scores, k_ref[0:n, p * lanes : (p + 1) * lanes], TN)
        gq = gq_e if e == 0 else jnp.where(lane == e, gq_e, gq)
        if e == heads - 1:
            span = (slice(i * QT, n), slice(p * lanes, (p + 1) * lanes))
            grad_ref[(0, *span)] = (gq * scale).astype(BF)
            grad_ref[(1, *span)] = gk_ref[i * QT : n, :].astype(BF)
            grad_ref[(2, *span)] = gv_ref[i * QT : n, :].astype(BF)
            if i == 0:
                copies.send(grad_ref.at[:, :, p * lanes : (p + 1) * lanes], grad_any.at[:, :, p * lanes : (p + 1) * lanes])
    copies.finish()


def split_small(value, out_ref):
    chunks = value.shape[1] // LANES
    for c in range(chunks):
        left = value[:, c * LANES : (c + 1) * LANES]
        for k in range(2):
            term = left.astype(BF)
            first = (k * chunks + c) * 16
            out_ref[first : first + 16, :] = term
            left = left - term.astype(F32)


def join_small(ref, width):
    chunks = width // LANES
    parts = []
    for c in range(chunks):
        terms = [ref[(k * chunks + c) * 16 : (k * chunks + c + 1) * 16, :].astype(F32) for k in range(2)]
        parts.append(terms[0] + terms[1])
    return jnp.concatenate(parts, axis=1)


def last_kernel(
    ids_ref, arow_ref, grad_a_any, grad_b_any, gh_any, wa0_any, wa1_any, wa2_any, wa3_any,
    gxs_any,
    sems, grad_ref, gh_ref, wcat_ref, hot_ref, gx_ref, gxs_ref,
):
    tensor = ids_ref[1]
    rows, width = gx_ref.shape
    lanes = wa0_any.shape[2]
    half = width // 2
    copies = Copies(sems)
    grads, weights = [], []
    for c in range(3):
        for n, g in enumerate((grad_a_any, grad_b_any)):
            grads.append(copies.start(g.at[c], grad_ref.at[:, c * width + n * half : c * width + (n + 1) * half]))
    for j, wa in enumerate((wa0_any, wa1_any, wa2_any, wa3_any)):
        place = pl.multiple_of(lax.bitwise_xor(tensor, j) * lanes, LANES)
        for c in range(3):
            weights.append(copies.start(wa.at[c], wcat_ref.at[:, pl.ds(c * width + place, lanes)]))
    hidden = copies.start(gh_any, gh_ref)
    for m in range(rows // FT):
        hot_ref[m * FT : (m + 1) * FT, :] = (iota((FT, rows), 0) + m * FT == arow_ref[0:1, :]).astype(F32).astype(BF)
    wait_all(grads)
    wait_all(weights)
    hidden.wait()
    for m in range(rows // FT):
        span = slice(m * FT, (m + 1) * FT)
        gx_ref[span, :] = (gh_ref[span, :] + dot(grad_ref[span, :], wcat_ref[...], NT)).astype(BF)
    for m in range(rows // FT):
        span = slice(m * FT, (m + 1) * FT)
        gxs_ref[span, :] = dot(hot_ref[span, :], gx_ref[...]).astype(BF)
        copies.send(gxs_ref.at[span], gxs_any.at[span])
    copies.finish()


def weight_kernel(
    ids_ref, small1_ref, grad_a_any, grad_b_any, x_any,
    small_ref, keep_any, send_any,
    sems, grad_ref, x_ref, keep_ref, part_ref, w_ref, split_ref,
):
    tensor = ids_ref[1]
    rows, width = x_ref.shape
    lanes = keep_ref.shape[2]
    half = width // 2
    blocks = keep_ref.shape[0] // 2
    copies = Copies(sems)
    xs = copies.start(x_any, x_ref)
    grads = [
        [
            copies.start(g.at[c], grad_ref.at[:, c * width + n * half : c * width + (n + 1) * half])
            for n, g in enumerate((grad_a_any, grad_b_any))
        ]
        for c in range(3)
    ]
    xs.wait()
    x_t = x_ref[...].T
    count = width // blocks
    small_ref[0:8, :] = small1_ref[...]
    small_ref[8:16, :] = jnp.zeros((8, width), F32)
    for c in range(3):
        wait_all(grads[c])
        span = slice(c * width, (c + 1) * width)
        w_ref[:, span] = dot(x_t, grad_ref[:, span])
        if c != 1:
            row = 8 + c // 2
            small_ref[row : row + 1, :] = jnp.sum(grad_ref[:, span].astype(F32), axis=0, keepdims=True)
    for j in range(width // lanes):
        at = pl.multiple_of(lax.bitwise_xor(tensor, j) * lanes, LANES)
        held, out = (keep_ref, keep_any) if j % 2 == 0 else (part_ref, send_any)
        first = j // 2 * blocks
        for c in range(3):
            for b in range(blocks):
                held[first + b, c * count : (c + 1) * count, :] = w_ref[
                    b * count : (b + 1) * count, pl.ds(c * width + at, lanes)
                ].astype(held.dtype)
        copies.send(held.at[pl.ds(first, blocks)], out.at[pl.ds(first, blocks)])
    split_small(small_ref[...], split_ref)
    copies.send(split_ref, send_any.at[send_any.shape[0] - 1, 0 : split_ref.shape[0]])
    copies.finish()


def halve_kernel(pick, keep_ref, got_ref, next_ref, send_ref):
    here = there = 0
    for b in range(keep_ref.shape[0]):
        total = keep_ref[b] + got_ref[b].astype(F32)
        if pick(b):
            next_ref[here] = total
            here += 1
        else:
            send_ref[there] = total.astype(BF)
            there += 1


def halve_small_kernel(pick, keep_ref, small_ref, got_ref, next_ref, total_ref, send_ref):
    halve_kernel(pick, keep_ref, got_ref, next_ref, send_ref)
    total = small_ref[...] + join_small(got_ref.at[got_ref.shape[0] - 1], small_ref.shape[1])
    total_ref[...] = total
    split_small(total, send_ref.at[send_ref.shape[0] - 1])


def part_kernel(keep_ref, got_ref, *outs):
    for b in range(keep_ref.shape[0]):
        outs[b][...] = (keep_ref[b] + got_ref[b].astype(F32)).astype(outs[b].dtype)


def whole_small_kernel(keep_ref, small_ref, got_ref, send_ref, total_ref):
    rows = keep_ref.shape[1]
    total = small_ref[...] + join_small(got_ref.at[got_ref.shape[0] - 1], small_ref.shape[1])
    total_ref[...] = total
    for b in range(keep_ref.shape[0]):
        send_ref[b, 0:rows, :] = (keep_ref[b] + got_ref[b].astype(F32)).astype(BF)
        if b == 0:
            split_small(total, send_ref.at[0, rows:])
        else:
            send_ref[b, rows:, :] = send_ref[0, rows:, :]


def sum_kernel(own_ref, a_ref, b_ref, c_ref, out_ref):
    out_ref[...] = own_ref[...] + a_ref[...].astype(F32) + b_ref[...].astype(F32) + c_ref[...].astype(F32)


def pack_kernel(own1_ref, got_ref, packed_ref, total_ref):
    first = own1_ref[...]
    ways = own1_ref.shape[1] // got_ref.shape[2]
    rows, lanes = got_ref.shape[1] - 2 * 16 * ways, got_ref.shape[2]
    value = total = 0.0
    for b in range(got_ref.shape[0]):
        value = value + got_ref[b, 0:rows, :].astype(F32)
        total = total + join_small(got_ref.at[b, rows:], total_ref.shape[1])
    total_ref[...] = total
    edge = own1_ref.shape[0]
    packed_ref[0:edge, :] = first.astype(packed_ref.dtype)
    for c in range(ways):
        packed_ref[edge:, c * lanes : (c + 1) * lanes] = value[c * (rows // ways) : (c + 1) * (rows // ways)].astype(packed_ref.dtype)


def add_one_kernel(a_ref, b_ref, small_ref, other_ref, out_ref, total_ref):
    out_ref[...] = (a_ref[...].astype(F32) + b_ref[...].astype(F32)).astype(out_ref.dtype)
    total_ref[...] = small_ref[...] + other_ref[...]


def spread_kernel(count, ids_ref, small_ref, *refs):
    blocks = refs[:count]
    qkv_ref, qv_ref, out_ref, ob_ref, up_ref, ub_ref, down_ref, db_ref, alpha_ref, turned_ref, second_ref = refs[count:]
    me, tensor = ids_ref[0], ids_ref[1]
    lanes = out_ref.shape[0]
    for j, ref in enumerate(blocks):
        slot = lax.bitwise_xor(me % count, j)
        first = 0
        for out in (up_ref, turned_ref, out_ref):
            size = out.shape[0] // count
            out[pl.ds(pl.multiple_of(slot * size, 8), size), :] = ref[first : first + size, :].astype(F32)
            first += size
        size = qkv_ref.shape[1] // count
        rest = ref.shape[0] - first
        for c in range(ref.shape[1] // lanes):
            second_ref[c * rest : (c + 1) * rest, :] = ref[first:, c * lanes : (c + 1) * lanes].astype(F32)
        for c in range(3):
            qkv_ref[c, pl.ds(pl.multiple_of(slot * size, 8), size), :] = second_ref[c * size : (c + 1) * size, :]
    down_ref[...] = turned_ref[...].T
    ub_ref[...] = small_ref[pl.ds(tensor, 1), :]
    ob_ref[...] = small_ref[4:5, :]
    db_ref[...] = small_ref[5:6, :]
    qv_ref[...] = small_ref[8:10, pl.ds(pl.multiple_of(tensor * lanes, LANES), lanes)]
    sums = jnp.sum(small_ref[6:8, :], axis=1, keepdims=True)
    spread = jnp.concatenate([sums, jnp.zeros((6, 1), F32)], axis=0)
    alpha_ref[...] = jnp.broadcast_to(spread, (8, LANES))


def widen_kernel(first, ids_ref, a_any, b_any, *refs):
    out_any, sems, wide_ref, low_ref = refs[-4:]
    rows = low_ref.shape[1]
    copies = Copies(sems)
    ins = [copies.start(a, low_ref.at[n]) for n, a in enumerate((a_any, b_any))]
    half = rows // 2
    for n in range(2):
        ins[n].wait()
        slot = lax.bitwise_xor(ids_ref[1], first + n)
        for m in range(2):
            span = slice(m * half, (m + 1) * half)
            wide_ref[n, span, :] = low_ref[n, span, :].astype(F32)
            copies.send(wide_ref.at[n, span], out_any.at[slot, span])
    copies.finish()


def settle_kernel(r_ref, scol_ref, out_ref):
    out_ref[...] = dot(one_hot_cols(scol_ref[:, 0:1], r_ref.shape[0]), r_ref[...]).astype(BF)


def shape(dims, kind):
    return jax.ShapeDtypeStruct(dims, kind)


marks = {}


def call(kernel, ins, outs, scratch=(), deps=(), us=1.0, scalars=0, ins_any=0, outs_any=0, limit=24, aliases=None):
    n_in, n_out = len(ins), len(outs)
    whole = pl.BlockSpec(memory_space=pl.ANY)
    held = pl.BlockSpec(memory_space=pltpu.HBM)
    before = [marks.get(id(d), (d, d))[1] for d in deps]

    def body(*refs):
        skip = n_in + len(before)
        kernel(*refs[:n_in], *refs[skip : skip + n_out], *refs[skip + n_out + 1 :])

    made = pl.pallas_call(
        body,
        out_shape=[*outs, shape((8, LANES), F32)],
        in_specs=[smem()] * scalars + vmem(n_in - scalars - ins_any) + [whole] * (ins_any - len(aliases or ())) + [held] * len(aliases or ()) + [held if id(d) in marks else whole for d in deps],
        out_specs=vmem(n_out - outs_any) + [held] * (outs_any + 1),
        scratch_shapes=list(scratch),
        input_output_aliases=aliases or {},
        compiler_params=params(limit << 20),
        cost_estimate=cost(1e9 * us, 0),
    )(*ins, *before)
    for out in made[:-1]:
        marks[id(out)] = (out, made[-1])
    return made[:-1]


def per_device(
    block_input, cotangent, source, seq_lengths, qkv_weight, qv_bias, out_weight, out_bias,
    up_weight, up_bias, down_weight, down_bias, rezero_alphas,
):
    marks.clear()
    micros, rows, width = block_input.shape
    groups = lax.axis_size("dp")
    tensors = lax.axis_size("tensor")
    lanes = qkv_weight.shape[2]
    units = up_weight.shape[1]
    blocks = min(groups, 8)
    me, tensor = lax.axis_index("dp"), lax.axis_index("tensor")
    ids = jnp.stack([me, tensor]).astype(I32)
    lengths = lax.dynamic_index_in_dim(seq_lengths, tensor, 0, keepdims=False)[0]

    def across(axis, bit, value):
        count = tensors if axis == "tensor" else groups
        return lax.ppermute(value, axis, [(i, i ^ bit) for i in range(count)])

    def after(value, *others):
        return lax.optimization_barrier((value, *others))[0] if others else value

    def by_micro(kernel, n_whole, out_shape, scratch):
        return pl.pallas_call(
            kernel,
            out_shape=out_shape,
            grid_spec=pltpu.PrefetchScalarGridSpec(
                num_scalar_prefetch=1,
                grid=(1,),
                in_specs=[
                    pl.BlockSpec(source.shape, lambda i, s: (0, 0)),
                    pl.BlockSpec((1, rows, width), lambda i, s: (s[1], 0, 0)),
                ]
                + [pl.BlockSpec((rows // LANES, LANES), lambda i, s: (0, 0))] * n_whole,
                out_specs=[pl.BlockSpec(o.shape, lambda i, s: (0, 0)) for o in out_shape],
                scratch_shapes=scratch,
            ),
            compiler_params=params(),
            cost_estimate=cost(1e9 * C["route"], 0),
        )

    hot = pltpu.VMEM((rows, rows), BF)
    xs, srow, scol = by_micro(
        functools.partial(route_kernel, groups), 0,
        [shape((rows, width), BF), shape((rows // LANES, LANES), I32), shape((rows, LANES), I32)], [hot],
    )(ids, source, block_input)

    def exchange(rows_out):
        return lax.all_to_all(rows_out.reshape(groups, rows // groups, width), "dp", 0, 0, tiled=True).reshape(rows, width)

    arr_x = exchange(xs)
    gs, arow, acol = by_micro(
        second_kernel, 1,
        [shape((rows, width), BF), shape((8, rows), I32), shape((rows, LANES), I32)], [hot],
    )(ids, source, cotangent, srow)
    head = jnp.concatenate([qv_bias, up_bias.reshape(units // lanes, lanes), jnp.zeros((2, lanes), BF)], axis=0)
    own = (head, qkv_weight, out_weight, up_weight, down_weight)
    far = [across("tensor", 2, w) for w in own]
    held = lax.optimization_barrier((*far[:3], arow))[:3]

    def four(own, far):
        return own, across("tensor", 1, own), far, across("tensor", 1, far)

    bias4, wa4, wo4 = [four(w, f) for w, f in zip(own, held)]
    arr_g = exchange(gs)

    def v16(*dims):
        return pltpu.VMEM(dims, BF)

    def v32(*dims):
        return pltpu.VMEM(dims, F32)

    def sems(count):
        return pltpu.SemaphoreType.DMA((count,))

    ff = tensors * units
    wide = [shape((rows, width), BF)] * 4
    logs, x, q, k, v, o, h, low, attn = call(
        attend_kernel,
        (ids, lengths, rezero_alphas, *bias4, out_bias.reshape(1, width), acol, arr_x, *wa4, *wo4),
        [shape((2 * tensors, rows), F32), *wide, shape((rows, width), BF), shape((rows, width), F32),
         shape((rows, width), BF), shape((rows, width), F32)],
        [sems(40), v16(rows, width), v16(width, 3 * width), v16(width, width), v32(8, width), hot, v16(rows, width),
         v16(rows, width), v16(rows, width), v16(rows, width), v16(rows, width), v32(rows, width),
         v16(rows, width), v32(rows, width)],
        scalars=3, ins_any=9, outs_any=8, us=C["attend"], limit=60,
    )
    held = lax.optimization_barrier((*far[3:], logs))[:2]
    wu4, wd4 = [four(w, f) for w, f in zip(own[3:], held)]
    ys, branch = call(
        forward_kernel,
        (rezero_alphas, *bias4, down_bias.reshape(1, width), arow, low, h, *wu4, *wd4),
        [shape((rows, width), BF), shape((rows, width), F32)],
        [sems(40), v16(rows, width), v32(rows, width), v16(width, ff), v16(ff, width), v16(rows, ff),
         v32(rows, width), v16(rows, width), hot, v16(rows, width)],
        scalars=1, ins_any=10, outs_any=2, us=C["forward"], limit=60,
    )
    bundle = (width + units + lanes) // blocks
    part = shape((tensors // 2, blocks, bundle, width), BF)
    small1, go, gh, keep1, send1 = call(
        feed_kernel,
        (ids, rezero_alphas, *bias4, acol, arr_g, *wu4, *wd4, *wo4, low, branch, attn, o),
        [shape((8, width), F32), shape((rows, width), BF), shape((rows, width), F32),
         shape(part.shape, F32), part],
        [sems(48), v16(rows, width), v16(width, ff), v16(ff, width), v16(width, width), v16(rows, ff),
         v16(rows, width), v32(rows, width), v32(rows, width), v16(rows, width),
         hot, v16(rows, width), v16(rows, width), v16(rows, ff), v32(rows, width), v16(rows, width), v16(rows, width),
         v32(*part.shape), v16(*part.shape), v32(width, width)],
        scalars=2, ins_any=17, outs_any=4, us=C["feed"], deps=(ys,), limit=60,
    )
    arr_y = exchange(ys)
    got = across("tensor", 1, send1)

    def back(first, last, deps):
        span = (last - first) * lanes
        return call(
            functools.partial(back_kernel, first), (lengths, logs, q, k, v, go),
            [shape((3, rows, span), BF)],
            [sems(16), v16(rows, span), v16(rows, span), v16(rows, span), v16(rows, span), v16(3, rows, span), v32(rows, lanes), v32(rows, lanes)],
            scalars=1, ins_any=4, outs_any=1, limit=60, deps=deps, us=C["back"],
        )[0]

    half = tensors // 2
    bare = shape((16, width), F32)

    def blocks_of(n, like, kind):
        return shape((n, *like.shape[1:]), kind)

    def settle(rows_back, deps):
        return call(settle_kernel, (rows_back, scol), [shape((rows, width), BF)], deps=deps, us=C["settle"])[0]

    def widen(first, a, b, into=None, deps=()):
        extra = () if into is None else (into,)
        return call(
            functools.partial(widen_kernel, first), (ids, a, b, *extra), [shape((tensors, rows, width), F32)],
            [sems(8), v32(2, rows, width), v16(2, rows, width)],
            scalars=1, ins_any=2 + len(extra), outs_any=1, us=C["widen"], deps=deps, aliases={3: 0} if extra else None,
        )[0]

    def relay(value, deps):
        return call(lambda *refs: None, (value,), [shape(value.shape, value.dtype)], ins_any=1, outs_any=1, aliases={0: 0}, deps=deps, us=0.1)[0]

    def gather(own):
        y0, r4, r2 = across("dp", 1, own), across("dp", 4, own), across("dp", 2, own)
        r4 = relay(r4, (y0, r2))
        y4, r6 = across("dp", 1, r4), across("dp", 2, r4)
        r2 = relay(r2, (y4, r6))
        return [own, y0, r2, across("dp", 1, r2), r4, y4, r6, across("dp", 1, r6)]

    keep1 = keep1.reshape(half * blocks, bundle, width)
    send1 = send1.reshape(half * blocks, bundle, width)
    got = across("tensor", 1, send1)
    n = half * blocks // 2
    even, low_half = (lambda b: b % 2 == 0), (lambda b: b < blocks // 2)
    keep1, send1 = call(
        functools.partial(halve_kernel, even), (keep1, got), [blocks_of(n, keep1, F32), blocks_of(n, keep1, BF)], us=C["halve"]
    )
    got_y = across("dp", 1, send1)
    grad_a = back(0, half, (keep1,))
    grad_b = back(half, tensors, (grad_a,))
    y_own = settle(arr_y, (grad_b,))
    y_far = across("tensor", 2, y_own)
    y_core = across("tensor", 1, y_own)
    share = (3 * width) // blocks
    split = 2 * 16 * width // LANES
    n2 = half * blocks
    small, keep2, send2 = call(
        weight_kernel, (ids, small1, grad_a, grad_b, x),
        [bare, shape((n2, share, lanes), F32), shape((n2 + 1, share, lanes), BF)],
        [sems(20), v16(rows, 3 * width), v16(rows, width), v32(n2, share, lanes), v16(n2, share, lanes), v32(width, 3 * width),
         v16(split, LANES)],
        scalars=1, ins_any=3, outs_any=2, us=C["weight"], deps=(y_own,), limit=60,
    )
    n = n // 2
    keep1, send1 = call(
        functools.partial(halve_kernel, low_half), (keep1, got_y), [blocks_of(n, keep1, F32), blocks_of(n, keep1, BF)],
        deps=(small,), us=C["halve"],
    )
    got_x = across("tensor", 2, send1)
    gxs = call(
        last_kernel, (ids, arow, grad_a, grad_b, gh, *wa4), [shape((rows, width), BF)],
        [sems(40), v16(rows, 3 * width), v32(rows, width), v16(width, 3 * width), hot, v16(rows, width), v16(rows, width)],
        scalars=1, ins_any=7, outs_any=1, us=C["last"], deps=(keep1,), limit=60,
    )[0]
    arr_gx = exchange(gxs)
    got = across("tensor", 1, send2)
    n2 = n2 // 2
    keep2, small, send2 = call(
        functools.partial(halve_small_kernel, lambda b: b < blocks), (keep2, small, got),
        [blocks_of(n2, keep2, F32), bare, blocks_of(n2 + 1, keep2, BF)], deps=(gxs,), us=C["part"],
    )
    got = across("tensor", 2, send2)
    own1, *parts1 = call(
        part_kernel, (keep1, got_x), [shape(keep1.shape[1:], F32)] + [shape(keep1.shape[1:], BF)] * (blocks // 2 - 1),
        deps=(keep2, y_far), us=C["part"],
    )
    got1 = [across("dp", 2 * (j + 1), v) for j, v in enumerate(parts1)]
    y_late = call(lambda *refs: None, (y_far,), [shape((rows, width), BF)], ins_any=1, outs_any=1, aliases={0: 0}, deps=(own1,), us=0.1)[0]
    output = widen(0, y_own, y_core, deps=(own1,))
    shared, small = call(
        whole_small_kernel, (keep2, small, got), [shape((blocks, share + split, lanes), BF), bare], deps=(output,), us=C["part"],
    )
    ranks = None if groups == blocks else [list(range(g, g + blocks)) for g in range(0, groups, blocks)]
    shared = lax.all_to_all(shared, "dp", 0, 0, tiled=True, axis_index_groups=ranks)
    gx_own = settle(arr_gx, (small, y_late))
    gx_far = across("tensor", 2, gx_own)
    gx_core = across("tensor", 1, gx_own)
    y_both = across("tensor", 1, y_late)
    own1 = call(sum_kernel, (own1, *got1), [shape(own1.shape, F32)], deps=(gx_own,), us=C["part"])[0]
    output = widen(2, y_late, y_both, output, deps=(own1,))
    gx_grad = widen(0, gx_own, gx_core, deps=(output,))
    kind = BF if groups <= blocks else F32
    own, small = call(
        pack_kernel, (own1, shared), [shape((bundle + share // 4, width), kind), bare], deps=(gx_grad,), us=C["halve"]
    )
    bit = blocks
    while bit < groups:
        kind = BF if 2 * bit == groups else F32
        own, small = call(
            add_one_kernel, (own, across("dp", bit, own), small, across("dp", bit, small)), [shape(own.shape, kind), bare]
        )
        bit *= 2
    gathered = gather(own)
    gx_far = relay(gx_far, (gathered[blocks - 2],))
    gx_both = across("tensor", 1, gx_far)
    qkv_grad, qv_grad, out_grad, ob_grad, up_grad, ub_grad, down_grad, db_grad, alphas = call(
        functools.partial(spread_kernel, blocks), (ids, small, *gathered),
        [shape((3, width, lanes), F32), shape((2, lanes), F32), shape((lanes, width), F32), shape((1, width), F32),
         shape((width, units), F32), shape((1, units), F32), shape((units, width), F32), shape((1, width), F32), shape((8, LANES), F32)],
        [v32(width, units), v32(share, lanes)], scalars=1, us=C["spread"],
    )
    input_grad = widen(2, gx_far, gx_both, gx_grad, deps=())
    return (
        output, input_grad, qkv_grad, qv_grad, out_grad, ob_grad[0], up_grad, ub_grad[0], down_grad, db_grad[0], alphas[0:2, 0],
    )


def solution(mesh):
    in_specs = (
        P(None, "dp", None), P(None, "dp", None), P(), P(None, "dp", None),
        P(None, None, "tensor"), P(None, "tensor"), P("tensor", None), P(),
        P(None, "tensor"), P("tensor"), P("tensor", None), P(), P(),
    )
    out_specs = (
        P(None, "dp", None), P(None, "dp", None), P(None, None, "tensor"), P(None, "tensor"),
        P("tensor", None), P(), P(None, "tensor"), P("tensor"), P("tensor", None), P(), P(),
    )
    return jax.shard_map(per_device, mesh=mesh, in_specs=in_specs, out_specs=out_specs, check_vma=False)
```

```python
import functools

import jax
import jax.numpy as jnp
from jax import lax
from jax.experimental import pallas as pl
from jax.experimental.pallas import tpu as pltpu
from jax.sharding import PartitionSpec as P

HEAD_SIZE = 64
LANES = 128
QT = 256
FT = 256
SLAB = 16
BF = jnp.bfloat16
F32 = jnp.float32
C = {"route": 6, "attend": 19, "forward": 5, "feed": 19, "back": 11, "halve": 1, "part": 5, "settle": 1, "last": 20, "weight": 0.2, "widen": 5, "spread": 3}
I32 = jnp.int32
NEG = -1e30
VMEM_LIMIT = 56 * 1024 * 1024
GELU_A = 0.7978845608028654
GELU_B = 0.044715

NN = (((1,), (0,)), ((), ()))
NT = (((1,), (1,)), ((), ()))
TN = (((0,), (0,)), ((), ()))


def dot(a, b, dims=NN):
    return lax.dot_general(a, b, dims, preferred_element_type=F32)


def iota(shape, dim):
    return lax.broadcasted_iota(I32, shape, dim)


def params(limit=VMEM_LIMIT):
    return pltpu.CompilerParams(vmem_limit_bytes=limit)


def cost(flops, nbytes, trans=0):
    return pl.CostEstimate(flops=int(flops), bytes_accessed=int(nbytes), transcendentals=int(trans))


def vmem(n):
    return [pl.BlockSpec(memory_space=pltpu.VMEM)] * n


def smem():
    return pl.BlockSpec(memory_space=pltpu.SMEM)


def one_hot_rows(row, count):
    return (iota((count, row.shape[1]), 0) == row).astype(F32).astype(BF)


def one_hot_cols(col, count):
    return (iota((col.shape[0], count), 1) == col).astype(F32).astype(BF)


def route_kernel(groups, ids_ref, src_ref, x_ref, xs_ref, srow_ref, scol_ref, hot_ref):
    me, micro = ids_ref[0], ids_ref[1]
    rows = x_ref.shape[1]
    chunks = rows // LANES
    share = rows // groups
    sub_hi = iota((chunks, rows), 0)
    sub_lo = iota((LANES, rows), 0)

    def gather_group(g, total):
        value = src_ref[pl.ds(micro, 1), pl.ds(pl.multiple_of(g * rows, LANES), rows)] - me * rows
        inside = (value >= 0) & (value < rows)
        high = jnp.where(inside, value // LANES, -1)
        low = jnp.where(inside, value % LANES, -1)
        hot_high = jnp.where(high == sub_hi, (g + 1).astype(F32), 0.0).astype(BF)
        hot_low = (low == sub_lo).astype(F32).astype(BF)
        return total + dot(hot_high, hot_low, NT)

    dest = lax.fori_loop(0, groups, gather_group, jnp.zeros((chunks, LANES), F32)).astype(I32) - 1
    before = (iota((LANES, LANES), 0) < iota((LANES, LANES), 1)).astype(F32).astype(BF)
    width = max(groups, 8)
    carry = jnp.zeros((width, 1), F32)
    for c in range(chunks):
        g_row = dest[c : c + 1, :]
        hot = (iota((width, LANES), 0) == g_row).astype(F32)
        ranks = dot(hot.astype(BF), before) + carry
        carry = carry + jnp.sum(hot, axis=1, keepdims=True)
        place = g_row * share + jnp.sum(hot * ranks, axis=0, keepdims=True).astype(I32)
        srow_ref[c : c + 1, :] = place
        spread = jnp.broadcast_to(place.astype(F32), (LANES, LANES))
        scol_ref[c * LANES : (c + 1) * LANES, :] = spread.T.astype(I32)
        hot_ref[:, c * LANES : (c + 1) * LANES] = one_hot_rows(place, rows)
    xs_ref[...] = dot(hot_ref[...], x_ref[0]).astype(BF)


def second_kernel(ids_ref, src_ref, g_ref, srow_ref, gs_ref, arow_ref, acol_ref, hot_ref):
    me, micro = ids_ref[0], ids_ref[1]
    rows = g_ref.shape[1]
    for c in range(rows // LANES):
        hot_ref[:, c * LANES : (c + 1) * LANES] = one_hot_rows(srow_ref[c : c + 1, :], rows)
    gs_ref[...] = dot(hot_ref[...], g_ref[0]).astype(BF)
    own = src_ref[pl.ds(micro, 1), pl.ds(pl.multiple_of(me * rows, LANES), rows)].astype(F32)
    for c in range(rows // LANES):
        piece = own[:, c * LANES : (c + 1) * LANES]
        column = jnp.broadcast_to(piece, (LANES, LANES)).T[:, 0:1]
        count = jnp.sum((own < column).astype(F32), axis=1, keepdims=True)
        spread = jnp.broadcast_to(count, (LANES, LANES))
        acol_ref[c * LANES : (c + 1) * LANES, :] = spread.astype(I32)
        arow_ref[0:1, c * LANES : (c + 1) * LANES] = spread.T[0:1, :].astype(I32)


def starts_of(len_ref, index):
    start = jnp.zeros_like(index)
    first = jnp.int32(0)
    for j in range(len_ref.shape[0] - 1):
        first = first + len_ref[j]
        start = jnp.where(index >= first, first, start)
    return start


class Copies:
    def __init__(self, sems):
        self.sems, self.used, self.left = sems, 0, []

    def start(self, source, target):
        copy = pltpu.make_async_copy(source, target, self.sems.at[self.used])
        self.used += 1
        copy.start()
        return copy

    def send(self, source, target):
        self.left.append(self.start(source, target))

    def finish(self):
        for copy in self.left:
            copy.wait()


def wait_all(copies):
    for copy in copies:
        copy.wait()


def attend_kernel(
    ids_ref, len_ref, alpha_ref, b0_ref, b1_ref, b2_ref, b3_ref, ob_ref, acol_ref,
    arr_any, wa0_any, wa1_any, wa2_any, wa3_any, wo0_any, wo1_any, wo2_any, wo3_any,
    l_ref, x_any, q_any, k_any, v_any, o_any, h_any, low_any, attn_any,
    sems, arr_ref, wcat_ref, wo_ref, bias_ref, hot_ref, x_ref, q_ref, k_ref, v_ref, ob16_ref, h_ref, low_ref, attn_ref,
):
    rows, width = arr_ref.shape
    lanes = wo0_any.shape[0]
    pieces = width // lanes
    heads = lanes // HEAD_SIZE
    tensor = ids_ref[1]
    copies = Copies(sems)
    first = copies.start(arr_any, arr_ref)
    weights, later = [], []
    for j, (wa, wo, b) in enumerate(
        ((wa0_any, wo0_any, b0_ref), (wa1_any, wo1_any, b1_ref), (wa2_any, wo2_any, b2_ref), (wa3_any, wo3_any, b3_ref))
    ):
        place = pl.multiple_of(lax.bitwise_xor(tensor, j) * lanes, LANES)
        for c in range(3):
            weights.append(copies.start(wa.at[c], wcat_ref.at[:, pl.ds(c * width + place, lanes)]))
        later.append(copies.start(wo, wo_ref.at[pl.ds(place, lanes), :]))
        bias_ref[:, pl.ds(place, lanes)] = b[...].astype(F32)
    hot_ref[...] = one_hot_cols(acol_ref[:, 0:1], rows)
    first.wait()
    x_ref[...] = dot(hot_ref[...], arr_ref[...]).astype(BF)
    copies.send(x_ref, x_any)
    wait_all(weights)
    q_ref[...] = (dot(x_ref[...], wcat_ref[:, 0:width]) + bias_ref[0:1, :]).astype(BF) * jnp.asarray(HEAD_SIZE**-0.5, BF)
    k_ref[...] = dot(x_ref[...], wcat_ref[:, width : 2 * width]).astype(BF)
    v_ref[...] = (dot(x_ref[...], wcat_ref[:, 2 * width :]) + bias_ref[1:2, :]).astype(BF)
    copies.send(q_ref, q_any)
    copies.send(k_ref, k_any)
    copies.send(v_ref, v_any)
    tiles = rows // QT
    lane = iota((QT, lanes), 1) // HEAD_SIZE
    masks = []
    for i in range(tiles):
        q_index = i * QT + iota((QT, 1), 0)
        k_index = iota((QT, (i + 1) * QT), 1)
        masks.append((k_index >= starts_of(len_ref, q_index)) & (k_index <= q_index))

    def scores_of(p, i, e):
        q = q_ref[i * QT : (i + 1) * QT, p * lanes : (p + 1) * lanes]
        return dot(jnp.where(lane == e, q, jnp.zeros_like(q)), k_ref[0 : (i + 1) * QT, p * lanes : (p + 1) * lanes], NT)

    items = [(p, i, e) for i in range(tiles) for p in range(pieces) for e in range(heads)]
    ahead = scores_of(*items[0])
    mixed = logs = None
    for step, (p, i, e) in enumerate(items):
        now = ahead
        if step + 1 < len(items):
            ahead = scores_of(*items[step + 1])
        scores = jnp.where(masks[i], now, NEG)
        top = jnp.max(scores, axis=1, keepdims=True)
        weights = jnp.exp(scores - top)
        total = jnp.sum(weights, axis=1, keepdims=True)
        low = (weights * (1.0 / total)).astype(BF)
        out = dot(low, v_ref[0 : (i + 1) * QT, p * lanes : (p + 1) * lanes])
        head = p * heads + e
        log_total = top + jnp.log(total)
        logs = jnp.where(iota((QT, LANES), 1) == head, log_total, 0.0 if head == 0 else logs)
        mixed = out if e == 0 else jnp.where(lane == e, out, mixed)
        if e == heads - 1:
            ob16_ref[i * QT : (i + 1) * QT, p * lanes : (p + 1) * lanes] = mixed.astype(BF)
        if head == pieces * heads - 1:
            l_ref[:, i * QT : (i + 1) * QT] = logs.T[0 : pieces * heads, :]
            if i == 0:
                wait_all(later)
            span = slice(i * QT, (i + 1) * QT)
            copies.send(ob16_ref.at[span], o_any.at[span])
            attn = dot(ob16_ref[span, :], wo_ref[...]) + ob_ref[...].astype(F32)
            hidden = x_ref[span, :].astype(F32) + alpha_ref[0] * attn
            attn_ref[span, :] = attn
            h_ref[span, :] = hidden
            low_ref[span, :] = hidden.astype(BF)
            copies.send(attn_ref.at[span], attn_any.at[span])
            copies.send(h_ref.at[span], h_any.at[span])
            copies.send(low_ref.at[span], low_any.at[span])
    copies.finish()


def unit_biases(refs, units):
    biases = []
    for b in refs:
        tail = b[...].astype(F32)
        biases.append(jnp.concatenate([tail[2 + n : 3 + n, :] for n in range(units // LANES)], axis=1))
    return biases


def rise_of(z):
    square = z * z
    return 0.5 + 0.5 * jnp.tanh(z * (GELU_A + (GELU_A * GELU_B) * square)), square


def forward_kernel(
    alpha_ref, b0_ref, b1_ref, b2_ref, b3_ref, db_ref, arow_ref,
    low_any, h_any, wu0_any, wu1_any, wu2_any, wu3_any, wd0_any, wd1_any, wd2_any, wd3_any,
    ys_any, f_any,
    sems, low_ref, h_ref, wu_ref, wd_ref, act_ref, f_ref, y_ref, hot_ref, ys_ref,
):
    rows, width = low_ref.shape
    units = wu0_any.shape[1]
    copies = Copies(sems)
    first = copies.start(low_any, low_ref)
    up, down = [], []
    for j, wu in enumerate((wu0_any, wu1_any, wu2_any, wu3_any)):
        up.append(copies.start(wu, wu_ref.at[:, j * units : (j + 1) * units]))
    for j, wd in enumerate((wd0_any, wd1_any, wd2_any, wd3_any)):
        down.append(copies.start(wd, wd_ref.at[j * units : (j + 1) * units, :]))
    hidden = copies.start(h_any, h_ref)
    biases = unit_biases((b0_ref, b1_ref, b2_ref, b3_ref), units)
    first.wait()
    items = [(j, m) for j in range(len(biases)) for m in range(rows // FT)]

    def z_of(j, m):
        if m == 0:
            up[j].wait()
        return dot(low_ref[m * FT : (m + 1) * FT, :], wu_ref[:, j * units : (j + 1) * units])

    ahead = z_of(*items[0])
    for step, (j, m) in enumerate(items):
        now = ahead
        if step + 1 < len(items):
            ahead = z_of(*items[step + 1])
        for n in range(FT // SLAB):
            z = now[n * SLAB : (n + 1) * SLAB] + biases[j]
            rise, _ = rise_of(z)
            act_ref[m * FT + n * SLAB : m * FT + (n + 1) * SLAB, j * units : (j + 1) * units] = (z * rise).astype(BF)
    wait_all(down)
    hidden.wait()
    for m in range(rows // FT):
        span = slice(m * FT, (m + 1) * FT)
        branch = dot(act_ref[span, :], wd_ref[...]) + db_ref[...].astype(F32)
        f_ref[span, :] = branch
        copies.send(f_ref.at[span], f_any.at[span])
        y_ref[span, :] = (h_ref[span, :] + alpha_ref[1] * branch).astype(BF)
        hot_ref[span, :] = (iota((FT, rows), 0) + m * FT == arow_ref[0:1, :]).astype(F32).astype(BF)
    for m in range(rows // FT):
        span = slice(m * FT, (m + 1) * FT)
        ys_ref[span, :] = dot(hot_ref[span, :], y_ref[...]).astype(BF)
        copies.send(ys_ref.at[span], ys_any.at[span])
    copies.finish()


def feed_kernel(
    ids_ref, alpha_ref, b0_ref, b1_ref, b2_ref, b3_ref, acol_ref,
    arr_any, wu0_any, wu1_any, wu2_any, wu3_any, wd0_any, wd1_any, wd2_any, wd3_any,
    wo0_any, wo1_any, wo2_any, wo3_any, low_any, f_any, attn_any, o_any,
    small_ref, go_any, gh_any, keep_any, send_any,
    sems, arr_ref, wu_ref, wd_ref, wo_ref, act_ref, low_ref, f_ref, attn_ref, o_ref,
    hot_ref, g_ref, gf_ref, gz_ref, gh_ref, ga_ref, go_ref, keep_ref, part_ref, w_ref,
):
    me, tensor = ids_ref[0], ids_ref[1]
    rows, width = low_ref.shape
    units = wu0_any.shape[1]
    lanes = wo0_any.shape[0]
    blocks = part_ref.shape[1]
    own = me % blocks
    copies = Copies(sems)
    first = copies.start(arr_any, arr_ref)
    lowed = copies.start(low_any, low_ref)
    down, up, later = [], [], []
    for j, (wu, wd) in enumerate(
        ((wu0_any, wd0_any), (wu1_any, wd1_any), (wu2_any, wd2_any), (wu3_any, wd3_any))
    ):
        span = slice(j * units, (j + 1) * units)
        up.append(copies.start(wu, wu_ref.at[:, span]))
        down.append(copies.start(wd, wd_ref.at[span, :]))
    for j, wo in enumerate((wo0_any, wo1_any, wo2_any, wo3_any)):
        place = pl.multiple_of(lax.bitwise_xor(tensor, j) * lanes, LANES)
        later.append(copies.start(wo, wo_ref.at[pl.ds(place, lanes), :]))
    later.append(copies.start(attn_any, attn_ref))
    later.append(copies.start(o_any, o_ref))
    branched = copies.start(f_any, f_ref)
    hot_ref[...] = one_hot_cols(acol_ref[:, 0:1], rows)
    first.wait()
    for m in range(rows // FT):
        span = slice(m * FT, (m + 1) * FT)
        grad = dot(hot_ref[span, :], arr_ref[...])
        g_ref[span, :] = grad.astype(BF)
        gf_ref[span, :] = (alpha_ref[1] * grad).astype(BF)
    items = [(j, m) for j in range(len(up)) for m in range(rows // FT)]

    biases = unit_biases((b0_ref, b1_ref, b2_ref, b3_ref), units)
    lowed.wait()

    def both_of(j, m):
        if m == 0:
            up[j].wait()
            down[j].wait()
        span, unit = slice(m * FT, (m + 1) * FT), slice(j * units, (j + 1) * units)
        return dot(low_ref[span, :], wu_ref[:, unit]), dot(gf_ref[span, :], wd_ref[unit, :], NT)

    ahead = both_of(*items[0])
    for step, (j, m) in enumerate(items):
        now = ahead
        if step + 1 < len(items):
            ahead = both_of(*items[step + 1])
        for n in range(FT // SLAB):
            slab = slice(n * SLAB, (n + 1) * SLAB)
            z = now[0][slab] + biases[j]
            rise, square = rise_of(z)
            slope = rise + z * (rise - rise * rise) * ((2 * GELU_A) + (6 * GELU_A * GELU_B) * square)
            span = (slice(m * FT + n * SLAB, m * FT + (n + 1) * SLAB), slice(j * units, (j + 1) * units))
            act_ref[span] = (z * rise).astype(BF)
            gz_ref[span] = (now[1][slab] * slope).astype(BF)
    wait_all(later)
    gh_sum = attn_sum = jnp.zeros((1, width), F32)
    for m in range(rows // FT):
        span = slice(m * FT, (m + 1) * FT)
        grad_hidden = g_ref[span, :].astype(F32) + dot(gz_ref[span, :], wu_ref[...], NT)
        gh_ref[span, :] = grad_hidden
        copies.send(gh_ref.at[span], gh_any.at[span])
        ga = (alpha_ref[0] * grad_hidden).astype(BF)
        ga_ref[span, :] = ga
        gh_sum = gh_sum + jnp.sum(ga.astype(F32), axis=0, keepdims=True)
        attn_sum = attn_sum + jnp.sum(grad_hidden * attn_ref[span, :], axis=0, keepdims=True)
    for m in range(rows // FT):
        span = slice(m * FT, (m + 1) * FT)
        go = dot(ga_ref[span, :], wo_ref[...], NT).astype(BF)
        go_ref[span, :] = go
        copies.send(go_ref.at[span], go_any.at[span])

    def place(j, first_row, value):
        count = value.shape[0] // blocks
        out = keep_ref if j % 2 == 0 else part_ref
        for b in range(blocks):
            out[j // 2, lax.bitwise_xor(own, b), first_row : first_row + count, :] = value[b * count : (b + 1) * count].astype(out.dtype)

    low_t = low_ref[...].T
    gf_t = gf_ref[...].T
    o_t = o_ref[...].T
    w_ref[...] = dot(o_t, ga_ref[...])
    edge = (width + units) // blocks
    for j in range(len(up)):
        span = slice(j * units, (j + 1) * units)
        place(j, 0, dot(low_t, gz_ref[:, span]))
        place(j, width // blocks, dot(gf_t, act_ref[:, span]))
        at = pl.multiple_of(lax.bitwise_xor(tensor, j) * lanes, LANES)
        place(j, edge, w_ref[pl.ds(at, lanes), :])
        held, out = (keep_ref, keep_any) if j % 2 == 0 else (part_ref, send_any)
        copies.send(held.at[j // 2], out.at[j // 2])
        small_ref[pl.ds(lax.bitwise_xor(tensor, j), 1), :] = jnp.sum(gz_ref[:, span].astype(F32), axis=0, keepdims=True)
    branched.wait()
    small_ref[4:5, :] = gh_sum
    small_ref[5:6, :] = jnp.sum(gf_ref[...].astype(F32), axis=0, keepdims=True)
    small_ref[6:7, :] = attn_sum
    small_ref[7:8, :] = jnp.sum(g_ref[...].astype(F32) * f_ref[...], axis=0, keepdims=True)
    copies.finish()


def starts_of(len_ref, index):
    start = jnp.zeros_like(index)
    first = jnp.int32(0)
    for j in range(len_ref.shape[0] - 1):
        first = first + len_ref[j]
        start = jnp.where(index >= first, first, start)
    return start


def back_kernel(
    first_pair, len_ref, l_ref, q_any, k_any, v_any, go_any,
    grad_any,
    sems, q_ref, k_ref, v_ref, go_ref, grad_ref, gk_ref, gv_ref,
):
    rows, width = q_ref.shape
    lanes = 2 * HEAD_SIZE
    heads = 2
    pairs = width // lanes
    scale = HEAD_SIZE**-0.5
    copies = Copies(sems)
    columns = slice(first_pair * lanes, first_pair * lanes + width)
    ins = [copies.start(a.at[:, columns], r) for a, r in ((q_any, q_ref), (k_any, k_ref), (v_any, v_ref), (go_any, go_ref))]
    tiles = rows // QT
    lane = iota((QT, lanes), 1) // HEAD_SIZE
    masks = []
    for i in range(tiles):
        q_index = i * QT + iota((1, QT), 1)
        k_index = iota(((i + 1) * QT, QT), 0)
        masks.append((k_index >= starts_of(len_ref, q_index)) & (k_index <= q_index))
    wait_all(ins)
    items = [(p, i, e) for p in range(pairs) for i in reversed(range(tiles)) for e in range(heads)]

    def pick(ref, p, i, e):
        value = ref[i * QT : (i + 1) * QT, p * lanes : (p + 1) * lanes]
        return jnp.where(lane == e, value, jnp.zeros_like(value))

    def both_of(p, i, e):
        pair = (slice(0, (i + 1) * QT), slice(p * lanes, (p + 1) * lanes))
        return dot(k_ref[pair], pick(q_ref, p, i, e), NT), dot(v_ref[pair], pick(go_ref, p, i, e), NT)

    ahead = both_of(*items[0])
    gq = None
    for step, (p, i, e) in enumerate(items):
        scores, grad_weights = ahead
        if step + 1 < len(items):
            ahead = both_of(*items[step + 1])
        head = (first_pair + p) * heads + e
        n = (i + 1) * QT
        weights = jnp.exp(jnp.where(masks[i], scores - l_ref[head : head + 1, i * QT : n], NEG))
        inner = jnp.sum(weights * grad_weights, axis=0, keepdims=True)
        grad_scores = (weights * (grad_weights - inner)).astype(BF)
        gv = dot(weights.astype(BF), pick(go_ref, p, i, e))
        gk = dot(grad_scores, pick(q_ref, p, i, e))
        if i == tiles - 1 and e == 0:
            gv_ref[...] = gv
            gk_ref[...] = gk
        else:
            gv_ref[0:n, :] += gv
            gk_ref[0:n, :] += gk
        gq_e = dot(grad_scores, k_ref[0:n, p * lanes : (p + 1) * lanes], TN)
        gq = gq_e if e == 0 else jnp.where(lane == e, gq_e, gq)
        if e == heads - 1:
            span = (slice(i * QT, n), slice(p * lanes, (p + 1) * lanes))
            grad_ref[(0, *span)] = (gq * scale).astype(BF)
            grad_ref[(1, *span)] = gk_ref[i * QT : n, :].astype(BF)
            grad_ref[(2, *span)] = gv_ref[i * QT : n, :].astype(BF)
            if i == 0:
                copies.send(grad_ref.at[:, :, p * lanes : (p + 1) * lanes], grad_any.at[:, :, p * lanes : (p + 1) * lanes])
    copies.finish()


def split_small(value, out_ref):
    chunks = value.shape[1] // LANES
    for c in range(chunks):
        left = value[:, c * LANES : (c + 1) * LANES]
        for k in range(2):
            term = left.astype(BF)
            first = (k * chunks + c) * 16
            out_ref[first : first + 16, :] = term
            left = left - term.astype(F32)


def join_small(ref, width):
    chunks = width // LANES
    parts = []
    for c in range(chunks):
        terms = [ref[(k * chunks + c) * 16 : (k * chunks + c + 1) * 16, :].astype(F32) for k in range(2)]
        parts.append(terms[0] + terms[1])
    return jnp.concatenate(parts, axis=1)


def last_kernel(
    ids_ref, arow_ref, grad_a_any, grad_b_any, gh_any, wa0_any, wa1_any, wa2_any, wa3_any,
    gxs_any,
    sems, grad_ref, gh_ref, wcat_ref, hot_ref, gx_ref, gxs_ref,
):
    tensor = ids_ref[1]
    rows, width = gx_ref.shape
    lanes = wa0_any.shape[2]
    half = width // 2
    copies = Copies(sems)
    grads, weights = [], []
    for c in range(3):
        for n, g in enumerate((grad_a_any, grad_b_any)):
            grads.append(copies.start(g.at[c], grad_ref.at[:, c * width + n * half : c * width + (n + 1) * half]))
    for j, wa in enumerate((wa0_any, wa1_any, wa2_any, wa3_any)):
        place = pl.multiple_of(lax.bitwise_xor(tensor, j) * lanes, LANES)
        for c in range(3):
            weights.append(copies.start(wa.at[c], wcat_ref.at[:, pl.ds(c * width + place, lanes)]))
    hidden = copies.start(gh_any, gh_ref)
    for m in range(rows // FT):
        hot_ref[m * FT : (m + 1) * FT, :] = (iota((FT, rows), 0) + m * FT == arow_ref[0:1, :]).astype(F32).astype(BF)
    wait_all(grads)
    wait_all(weights)
    hidden.wait()
    for m in range(rows // FT):
        span = slice(m * FT, (m + 1) * FT)
        gx_ref[span, :] = (gh_ref[span, :] + dot(grad_ref[span, :], wcat_ref[...], NT)).astype(BF)
    for m in range(rows // FT):
        span = slice(m * FT, (m + 1) * FT)
        gxs_ref[span, :] = dot(hot_ref[span, :], gx_ref[...]).astype(BF)
        copies.send(gxs_ref.at[span], gxs_any.at[span])
    copies.finish()


def weight_kernel(
    ids_ref, small1_ref, grad_a_any, grad_b_any, x_any,
    small_ref, keep_any, send_any,
    sems, grad_ref, x_ref, keep_ref, part_ref, w_ref, split_ref,
):
    tensor = ids_ref[1]
    rows, width = x_ref.shape
    lanes = keep_ref.shape[2]
    half = width // 2
    blocks = keep_ref.shape[0] // 2
    copies = Copies(sems)
    xs = copies.start(x_any, x_ref)
    grads = [
        [
            copies.start(g.at[c], grad_ref.at[:, c * width + n * half : c * width + (n + 1) * half])
            for n, g in enumerate((grad_a_any, grad_b_any))
        ]
        for c in range(3)
    ]
    xs.wait()
    x_t = x_ref[...].T
    count = width // blocks
    small_ref[0:8, :] = small1_ref[...]
    small_ref[8:16, :] = jnp.zeros((8, width), F32)
    for c in range(3):
        wait_all(grads[c])
        span = slice(c * width, (c + 1) * width)
        w_ref[:, span] = dot(x_t, grad_ref[:, span])
        if c != 1:
            row = 8 + c // 2
            small_ref[row : row + 1, :] = jnp.sum(grad_ref[:, span].astype(F32), axis=0, keepdims=True)
    for j in range(width // lanes):
        at = pl.multiple_of(lax.bitwise_xor(tensor, j) * lanes, LANES)
        held, out = (keep_ref, keep_any) if j % 2 == 0 else (part_ref, send_any)
        first = j // 2 * blocks
        for c in range(3):
            for b in range(blocks):
                held[first + b, c * count : (c + 1) * count, :] = w_ref[
                    b * count : (b + 1) * count, pl.ds(c * width + at, lanes)
                ].astype(held.dtype)
        copies.send(held.at[pl.ds(first, blocks)], out.at[pl.ds(first, blocks)])
    split_small(small_ref[...], split_ref)
    copies.send(split_ref, send_any.at[send_any.shape[0] - 1, 0 : split_ref.shape[0]])
    copies.finish()


def halve_kernel(pick, keep_ref, got_ref, next_ref, send_ref):
    here = there = 0
    for b in range(keep_ref.shape[0]):
        total = keep_ref[b] + got_ref[b].astype(F32)
        if pick(b):
            next_ref[here] = total
            here += 1
        else:
            send_ref[there] = total.astype(BF)
            there += 1


def halve_small_kernel(pick, keep_ref, small_ref, got_ref, next_ref, total_ref, send_ref):
    halve_kernel(pick, keep_ref, got_ref, next_ref, send_ref)
    total = small_ref[...] + join_small(got_ref.at[got_ref.shape[0] - 1], small_ref.shape[1])
    total_ref[...] = total
    split_small(total, send_ref.at[send_ref.shape[0] - 1])


def part_kernel(keep_ref, got_ref, *outs):
    for b in range(keep_ref.shape[0]):
        outs[b][...] = (keep_ref[b] + got_ref[b].astype(F32)).astype(outs[b].dtype)


def whole_small_kernel(keep_ref, small_ref, got_ref, send_ref, total_ref):
    rows = keep_ref.shape[1]
    total = small_ref[...] + join_small(got_ref.at[got_ref.shape[0] - 1], small_ref.shape[1])
    total_ref[...] = total
    for b in range(keep_ref.shape[0]):
        send_ref[b, 0:rows, :] = (keep_ref[b] + got_ref[b].astype(F32)).astype(BF)
        if b == 0:
            split_small(total, send_ref.at[0, rows:])
        else:
            send_ref[b, rows:, :] = send_ref[0, rows:, :]


def sum_kernel(own_ref, a_ref, b_ref, c_ref, out_ref):
    total = own_ref[...] + a_ref[...].astype(F32) + b_ref[...].astype(F32) + c_ref[...].astype(F32)
    out_ref[...] = total.astype(out_ref.dtype)


def add_kernel(a_ref, b_ref, out_ref):
    out_ref[...] = (a_ref[...].astype(F32) + b_ref[...].astype(F32)).astype(out_ref.dtype)


def pack_kernel(got_ref, packed_ref, total_ref):
    ways = packed_ref.shape[2] // got_ref.shape[2]
    rows, lanes = got_ref.shape[1] - 2 * 16 * ways, got_ref.shape[2]
    value = total = 0.0
    for b in range(got_ref.shape[0]):
        value = value + got_ref[b, 0:rows, :].astype(F32)
        total = total + join_small(got_ref.at[b, rows:], total_ref.shape[1])
    total_ref[...] = total
    for c in range(ways):
        part = value[c * (rows // ways) : (c + 1) * (rows // ways)].astype(packed_ref.dtype)
        for b in range(packed_ref.shape[0]):
            packed_ref[b, :, c * lanes : (c + 1) * lanes] = part


def add_one_kernel(a_ref, b_ref, small_ref, other_ref, out_ref, total_ref):
    out_ref[...] = (a_ref[...].astype(F32) + b_ref[...].astype(F32)).astype(out_ref.dtype)
    total_ref[...] = small_ref[...] + other_ref[...]


def spread_kernel(count, ids_ref, small_ref, *refs):
    firsts, seconds = refs[:count], refs[count]
    qkv_ref, qv_ref, out_ref, ob_ref, up_ref, ub_ref, down_ref, db_ref, alpha_ref, turned_ref, second_ref = refs[count + 1 :]
    me, tensor = ids_ref[0], ids_ref[1]
    lanes = out_ref.shape[0]
    for j in range(count):
        slot = lax.bitwise_xor(me % count, j)
        first = 0
        for out in (up_ref, turned_ref, out_ref):
            size = out.shape[0] // count
            out[pl.ds(pl.multiple_of(slot * size, 8), size), :] = firsts[j][first : first + size, :].astype(F32)
            first += size
        size = qkv_ref.shape[1] // count
        rest = seconds.shape[1]
        for c in range(seconds.shape[2] // lanes):
            second_ref[c * rest : (c + 1) * rest, :] = seconds[j, :, c * lanes : (c + 1) * lanes].astype(F32)
        for c in range(3):
            qkv_ref[c, j * size : (j + 1) * size, :] = second_ref[c * size : (c + 1) * size, :]
    down_ref[...] = turned_ref[...].T
    ub_ref[...] = small_ref[pl.ds(tensor, 1), :]
    ob_ref[...] = small_ref[4:5, :]
    db_ref[...] = small_ref[5:6, :]
    qv_ref[...] = small_ref[8:10, pl.ds(pl.multiple_of(tensor * lanes, LANES), lanes)]
    sums = jnp.sum(small_ref[6:8, :], axis=1, keepdims=True)
    spread = jnp.concatenate([sums, jnp.zeros((6, 1), F32)], axis=0)
    alpha_ref[...] = jnp.broadcast_to(spread, (8, LANES))


def widen_kernel(first, ids_ref, a_any, b_any, *refs):
    out_any, sems, wide_ref, low_ref = refs[-4:]
    rows = low_ref.shape[1]
    copies = Copies(sems)
    ins = [copies.start(a, low_ref.at[n]) for n, a in enumerate((a_any, b_any))]
    half = rows // 2
    for n in range(2):
        ins[n].wait()
        slot = lax.bitwise_xor(ids_ref[1], first + n)
        for m in range(2):
            span = slice(m * half, (m + 1) * half)
            wide_ref[n, span, :] = low_ref[n, span, :].astype(F32)
            copies.send(wide_ref.at[n, span], out_any.at[slot, span])
    copies.finish()


def settle_kernel(r_ref, scol_ref, out_ref):
    out_ref[...] = dot(one_hot_cols(scol_ref[:, 0:1], r_ref.shape[0]), r_ref[...]).astype(BF)


def shape(dims, kind):
    return jax.ShapeDtypeStruct(dims, kind)


marks = {}


def call(kernel, ins, outs, scratch=(), deps=(), us=1.0, scalars=0, ins_any=0, outs_any=0, limit=24, aliases=None):
    n_in, n_out = len(ins), len(outs)
    whole = pl.BlockSpec(memory_space=pl.ANY)
    held = pl.BlockSpec(memory_space=pltpu.HBM)
    before = [marks.get(id(d), (d, d))[1] for d in deps]

    def body(*refs):
        skip = n_in + len(before)
        kernel(*refs[:n_in], *refs[skip : skip + n_out], *refs[skip + n_out + 1 :])

    made = pl.pallas_call(
        body,
        out_shape=[*outs, shape((8, LANES), F32)],
        in_specs=[smem()] * scalars + vmem(n_in - scalars - ins_any) + [whole] * (ins_any - len(aliases or ())) + [held] * len(aliases or ()) + [held if id(d) in marks else whole for d in deps],
        out_specs=vmem(n_out - outs_any) + [held] * (outs_any + 1),
        scratch_shapes=list(scratch),
        input_output_aliases=aliases or {},
        compiler_params=params(limit << 20),
        cost_estimate=cost(1e9 * us, 0),
    )(*ins, *before)
    for out in made[:-1]:
        marks[id(out)] = (out, made[-1])
    return made[:-1]


def per_device(
    block_input, cotangent, source, seq_lengths, qkv_weight, qv_bias, out_weight, out_bias,
    up_weight, up_bias, down_weight, down_bias, rezero_alphas,
):
    marks.clear()
    micros, rows, width = block_input.shape
    groups = lax.axis_size("dp")
    tensors = lax.axis_size("tensor")
    lanes = qkv_weight.shape[2]
    units = up_weight.shape[1]
    blocks = min(groups, 8)
    me, tensor = lax.axis_index("dp"), lax.axis_index("tensor")
    ids = jnp.stack([me, tensor]).astype(I32)
    lengths = lax.dynamic_index_in_dim(seq_lengths, tensor, 0, keepdims=False)[0]

    def across(axis, bit, value):
        count = tensors if axis == "tensor" else groups
        return lax.ppermute(value, axis, [(i, i ^ bit) for i in range(count)])

    def after(value, *others):
        return lax.optimization_barrier((value, *others))[0] if others else value

    def by_micro(kernel, n_whole, out_shape, scratch):
        return pl.pallas_call(
            kernel,
            out_shape=out_shape,
            grid_spec=pltpu.PrefetchScalarGridSpec(
                num_scalar_prefetch=1,
                grid=(1,),
                in_specs=[
                    pl.BlockSpec(source.shape, lambda i, s: (0, 0)),
                    pl.BlockSpec((1, rows, width), lambda i, s: (s[1], 0, 0)),
                ]
                + [pl.BlockSpec((rows // LANES, LANES), lambda i, s: (0, 0))] * n_whole,
                out_specs=[pl.BlockSpec(o.shape, lambda i, s: (0, 0)) for o in out_shape],
                scratch_shapes=scratch,
            ),
            compiler_params=params(),
            cost_estimate=cost(1e9 * C["route"], 0),
        )

    hot = pltpu.VMEM((rows, rows), BF)
    xs, srow, scol = by_micro(
        functools.partial(route_kernel, groups), 0,
        [shape((rows, width), BF), shape((rows // LANES, LANES), I32), shape((rows, LANES), I32)], [hot],
    )(ids, source, block_input)

    def exchange(rows_out):
        return lax.all_to_all(rows_out.reshape(groups, rows // groups, width), "dp", 0, 0, tiled=True).reshape(rows, width)

    arr_x = exchange(xs)
    gs, arow, acol = by_micro(
        second_kernel, 1,
        [shape((rows, width), BF), shape((8, rows), I32), shape((rows, LANES), I32)], [hot],
    )(ids, source, cotangent, srow)
    head = jnp.concatenate([qv_bias, up_bias.reshape(units // lanes, lanes), jnp.zeros((2, lanes), BF)], axis=0)
    own = (head, qkv_weight, out_weight, up_weight, down_weight)
    far = [across("tensor", 2, w) for w in own]
    held = lax.optimization_barrier((*far[:3], arow))[:3]

    def four(own, far):
        return own, across("tensor", 1, own), far, across("tensor", 1, far)

    bias4, wa4, wo4 = [four(w, f) for w, f in zip(own, held)]
    arr_g = exchange(gs)

    def v16(*dims):
        return pltpu.VMEM(dims, BF)

    def v32(*dims):
        return pltpu.VMEM(dims, F32)

    def sems(count):
        return pltpu.SemaphoreType.DMA((count,))

    ff = tensors * units
    wide = [shape((rows, width), BF)] * 4
    logs, x, q, k, v, o, h, low, attn = call(
        attend_kernel,
        (ids, lengths, rezero_alphas, *bias4, out_bias.reshape(1, width), acol, arr_x, *wa4, *wo4),
        [shape((2 * tensors, rows), F32), *wide, shape((rows, width), BF), shape((rows, width), F32),
         shape((rows, width), BF), shape((rows, width), F32)],
        [sems(40), v16(rows, width), v16(width, 3 * width), v16(width, width), v32(8, width), hot, v16(rows, width),
         v16(rows, width), v16(rows, width), v16(rows, width), v16(rows, width), v32(rows, width),
         v16(rows, width), v32(rows, width)],
        scalars=3, ins_any=9, outs_any=8, us=C["attend"], limit=60,
    )
    held = lax.optimization_barrier((*far[3:], logs))[:2]
    wu4, wd4 = [four(w, f) for w, f in zip(own[3:], held)]
    ys, branch = call(
        forward_kernel,
        (rezero_alphas, *bias4, down_bias.reshape(1, width), arow, low, h, *wu4, *wd4),
        [shape((rows, width), BF), shape((rows, width), F32)],
        [sems(40), v16(rows, width), v32(rows, width), v16(width, ff), v16(ff, width), v16(rows, ff),
         v32(rows, width), v16(rows, width), hot, v16(rows, width)],
        scalars=1, ins_any=10, outs_any=2, us=C["forward"], limit=60,
    )
    bundle = (width + units + lanes) // blocks
    part = shape((tensors // 2, blocks, bundle, width), BF)
    small1, go, gh, keep1, send1 = call(
        feed_kernel,
        (ids, rezero_alphas, *bias4, acol, arr_g, *wu4, *wd4, *wo4, low, branch, attn, o),
        [shape((8, width), F32), shape((rows, width), BF), shape((rows, width), F32),
         shape(part.shape, F32), part],
        [sems(48), v16(rows, width), v16(width, ff), v16(ff, width), v16(width, width), v16(rows, ff),
         v16(rows, width), v32(rows, width), v32(rows, width), v16(rows, width),
         hot, v16(rows, width), v16(rows, width), v16(rows, ff), v32(rows, width), v16(rows, width), v16(rows, width),
         v32(*part.shape), v16(*part.shape), v32(width, width)],
        scalars=2, ins_any=17, outs_any=4, us=C["feed"], deps=(ys,), limit=60,
    )
    arr_y = exchange(ys)
    got = across("tensor", 1, send1)

    def back(first, last, deps):
        span = (last - first) * lanes
        return call(
            functools.partial(back_kernel, first), (lengths, logs, q, k, v, go),
            [shape((3, rows, span), BF)],
            [sems(16), v16(rows, span), v16(rows, span), v16(rows, span), v16(rows, span), v16(3, rows, span), v32(rows, lanes), v32(rows, lanes)],
            scalars=1, ins_any=4, outs_any=1, limit=60, deps=deps, us=C["back"],
        )[0]

    half = tensors // 2
    bare = shape((16, width), F32)

    def blocks_of(n, like, kind):
        return shape((n, *like.shape[1:]), kind)

    def settle(rows_back, deps):
        return call(settle_kernel, (rows_back, scol), [shape((rows, width), BF)], deps=deps, us=C["settle"])[0]

    def widen(first, a, b, into=None, deps=()):
        extra = () if into is None else (into,)
        return call(
            functools.partial(widen_kernel, first), (ids, a, b, *extra), [shape((tensors, rows, width), F32)],
            [sems(8), v32(2, rows, width), v16(2, rows, width)],
            scalars=1, ins_any=2 + len(extra), outs_any=1, us=C["widen"], deps=deps, aliases={3: 0} if extra else None,
        )[0]

    def relay(value, deps):
        return call(lambda *refs: None, (value,), [shape(value.shape, value.dtype)], ins_any=1, outs_any=1, aliases={0: 0}, deps=deps, us=0.1)[0]

    keep1 = keep1.reshape(half * blocks, bundle, width)
    send1 = send1.reshape(half * blocks, bundle, width)
    got = across("tensor", 1, send1)
    n = half * blocks // 2
    even, low_half = (lambda b: b % 2 == 0), (lambda b: b < blocks // 2)
    keep1, send1 = call(
        functools.partial(halve_kernel, even), (keep1, got), [blocks_of(n, keep1, F32), blocks_of(n, keep1, BF)], us=C["halve"]
    )
    got_y = across("dp", 1, send1)
    grad_a = back(0, half, (keep1,))
    grad_b = back(half, tensors, (grad_a,))
    y_own = settle(arr_y, (grad_b,))
    y_far = across("tensor", 2, y_own)
    y_core = across("tensor", 1, y_own)
    share = (3 * width) // blocks
    split = 2 * 16 * width // LANES
    n2 = half * blocks
    small, keep2, send2 = call(
        weight_kernel, (ids, small1, grad_a, grad_b, x),
        [bare, shape((n2, share, lanes), F32), shape((n2 + 1, share, lanes), BF)],
        [sems(20), v16(rows, 3 * width), v16(rows, width), v32(n2, share, lanes), v16(n2, share, lanes), v32(width, 3 * width),
         v16(split, LANES)],
        scalars=1, ins_any=3, outs_any=2, us=C["weight"], deps=(y_own,), limit=60,
    )
    n = n // 2
    keep1, send1 = call(
        functools.partial(halve_kernel, low_half), (keep1, got_y), [blocks_of(n, keep1, F32), blocks_of(n, keep1, BF)],
        deps=(small,), us=C["halve"],
    )
    got_x = across("tensor", 2, send1)
    gxs = call(
        last_kernel, (ids, arow, grad_a, grad_b, gh, *wa4), [shape((rows, width), BF)],
        [sems(40), v16(rows, 3 * width), v32(rows, width), v16(width, 3 * width), hot, v16(rows, width), v16(rows, width)],
        scalars=1, ins_any=7, outs_any=1, us=C["last"], deps=(keep1,), limit=60,
    )[0]
    arr_gx = exchange(gxs)
    got = across("tensor", 1, send2)
    n2 = n2 // 2
    keep2, small, send2 = call(
        functools.partial(halve_small_kernel, lambda b: b < blocks), (keep2, small, got),
        [blocks_of(n2, keep2, F32), bare, blocks_of(n2 + 1, keep2, BF)], deps=(gxs,), us=C["part"],
    )
    got = across("tensor", 2, send2)
    own1, *parts1 = call(
        part_kernel, (keep1, got_x), [shape(keep1.shape[1:], F32)] + [shape(keep1.shape[1:], BF)] * (blocks // 2 - 1),
        deps=(keep2, y_far), us=C["part"],
    )
    got1 = [across("dp", 2 * (j + 1), v) for j, v in enumerate(parts1)]
    y_late = call(lambda *refs: None, (y_far,), [shape((rows, width), BF)], ins_any=1, outs_any=1, aliases={0: 0}, deps=(own1,), us=0.1)[0]
    output = widen(0, y_own, y_core, deps=(own1,))
    shared, small = call(
        whole_small_kernel, (keep2, small, got), [shape((blocks, share + split, lanes), BF), bare], deps=(output,), us=C["part"],
    )
    ranks = None if groups == blocks else [list(range(g, g + blocks)) for g in range(0, groups, blocks)]
    shared = lax.all_to_all(shared, "dp", 0, 0, tiled=True, axis_index_groups=ranks)
    gx_own = settle(arr_gx, (small, y_late))
    gx_far = across("tensor", 2, gx_own)
    gx_core = across("tensor", 1, gx_own)
    y_both = across("tensor", 1, y_late)
    kind = BF if groups <= blocks else F32
    own1 = call(sum_kernel, (own1, *got1), [shape(own1.shape, kind)], deps=(gx_own,), us=C["part"])[0]
    bit = blocks
    while bit < groups:
        kind = BF if 2 * bit == groups else F32
        own1 = call(add_kernel, (own1, across("dp", bit, own1)), [shape(own1.shape, kind)])[0]
        bit *= 2
    a1, a4, a2 = across("dp", 1, own1), across("dp", 4, own1), across("dp", 2, own1)
    output = widen(2, y_late, y_both, output, deps=(own1,))
    gx_grad = widen(0, gx_own, gx_core, deps=(output,))
    spread_out = groups <= blocks
    own, small = call(
        pack_kernel, (shared,), [shape((blocks if spread_out else 1, share // 4, width), BF if spread_out else F32), bare],
        deps=(gx_grad, a1, a4, a2), us=C["halve"],
    )
    bit = blocks
    while bit < groups:
        kind = BF if 2 * bit == groups else F32
        own, small = call(
            add_one_kernel, (own, across("dp", bit, own), small, across("dp", bit, small)), [shape(own.shape, kind), bare]
        )
        bit *= 2
    if not spread_out:
        own = jnp.broadcast_to(own, (blocks, *own.shape[1:]))
    second = lax.all_to_all(own, "dp", 0, 0, tiled=True, axis_index_groups=ranks)
    a4 = relay(a4, (own,))
    a2 = relay(a2, (own,))
    a5, a6, a3 = across("dp", 1, a4), across("dp", 2, a4), across("dp", 1, a2)
    gathered = [own1, a1, a2, a3, a4, a5, a6, across("dp", 1, a6), second]
    gx_far = relay(gx_far, (a6, a5, a3))
    gx_both = across("tensor", 1, gx_far)
    qkv_grad, qv_grad, out_grad, ob_grad, up_grad, ub_grad, down_grad, db_grad, alphas = call(
        functools.partial(spread_kernel, blocks), (ids, small, *gathered),
        [shape((3, width, lanes), F32), shape((2, lanes), F32), shape((lanes, width), F32), shape((1, width), F32),
         shape((width, units), F32), shape((1, units), F32), shape((units, width), F32), shape((1, width), F32), shape((8, LANES), F32)],
        [v32(width, units), v32(share, lanes)], scalars=1, us=C["spread"],
    )
    input_grad = widen(2, gx_far, gx_both, gx_grad, deps=())
    return (
        output, input_grad, qkv_grad, qv_grad, out_grad, ob_grad[0], up_grad, ub_grad[0], down_grad, db_grad[0], alphas[0:2, 0],
    )


def solution(mesh):
    in_specs = (
        P(None, "dp", None), P(None, "dp", None), P(), P(None, "dp", None),
        P(None, None, "tensor"), P(None, "tensor"), P("tensor", None), P(),
        P(None, "tensor"), P("tensor"), P("tensor", None), P(), P(),
    )
    out_specs = (
        P(None, "dp", None), P(None, "dp", None), P(None, None, "tensor"), P(None, "tensor"),
        P("tensor", None), P(), P(None, "tensor"), P("tensor"), P("tensor", None), P(), P(),
    )
    return jax.shard_map(per_device, mesh=mesh, in_specs=in_specs, out_specs=out_specs, check_vma=False)
```
